32 devices in a mesh: walk: 2 (over x), chol: 16 (over z, y, core).
Axes of the slice: x: 2, y: 2, z: 4, core: 2. Of those that a mesh axis runs over, the one named last changes fastest.
Arguments:
- walkers: bfloat16 [16, 2048, 256], P('walk', 'chol'), may hold values from -2.5 to 2.5
- trial: bfloat16 [2048, 256], P('chol'), may hold values from -1.05 to 1.05
- cholesky: bfloat16 [32, 2048, 2048], P(None, 'chol'), may hold values from -0.125 to 0.125
- rotated: bfloat16 [32, 2048, 256], P(None, 'chol'), may hold values from -0.09375 to 0.09375
- fields: float32 [16, 32], P('walk'), may hold values from -4 to 4
- source: int32 [16], replicated, may hold values from 0 to 15, as said below
Outputs:
- propagated: bfloat16 [16, 2048, 256], P('walk', 'chol')
- force_bias: float32 [16, 32], P('walk')
The draws below stay inside these ranges and needn't reach their ends.
Inputs may be any that keep to these rules, and one draw needn't show every extreme that they name: source is a permutation of the walkers. New slots g * 8 to (g + 1) * 8 - 1 form group g, as do the old walkers. Of the old walkers of one group at most 4 fill slots of any one new group, and in every draw some group sends exactly 4 to some group.
All inputs are finite; a program needn't handle non-finite values.
Results may differ from the reference program's by a relative error of at most 0.0051.
Values may be sent and summed in bfloat16 or wider, within the bound.
No kernel may reach another device: no remote copies, remote signals or barrier semaphores. Data moves between devices by JAX's collectives and lax.ppermute only.
A program may use at most 128 MiB of HBM per device.

```python
import math
import jax
import jax.numpy as jnp
from jax import lax

M = 2048
N = 256
CHOL = 32
WG = 8
ITERS = 3
W = 16


def draw_walkers(key, part):
    subkeys = jax.random.split(jax.random.fold_in(key, 23), 2)
    diagonal = jnp.exp(jax.random.uniform(subkeys[0], (W, N), minval=-0.22, maxval=0.22))
    noise_draw = jnp.clip(jax.random.normal(subkeys[1], (W, M, N)), -5.0, 5.0)
    row_index = jnp.arange(M)[:, None]
    col_index = jnp.arange(N)[None, :]
    scales = jnp.where(row_index < N, 0.13 / math.sqrt(N), 0.5)
    identity = (row_index == col_index).astype(jnp.float32)
    values = noise_draw * scales[None] + identity[None] * diagonal[:, None, :]
    return values.astype(jnp.bfloat16)


def draw_trial(key, part):
    subkey = jax.random.fold_in(key, 37)
    noise_draw = jnp.clip(jax.random.normal(subkey, (M, N)), -4.0, 4.0)
    row_index = jnp.arange(M)[:, None]
    col_index = jnp.arange(N)[None, :]
    scales = jnp.where(row_index < N, 0.08 / math.sqrt(N), 0.54 / math.sqrt(N * (M - N)))
    identity = (row_index == col_index).astype(jnp.float32)
    return (identity + scales * noise_draw).astype(jnp.bfloat16)


def draw_source(key, part):
    groups = W // WG
    half_group = WG // 2
    subkeys = jax.random.split(jax.random.fold_in(key, 11), 4)
    first_dest = jax.random.permutation(subkeys[0], groups)
    rotation = jax.random.randint(subkeys[1], (), 1, groups)
    first_source = jnp.argsort(first_dest)
    second_source = (first_source - rotation) % groups
    orders = jax.vmap(lambda subkey: jax.random.permutation(subkey, WG))(jax.random.split(subkeys[2], groups))
    from_first = first_source[:, None] * WG + orders[first_source][:, :half_group]
    from_second = second_source[:, None] * WG + orders[second_source][:, half_group:]
    incoming = jnp.concatenate([from_first, from_second], axis=1)
    places = jax.vmap(lambda subkey: jax.random.permutation(subkey, WG))(jax.random.split(subkeys[3], groups))
    arranged = jnp.take_along_axis(incoming, places, axis=1)
    return arranged.reshape(W).astype(jnp.int32)


def block_levels(stream_key, shape, shards, smallest, top_value):
    level = 1.0
    for axis_at, shards_of in shards:
        steps = jax.random.uniform(jax.random.fold_in(jax.random.fold_in(stream_key, 6), axis_at), (shards_of,), jnp.float32, smallest / len(shards), top_value / len(shards))
        level = level * jnp.repeat(jnp.exp(steps), shape[axis_at] // shards_of).reshape((-1,) + (1,) * (len(shape) - 1 - axis_at))
    return level


def gaussian(key, extent, scale, limit, shards=(), kind=jnp.bfloat16):
    entries = scale * jax.random.normal(key, extent, jnp.float32)
    if shards:
        entries = entries * block_levels(key, extent, shards, -0.22, 0.18)
    return jnp.clip(entries, -limit, limit).astype(kind)


def setup_inputs(seed: int = 0) -> dict:
    arg_keys = jax.random.split(jax.random.key(seed), 7)
    return {
        "walkers": draw_walkers(jax.random.fold_in(arg_keys[6], 71), 0),
        "trial": draw_trial(jax.random.fold_in(arg_keys[6], 71), 0),
        "cholesky": gaussian(arg_keys[2], (CHOL, M, M), M ** -0.5, 0.125, ((1, 16),)),
        "rotated": gaussian(arg_keys[3], (CHOL, M, N), (M * N // 128) ** -0.5, 0.09375, ((1, 16),)),
        "fields": gaussian(arg_keys[4], (W, CHOL), 1.0, 4.0, ((0, 2),), jnp.float32),
        "source": draw_source(jax.random.fold_in(arg_keys[6], 71), 0),
    }


TAU_ROOT = 0.1


def newton_inverse(intersections):
    identity = jnp.eye(intersections.shape[-1], dtype=jnp.float32)
    estimate = jnp.broadcast_to(identity, intersections.shape)
    for sweep_index in range(ITERS):
        product = jnp.einsum("wij,wjk->wik", intersections, estimate, precision=lax.Precision.HIGHEST)
        estimate = jnp.einsum("wij,wjk->wik", estimate, 2.0 * identity - product, precision=lax.Precision.HIGHEST)
    return estimate


def reference(walkers, trial, cholesky, rotated, fields, source):
    migrated = jnp.take(walkers, source, axis=0)
    intersections = jnp.einsum("pi,wpj->wij", trial.astype(jnp.float32), migrated.astype(jnp.float32))
    inverse = newton_inverse(intersections).astype(jnp.bfloat16)
    greens = jnp.einsum("wpj,wji->wpi", migrated.astype(jnp.float32), inverse.astype(jnp.float32)).astype(jnp.bfloat16)
    force_bias = TAU_ROOT * jnp.einsum("lpi,wpi->wl", rotated.astype(jnp.float32), greens.astype(jnp.float32))
    shifted = (fields - force_bias).astype(jnp.bfloat16)
    flat_chol = cholesky.reshape(cholesky.shape[0], -1)

    def propagate(paired):
        walker, weights = paired
        potential = (TAU_ROOT * jnp.dot(weights[None, :], flat_chol, preferred_element_type=jnp.float32)).astype(jnp.bfloat16).reshape(M, M)
        first_term = jnp.dot(potential, walker, preferred_element_type=jnp.float32)
        second_term = jnp.dot(potential, first_term.astype(jnp.bfloat16), preferred_element_type=jnp.float32)
        return (walker.astype(jnp.float32) + first_term + 0.5 * second_term).astype(jnp.bfloat16)

    propagated = lax.map(propagate, (migrated, shifted))
    return propagated, force_bias
```

```python
import functools

import jax
import jax.numpy as jnp
from jax import lax
from jax.experimental import pallas as pl
from jax.experimental.pallas import tpu as pltpu
from jax.sharding import PartitionSpec as P

ITERS = 3
TAU_ROOT = 0.1
BLOCK = 16
HIGHEST = lax.Precision.HIGHEST
VMEM_LIMIT = 48 * 1024 * 1024

F32 = jnp.float32
BF16 = jnp.bfloat16


def params(limit=VMEM_LIMIT):
    return pltpu.CompilerParams(vmem_limit_bytes=limit)


def vmem_specs(count):
    return [pl.BlockSpec(memory_space=pltpu.VMEM)] * count


class Layout:
    def __init__(self, walk_size, chol_size):
        self.walk = walk_size
        self.chol = chol_size
        self.z = chol_size // 4

    def shift(self, array, dz=0, dy=0, db=0):
        pairs = []
        for index in range(self.chol):
            z, y, b = index // 4, (index // 2) % 2, index % 2
            target = (((z + dz) % self.z) * 2 + (y ^ dy)) * 2 + (b ^ db)
            pairs.append((index, target))
        return lax.ppermute(array, "chol", pairs)

    def shift_all(self, array, dw=0, dy=0, db=0):
        pairs = []
        for group in range(self.walk):
            for index in range(self.chol):
                z, y, b = index // 4, (index // 2) % 2, index % 2
                target = (z * 2 + (y ^ dy)) * 2 + (b ^ db)
                pairs.append(
                    (group * self.chol + index, ((group + dw) % self.walk) * self.chol + target)
                )
        return lax.ppermute(array, ("walk", "chol"), pairs)

    def gather(self, piece):
        along_z = [piece]
        for _ in range(self.z - 1):
            along_z.append(self.shift(along_z[-1], dz=1))
        chips = []
        for dz, array in enumerate(along_z):
            chips.append((array, dz, 0))
            chips.append((self.shift(array, dy=1), dz, 1))
        pieces = []
        for array, dz, dy in chips:
            pieces.append((array, dz, dy, 0))
            pieces.append((self.shift(array, db=1), dz, dy, 1))
        return pieces


def intersection_kernel(places, mine, theirs, trial_mine, trial_theirs, *outs):
    count = mine.shape[0]
    first = trial_mine[...].T
    second = trial_theirs[...].T
    z = lax.rem(lax.axis_index("chol") // 4, count)
    for step in range(count):
        walker = lax.rem(z + step, count) if places else step
        total = jnp.dot(first, mine[walker], preferred_element_type=F32)
        total += jnp.dot(second, theirs[walker], preferred_element_type=F32)
        outs[step][...] = total.astype(outs[step].dtype)


def intersections_of(mine, theirs, trial_mine, trial_theirs, places):
    count, _, electrons = mine.shape
    kinds = [F32] + [BF16 if places else F32] * (count - 1)
    return pl.pallas_call(
        functools.partial(intersection_kernel, places),
        out_shape=[jax.ShapeDtypeStruct((electrons, electrons), kind) for kind in kinds],
        in_specs=vmem_specs(4),
        out_specs=vmem_specs(count),
        compiler_params=params(),
    )(mine, theirs, trial_mine, trial_theirs)


def newton_kernel(*refs):
    parts, out = refs[:-1], refs[-1]
    matrix = parts[0][...]
    for part in parts[1:]:
        matrix = matrix + part[...].astype(F32)
    shape = matrix.shape
    twice = jnp.where(
        lax.broadcasted_iota(jnp.int32, shape, 0) == lax.broadcasted_iota(jnp.int32, shape, 1),
        2.0,
        0.0,
    ).astype(F32)
    estimate = twice - matrix
    for _ in range(ITERS - 1):
        product = jnp.dot(matrix, estimate, precision=HIGHEST, preferred_element_type=F32)
        estimate = jnp.dot(
            estimate, twice - product, precision=HIGHEST, preferred_element_type=F32
        )
    out[...] = estimate.astype(out.dtype)


def newton_of(parts):
    return pl.pallas_call(
        newton_kernel,
        out_shape=jax.ShapeDtypeStruct(parts[0].shape, BF16),
        in_specs=vmem_specs(len(parts)),
        out_specs=pl.BlockSpec(memory_space=pltpu.VMEM),
        compiler_params=params(),
    )(*parts)


def bias_kernel(places, count, mine, theirs, rot_mine, rot_theirs, *refs):
    inverses, out, total = refs[:count], refs[count], refs[count + 1]
    step = pl.program_id(0)
    z = lax.axis_index("chol") // 4

    @pl.when(step == 0)
    def _():
        total[...] = jnp.zeros_like(total)

    rows, electrons = mine.shape[1], mine.shape[2]
    vectors = rot_mine.shape[0]
    both = []
    for index in range(count):
        walker = lax.rem(z + (count - index), count) if places else index
        walker_rows = jnp.concatenate([mine[walker], theirs[walker]], axis=0)
        both.append(
            jnp.dot(walker_rows, inverses[index][...], preferred_element_type=F32).astype(BF16)
        )
    for half, rot in enumerate((rot_mine, rot_theirs)):
        greens = jnp.concatenate([g[half * rows : (half + 1) * rows] for g in both], axis=0)
        total[...] += lax.dot_general(
            greens,
            rot[...].reshape(vectors * rows, electrons),
            (((1,), (1,)), ((), ())),
            preferred_element_type=F32,
        )

    @pl.when(step == pl.num_programs(0) - 1)
    def _():
        shape = total.shape
        same = lax.rem(lax.broadcasted_iota(jnp.int32, shape, 0), rows) == lax.rem(
            lax.broadcasted_iota(jnp.int32, shape, 1), rows
        )
        kept = jnp.where(same, total[...], 0.0)
        summed = jnp.sum(kept.reshape(count, rows, shape[1]), axis=1)
        wide = (vectors * rows, vectors)
        pick = (
            lax.broadcasted_iota(jnp.int32, wide, 0) // rows
            == lax.broadcasted_iota(jnp.int32, wide, 1)
        ).astype(F32)
        result = jnp.dot(summed, pick, precision=HIGHEST, preferred_element_type=F32)
        row = lax.broadcasted_iota(jnp.int32, (count, 1), 0)
        ordered = jnp.zeros_like(result)
        for index in range(count):
            walker = lax.rem(z + (count - index), count) if places else index
            ordered += jnp.where(row == walker, result[index : index + 1], 0.0)
        out[...] = ordered


def bias_of(mine, theirs, rot_mine, rot_theirs, inverses, places):
    count, rows, electrons = mine.shape
    vectors = rot_mine.shape[0]
    walker_spec = pl.BlockSpec((count, BLOCK, electrons), lambda step: (0, step, 0))
    rot_spec = pl.BlockSpec((vectors, BLOCK, electrons), lambda step: (0, step, 0))
    whole = pl.BlockSpec((electrons, electrons), lambda step: (0, 0))
    return pl.pallas_call(
        functools.partial(bias_kernel, places, count),
        grid=(rows // BLOCK,),
        out_shape=jax.ShapeDtypeStruct((count, vectors), F32),
        in_specs=[walker_spec, walker_spec, rot_spec, rot_spec] + [whole] * count,
        out_specs=pl.BlockSpec((count, vectors), lambda step: (0, 0)),
        scratch_shapes=[pltpu.VMEM((count * BLOCK, vectors * BLOCK), F32)],
        compiler_params=params(),
        cost_estimate=pl.CostEstimate(
            flops=4 * count * rows * electrons * (electrons + vectors * BLOCK),
            bytes_accessed=4 * (vectors + count) * rows * electrons,
            transcendentals=0,
        ),
    )(mine, theirs, rot_mine, rot_theirs, *inverses)


def potential_kernel(origins, layout, fields, source, position, *refs):
    pieces = refs[: len(origins)]
    cholesky, bias_out, potential, weights = refs[len(origins) :]
    per_group, vectors = fields.shape
    half = pieces[0].shape[0]
    step = pl.program_id(0)

    @pl.when(step == 0)
    def _():
        group = lax.axis_index("walk")
        b = lax.rem(lax.axis_index("chol"), 2)
        wanted = source[...]
        bias = jnp.zeros((per_group, vectors), F32)
        for (dw, db), piece in zip(origins, pieces):
            from_group = lax.rem(group + (layout.walk - dw), layout.walk)
            from_b = b + db - 2 * b * db
            base = from_group * per_group + from_b * half
            for row in range(half):
                bias += jnp.where(wanted == base + row, piece[row : row + 1, :], 0.0)
        bias = TAU_ROOT * bias
        bias_out[...] = bias
        shifted = (fields[...] - bias).astype(BF16)
        tall = (per_group * BLOCK, per_group)
        rows = (
            lax.broadcasted_iota(jnp.int32, tall, 0) // BLOCK == position[...]
        ).astype(BF16)
        wide = (vectors, vectors * BLOCK)
        columns = (
            lax.broadcasted_iota(jnp.int32, wide, 1) // BLOCK
            == lax.broadcasted_iota(jnp.int32, wide, 0)
        ).astype(BF16)
        spread = jnp.dot(rows, shifted, preferred_element_type=F32).astype(BF16)
        spread = jnp.dot(spread, columns, preferred_element_type=F32)
        same = lax.rem(lax.broadcasted_iota(jnp.int32, spread.shape, 0), BLOCK) == lax.rem(
            lax.broadcasted_iota(jnp.int32, spread.shape, 1), BLOCK
        )
        weights[...] = jnp.where(same, spread, 0.0).astype(BF16)

    block = cholesky[...].reshape(vectors * BLOCK, cholesky.shape[2])
    result = TAU_ROOT * jnp.dot(weights[...], block, preferred_element_type=F32)
    potential[...] = result.astype(BF16).reshape(potential.shape)


def potential_of(layout, fields, source, position, pieces, cholesky):
    per_group, vectors = fields.shape
    rows, orbitals = cholesky.shape[1], cholesky.shape[2]
    origins = [origin for origin, _ in pieces]
    arrays = [array for _, array in pieces]

    def whole(array):
        return pl.BlockSpec(array.shape, lambda step: (0, 0))

    return pl.pallas_call(
        functools.partial(potential_kernel, origins, layout),
        grid=(rows // BLOCK,),
        out_shape=[
            jax.ShapeDtypeStruct((per_group, vectors), F32),
            jax.ShapeDtypeStruct((per_group, rows, orbitals), BF16),
        ],
        in_specs=[whole(a) for a in (fields, source, position, *arrays)]
        + [pl.BlockSpec((vectors, BLOCK, orbitals), lambda step: (0, step, 0))],
        out_specs=[
            pl.BlockSpec((per_group, vectors), lambda step: (0, 0)),
            pl.BlockSpec((per_group, BLOCK, orbitals), lambda step: (0, step, 0)),
        ],
        scratch_shapes=[pltpu.VMEM((per_group * BLOCK, vectors * BLOCK), BF16)],
        compiler_params=params(),
        cost_estimate=pl.CostEstimate(
            flops=2 * per_group * vectors * rows * BLOCK * orbitals,
            bytes_accessed=2 * (vectors + per_group) * rows * orbitals,
            transcendentals=0,
        ),
    )(fields, source, position, *arrays, cholesky)


def load_pieces(layout, places, pieces, buffer, semaphores):
    index = lax.axis_index("chol")
    z, y, b = index // 4, lax.rem(index // 2, 2), lax.rem(index, 2)
    rows = pieces[0].shape[1]
    copies = []
    for number, ((dz, dy, db), piece) in enumerate(zip(places, pieces)):
        from_z = lax.rem(z + (layout.z - dz), layout.z)
        from_y = y + dy - 2 * y * dy
        from_b = b + db - 2 * b * db
        owner = (from_z * 2 + from_y) * 2 + from_b
        copies.append(
            pltpu.make_async_copy(
                piece,
                buffer.at[:, pl.ds(pl.multiple_of(owner * rows, rows), rows), :],
                semaphores.at[number],
            )
        )
    return copies


def first_kernel(layout, places, potential, *refs):
    pieces = refs[: len(places)]
    rounded, base, buffer, semaphores = refs[len(places) :]
    step = pl.program_id(0)

    @pl.when(step == 0)
    def _():
        copies = load_pieces(layout, places, pieces, buffer, semaphores)
        for copy in copies:
            copy.start()
        for copy in copies:
            copy.wait()

    rows = base.shape[1]
    own = pl.ds(pl.multiple_of(lax.axis_index("chol") * rows, rows), rows)
    term = jnp.dot(potential[0], buffer[step], preferred_element_type=F32)
    rounded[0] = term.astype(BF16)
    base[0] = buffer[step, own, :].astype(F32) + term


def second_kernel(layout, places, order, potential, base, *refs):
    del order
    pieces = refs[: len(places)]
    out, buffer, semaphores = refs[-3:]
    step = pl.program_id(0)

    @pl.when(step == 0)
    def _():
        copies = load_pieces(layout, places, pieces, buffer, semaphores)
        for copy in copies:
            copy.start()
        for copy in copies:
            copy.wait()

    term = jnp.dot(potential[0], buffer[step], preferred_element_type=F32)
    out[0] = (base[0] + 0.5 * term).astype(BF16)


def fold_cost(count, rows, orbitals, electrons):
    return pl.CostEstimate(
        flops=2 * count * rows * orbitals * electrons,
        bytes_accessed=2 * count * orbitals * (rows + electrons),
        transcendentals=0,
    )


def first_of(layout, part, potential, gathered):
    places = [piece[1:] for piece in gathered]
    arrays = [piece[0] for piece in gathered]
    count, rows, electrons = arrays[0].shape
    orbitals = potential.shape[2]
    out_spec = pl.BlockSpec((1, rows, electrons), lambda step: (step, 0, 0))
    return pl.pallas_call(
        functools.partial(first_kernel, layout, places),
        grid=(count,),
        out_shape=[
            jax.ShapeDtypeStruct((count, rows, electrons), BF16),
            jax.ShapeDtypeStruct((count, rows, electrons), F32),
        ],
        in_specs=[pl.BlockSpec((1, rows, orbitals), lambda step: (part * count + step, 0, 0))]
        + [pl.BlockSpec(memory_space=pl.ANY)] * len(arrays),
        out_specs=[out_spec, out_spec],
        scratch_shapes=[
            pltpu.VMEM((count, orbitals, electrons), BF16),
            pltpu.SemaphoreType.DMA((len(arrays),)),
        ],
        compiler_params=params(),
        cost_estimate=fold_cost(count, rows, orbitals, electrons),
    )(potential, *arrays)


def second_of(layout, part, potential, base, gathered, order, previous):
    places = [piece[1:] for piece in gathered]
    arrays = [piece[0] for piece in gathered]
    count, rows, electrons = arrays[0].shape
    per_group, _, orbitals = potential.shape
    extra = [] if previous is None else [previous]
    inputs = [order, potential, base, *arrays, *extra]
    return pl.pallas_call(
        functools.partial(second_kernel, layout, places),
        out_shape=jax.ShapeDtypeStruct((per_group, rows, electrons), BF16),
        grid_spec=pltpu.PrefetchScalarGridSpec(
            num_scalar_prefetch=1,
            grid=(count,),
            in_specs=[
                pl.BlockSpec((1, rows, orbitals), lambda step, order: (part * count + step, 0, 0)),
                pl.BlockSpec((1, rows, electrons), lambda step, order: (step, 0, 0)),
            ]
            + [pl.BlockSpec(memory_space=pl.ANY)] * (len(arrays) + len(extra)),
            out_specs=pl.BlockSpec(
                (1, rows, electrons), lambda step, order: (order[part * count + step], 0, 0)
            ),
            scratch_shapes=[
                pltpu.VMEM((count, orbitals, electrons), BF16),
                pltpu.SemaphoreType.DMA((len(arrays),)),
            ],
        ),
        input_output_aliases={} if previous is None else {len(inputs) - 1: 0},
        compiler_params=params(),
        cost_estimate=fold_cost(count, rows, orbitals, electrons),
    )(*inputs)


def ranks(flags):
    count = flags.shape[-1]
    before = jnp.arange(count)[None, :] < jnp.arange(count)[:, None]
    return jnp.sum(jnp.where(before & flags[..., None, :], 1, 0), axis=-1)


def migrate(layout, walkers, source):
    per_group = walkers.shape[0]
    half = per_group // 2
    group = lax.axis_index("walk")
    table = source.reshape(layout.walk, per_group)
    incoming = lax.dynamic_index_in_dim(table, group, 0, keepdims=False)
    incoming_groups = incoming // per_group

    def outgoing(distance):
        row = lax.dynamic_index_in_dim(table, (group + distance) % layout.walk, 0, keepdims=False)
        local = row - group * per_group
        here = (local >= 0) & (local < per_group)
        match = here[None, :] & (ranks(here)[None, :] == jnp.arange(half)[:, None])
        return jnp.take(walkers, jnp.sum(jnp.where(match, local[None, :], 0), axis=1), axis=0)

    arrived = []
    for distance in range(layout.walk):
        block = outgoing(distance)
        if distance:
            pairs = [(g, (g + distance) % layout.walk) for g in range(layout.walk)]
            block = lax.ppermute(block, "walk", pairs)
        arrived.append(block)
    slots = jnp.arange(per_group)
    if layout.walk == 2:
        stays = incoming_groups == group
        position = jnp.where(stays, ranks(stays), half + ranks(~stays))
        hit = position[None, :] == slots[:, None]
        order = jnp.sum(jnp.where(hit, slots[None, :], 0), axis=1)
        return arrived, position.astype(jnp.int32), order.astype(jnp.int32)
    same = (incoming_groups[:, None] == incoming_groups[None, :]) & (slots[None, :] < slots[:, None])
    rank = jnp.sum(same.astype(jnp.int32), axis=1)
    distance = (group - incoming_groups) % layout.walk
    migrated = jnp.take(jnp.concatenate(arrived, axis=0), distance * half + rank, axis=0)
    slots = slots.astype(jnp.int32)
    return [migrated[:half], migrated[half:]], slots, slots


def shards(layout, walkers, trial, cholesky, rotated, fields, source):
    per_group = walkers.shape[0]
    half = per_group // 2
    group = lax.axis_index("walk")
    b = lax.axis_index("chol") % 2

    trial_theirs = layout.shift(trial, db=1)
    mine = lax.dynamic_slice_in_dim(walkers, b * half, half, 0)
    theirs = layout.shift(lax.dynamic_slice_in_dim(walkers, (1 - b) * half, half, 0), db=1)
    rot_theirs = layout.shift(rotated, db=1)
    halves, position, order = migrate(layout, walkers, source)
    places = layout.z == half
    partial = intersections_of(mine, theirs, trial, trial_theirs, places)
    if places:
        total = partial[0]
        for dz in range(1, half):
            total = total + layout.shift(partial[dz], dz=dz).astype(F32)
        other = layout.shift(total.astype(BF16), dy=1)
        inverse = newton_of([total, other])
        inverses = [inverse] + [layout.shift(inverse, dz=dz) for dz in range(1, half)]
    else:
        spread = jnp.zeros((2 * half,) + partial[0].shape, F32)
        spread = lax.dynamic_update_slice_in_dim(spread, jnp.stack(partial), b * half, 0)
        summed = lax.dynamic_slice_in_dim(lax.psum(spread, "chol"), b * half, half, 0)
        inverses = [newton_of([summed[index]]) for index in range(half)]
    bias = bias_of(mine, theirs, rotated, rot_theirs, inverses, places)
    parts = [bias] + [layout.shift(bias, dz=dz) for dz in range(1, layout.z)]
    while len(parts) > 1:
        far = (len(parts) + 1) // 2
        parts = [sum(parts[at::far][1:], parts[at]) for at in range(far)]
    total = parts[0]
    pieces = []
    for dw in range(layout.walk):
        for dy in range(2):
            for db in range(2):
                moved = total if dw + dy + db == 0 else layout.shift_all(total, dw, dy, db)
                pieces.append(((dw, db), moved))

    wanted = lax.dynamic_slice_in_dim(source, group * per_group, per_group)[:, None]
    force_bias, potential = potential_of(
        layout, fields, wanted, position[None, :], pieces, cholesky
    )

    bases, seconds = [], []
    gathered = [layout.gather(piece) for piece in halves]
    for part in range(2):
        rounded, base = first_of(layout, part, potential, gathered[part])
        bases.append(base)
        seconds.append(layout.gather(rounded))
    out = None
    for part in range(2):
        out = second_of(layout, part, potential, bases[part], seconds[part], order, out)
    return out, force_bias


def solution(mesh):
    in_specs = (
        P("walk", "chol", None),
        P("chol", None),
        P(None, "chol", None),
        P(None, "chol", None),
        P("walk", None),
        P(),
    )
    out_specs = (P("walk", "chol", None), P("walk", None))
    layout = Layout(mesh.shape["walk"], mesh.shape["chol"])
    return jax.shard_map(
        functools.partial(shards, layout),
        mesh=mesh,
        in_specs=in_specs,
        out_specs=out_specs,
        check_vma=False,
    )
```

```python
import functools

import jax
import jax.numpy as jnp
from jax import lax
from jax.experimental import pallas as pl
from jax.experimental.pallas import tpu as pltpu
from jax.sharding import PartitionSpec as P

ITERS = 3
TAU_ROOT = 0.1
BLOCK = 16
HIGHEST = lax.Precision.HIGHEST
MIB = 1024 * 1024

F32 = jnp.float32
BF16 = jnp.bfloat16


def params(mebibytes):
    return pltpu.CompilerParams(vmem_limit_bytes=mebibytes * MIB)


def vmem_specs(count):
    return [pl.BlockSpec(memory_space=pltpu.VMEM)] * count


class Layout:
    def __init__(self, walk_size, chol_size):
        self.walk = walk_size
        self.chol = chol_size
        self.z = chol_size // 4

    def shift(self, array, dz=0, dy=0, db=0):
        pairs = []
        for index in range(self.chol):
            z, y, b = index // 4, (index // 2) % 2, index % 2
            target = (((z + dz) % self.z) * 2 + (y ^ dy)) * 2 + (b ^ db)
            pairs.append((index, target))
        return lax.ppermute(array, "chol", pairs)

    def shift_all(self, array, dw, db):
        pairs = []
        for group in range(self.walk):
            for index in range(self.chol):
                target = ((group + dw) % self.walk) * self.chol + (index ^ db)
                pairs.append((group * self.chol + index, target))
        return lax.ppermute(array, ("walk", "chol"), pairs)

    def swap(self, array, distance):
        pairs = [(i, (((i // 4) ^ distance) * 4) + i % 4) for i in range(self.chol)]
        return lax.ppermute(array, "chol", pairs)

    def gather_plane(self, piece):
        planes = [[i for i in range(self.chol) if i % 2 == b] for b in range(2)]
        return lax.all_gather(piece, "chol", axis_index_groups=planes, axis=1, tiled=True)

    def with_sibling(self, plane, rows):
        both = (plane, self.shift(plane, db=1))
        shape = (plane.shape[0], self.chol // 2, rows, plane.shape[2])
        return [array.reshape(shape) for array in both]


def intersection_kernel(places, mine, theirs, trial_mine, trial_theirs, *outs):
    count = mine.shape[0] // 2
    first = trial_mine[...].T
    second = trial_theirs[...].T
    index = lax.axis_index("chol")
    z, base = index // 4, lax.rem(index, 2) * count
    for step in range(count):
        walker = base + (lax.rem(z + step, count) if places else step)
        total = jnp.dot(first, mine[walker], preferred_element_type=F32)
        total += jnp.dot(second, theirs[walker], preferred_element_type=F32)
        outs[step][...] = total.astype(outs[step].dtype)


def intersections_of(mine, theirs, trial_mine, trial_theirs, places):
    per_group, _, electrons = mine.shape
    count = per_group // 2
    kinds = [F32] + [BF16 if places else F32] * (count - 1)
    return pl.pallas_call(
        functools.partial(intersection_kernel, places),
        out_shape=[jax.ShapeDtypeStruct((electrons, electrons), kind) for kind in kinds],
        in_specs=vmem_specs(4),
        out_specs=vmem_specs(count),
        compiler_params=params(8),
    )(mine, theirs, trial_mine, trial_theirs)


def newton_kernel(*refs):
    parts, out = refs[:-1], refs[-1]
    matrix = parts[0][...]
    for part in parts[1:]:
        matrix = matrix + part[...].astype(F32)
    shape = matrix.shape
    twice = jnp.where(
        lax.broadcasted_iota(jnp.int32, shape, 0) == lax.broadcasted_iota(jnp.int32, shape, 1),
        2.0,
        0.0,
    ).astype(F32)
    estimate = twice - matrix
    for _ in range(ITERS - 1):
        product = jnp.dot(matrix, estimate, precision=HIGHEST, preferred_element_type=F32)
        estimate = jnp.dot(
            estimate, twice - product, precision=HIGHEST, preferred_element_type=F32
        )
    out[...] = estimate.astype(out.dtype)


def newton_of(parts):
    return pl.pallas_call(
        newton_kernel,
        out_shape=jax.ShapeDtypeStruct(parts[0].shape, BF16),
        in_specs=vmem_specs(len(parts)),
        out_specs=pl.BlockSpec(memory_space=pltpu.VMEM),
        compiler_params=params(8),
    )(*parts)


def bias_kernel(places, mine, theirs, rot_mine, rot_theirs, *refs):
    inverses, out, greens = refs[:-2], refs[-2], refs[-1]
    count = len(inverses)
    rows, electrons = mine.shape[1], mine.shape[2]
    vectors = rot_mine.shape[0]
    index = lax.axis_index("chol")
    z, base = index // 4, lax.rem(index, 2) * count
    for at in range(count):
        walker = base + (lax.rem(z + (count - at), count) if places else at)
        both = jnp.concatenate([mine[walker], theirs[walker]], axis=0)
        product = jnp.dot(both, inverses[at][...], preferred_element_type=F32).astype(BF16)
        greens[:, :, at] = product.reshape(2, rows // BLOCK, BLOCK, electrons)
    total = jnp.zeros((vectors * BLOCK, count * BLOCK), F32)
    for half, rot in enumerate((rot_mine, rot_theirs)):
        for block in range(rows // BLOCK):
            total += lax.dot_general(
                rot[:, block * BLOCK : (block + 1) * BLOCK, :].reshape(vectors * BLOCK, electrons),
                greens[half, block].reshape(count * BLOCK, electrons),
                (((1,), (1,)), ((), ())),
                preferred_element_type=F32,
            )
    same = lax.rem(lax.broadcasted_iota(jnp.int32, total.shape, 0), BLOCK) == lax.rem(
        lax.broadcasted_iota(jnp.int32, total.shape, 1), BLOCK
    )
    summed = jnp.sum(
        jnp.where(same, total, 0.0).reshape(vectors, BLOCK, count * BLOCK), axis=1
    )
    shape = (count, count * BLOCK)
    walker = lax.broadcasted_iota(jnp.int32, shape, 0)
    place = lax.rem(lax.rem(z, count) + (count - walker), count) if places else walker
    pick = (lax.broadcasted_iota(jnp.int32, shape, 1) // BLOCK == place).astype(F32)
    out[...] = lax.dot_general(
        pick, summed, (((1,), (1,)), ((), ())), precision=HIGHEST, preferred_element_type=F32
    )


def bias_of(mine, theirs, rot_mine, rot_theirs, inverses, places):
    _, rows, electrons = mine.shape
    count = len(inverses)
    vectors = rot_mine.shape[0]
    return pl.pallas_call(
        functools.partial(bias_kernel, places),
        out_shape=jax.ShapeDtypeStruct((count, vectors), F32),
        in_specs=vmem_specs(4 + count),
        out_specs=pl.BlockSpec(memory_space=pltpu.VMEM),
        scratch_shapes=[pltpu.VMEM((2, rows // BLOCK, count, BLOCK, electrons), BF16)],
        compiler_params=params(12),
        cost_estimate=pl.CostEstimate(
            flops=4 * count * rows * electrons * (electrons + vectors * BLOCK),
            bytes_accessed=4 * (vectors + count) * rows * electrons,
            transcendentals=0,
        ),
    )(mine, theirs, rot_mine, rot_theirs, *inverses)


def potential_kernel(origins, layout, order, fields, source, *refs):
    pieces = refs[: len(origins)]
    cholesky, bias_out, potential, weights = refs[len(origins) :]
    per_group, vectors = fields.shape
    half = pieces[0].shape[0]
    step = pl.program_id(0)

    @pl.when(step == 0)
    def _():
        group = lax.axis_index("walk")
        b = lax.rem(lax.axis_index("chol"), 2)
        wanted = source[...]
        bias = jnp.zeros((per_group, vectors), F32)
        for (dw, db), piece in zip(origins, pieces):
            from_group = lax.rem(group + (layout.walk - dw), layout.walk)
            from_b = b + db - 2 * b * db
            base = from_group * per_group + from_b * half
            for row in range(half):
                bias += jnp.where(wanted == base + row, piece[row : row + 1, :], 0.0)
        bias = TAU_ROOT * bias
        bias_out[...] = bias
        shifted = (fields[...] - bias).astype(BF16)
        tall = (per_group * BLOCK, per_group)
        slot = jnp.zeros((per_group * BLOCK, 1), jnp.int32)
        place = lax.broadcasted_iota(jnp.int32, slot.shape, 0) // BLOCK
        for at in range(per_group):
            slot = jnp.where(place == at, order[at], slot)
        rows = (lax.broadcasted_iota(jnp.int32, tall, 1) == slot).astype(BF16)
        wide = (vectors, vectors * BLOCK)
        columns = (
            lax.broadcasted_iota(jnp.int32, wide, 1) // BLOCK
            == lax.broadcasted_iota(jnp.int32, wide, 0)
        ).astype(BF16)
        spread = jnp.dot(rows, shifted, preferred_element_type=F32).astype(BF16)
        spread = jnp.dot(spread, columns, preferred_element_type=F32)
        same = lax.rem(lax.broadcasted_iota(jnp.int32, spread.shape, 0), BLOCK) == lax.rem(
            lax.broadcasted_iota(jnp.int32, spread.shape, 1), BLOCK
        )
        weights[...] = jnp.where(same, spread, 0.0).astype(BF16)

    block = cholesky[...].reshape(vectors * BLOCK, cholesky.shape[2])
    result = TAU_ROOT * jnp.dot(weights[...], block, preferred_element_type=F32)
    potential[...] = result.astype(BF16).reshape(potential.shape)


def potential_of(layout, order, fields, source, pieces, cholesky):
    per_group, vectors = fields.shape
    rows, orbitals = cholesky.shape[1], cholesky.shape[2]
    origins = [origin for origin, _ in pieces]
    arrays = [array for _, array in pieces]

    def whole(array):
        return pl.BlockSpec(array.shape, lambda step: (0, 0))

    return pl.pallas_call(
        functools.partial(potential_kernel, origins, layout),
        grid=(rows // BLOCK,),
        out_shape=[
            jax.ShapeDtypeStruct((per_group, vectors), F32),
            jax.ShapeDtypeStruct((per_group, rows, orbitals), BF16),
        ],
        in_specs=[pl.BlockSpec(memory_space=pltpu.SMEM)]
        + [whole(a) for a in (fields, source, *arrays)]
        + [pl.BlockSpec((vectors, BLOCK, orbitals), lambda step: (0, step, 0))],
        out_specs=[
            pl.BlockSpec((per_group, vectors), lambda step: (0, 0)),
            pl.BlockSpec((per_group, BLOCK, orbitals), lambda step: (0, step, 0)),
        ],
        scratch_shapes=[pltpu.VMEM((per_group * BLOCK, vectors * BLOCK), BF16)],
        compiler_params=params(12),
        cost_estimate=pl.CostEstimate(
            flops=2 * per_group * vectors * rows * BLOCK * orbitals,
            bytes_accessed=2 * (vectors + per_group) * rows * orbitals,
            transcendentals=0,
        ),
    )(order, fields, source, *arrays, cholesky)


def plane_copies(planes, buffer, semaphores, walker):
    b = lax.rem(lax.axis_index("chol"), 2)
    return [
        pltpu.make_async_copy(
            plane.at[walker], buffer.at[walker, :, core], semaphores.at[number, walker]
        )
        for number, (plane, core) in enumerate(zip(planes, (b, 1 - b)))
    ]


def gathered_walker(planes, buffer, semaphores):
    step = pl.program_id(0)

    @pl.when(step == 0)
    def _():
        for walker in range(buffer.shape[0]):
            for copy in plane_copies(planes, buffer, semaphores, walker):
                copy.start()

    for copy in plane_copies(planes, buffer, semaphores, step):
        copy.wait()
    walker = buffer[step]
    return walker.reshape(-1, walker.shape[-1])


def first_kernel(potential, *refs):
    planes, (rounded, base, buffer, semaphores) = refs[:2], refs[2:]
    walker = gathered_walker(planes, buffer, semaphores)
    term = jnp.dot(potential[0], walker, preferred_element_type=F32)
    index = lax.axis_index("chol")
    own = buffer[pl.program_id(0), index // 2, lax.rem(index, 2)]
    rounded[0] = term.astype(BF16)
    base[0] = own.astype(F32) + term


def second_kernel(order, potential, base, *refs):
    del order
    planes, (out, buffer, semaphores) = refs[:2], refs[-3:]
    walker = gathered_walker(planes, buffer, semaphores)
    term = jnp.dot(potential[0], walker, preferred_element_type=F32)
    out[0] = (base[0] + 0.5 * term).astype(BF16)


def fold_cost(count, rows, orbitals, electrons):
    return pl.CostEstimate(
        flops=2 * count * rows * orbitals * electrons,
        bytes_accessed=2 * count * orbitals * (rows + electrons),
        transcendentals=0,
    )


def first_of(part, potential, planes):
    count, _, rows, electrons = planes[0].shape
    orbitals = potential.shape[2]
    out_spec = pl.BlockSpec((1, rows, electrons), lambda step: (step, 0, 0))
    return pl.pallas_call(
        first_kernel,
        grid=(count,),
        out_shape=[
            jax.ShapeDtypeStruct((count, rows, electrons), BF16),
            jax.ShapeDtypeStruct((count, rows, electrons), F32),
        ],
        in_specs=[pl.BlockSpec((1, rows, orbitals), lambda step: (part * count + step, 0, 0))]
        + [pl.BlockSpec(memory_space=pl.ANY)] * 2,
        out_specs=[out_spec, out_spec],
        scratch_shapes=[
            pltpu.VMEM((count, orbitals // (2 * rows), 2, rows, electrons), BF16),
            pltpu.SemaphoreType.DMA((2, count)),
        ],
        compiler_params=params(10),
        cost_estimate=fold_cost(count, rows, orbitals, electrons),
    )(potential, *planes)


def second_of(part, potential, base, planes, order, previous):
    count, _, rows, electrons = planes[0].shape
    per_group, _, orbitals = potential.shape
    extra = [] if previous is None else [previous]
    inputs = [order, potential, base, *planes, *extra]
    return pl.pallas_call(
        second_kernel,
        out_shape=jax.ShapeDtypeStruct((per_group, rows, electrons), BF16),
        grid_spec=pltpu.PrefetchScalarGridSpec(
            num_scalar_prefetch=1,
            grid=(count,),
            in_specs=[
                pl.BlockSpec((1, rows, orbitals), lambda step, order: (part * count + step, 0, 0)),
                pl.BlockSpec((1, rows, electrons), lambda step, order: (step, 0, 0)),
            ]
            + [pl.BlockSpec(memory_space=pl.ANY)] * (2 + len(extra)),
            out_specs=pl.BlockSpec(
                (1, rows, electrons), lambda step, order: (order[part * count + step], 0, 0)
            ),
            scratch_shapes=[
                pltpu.VMEM((count, orbitals // (2 * rows), 2, rows, electrons), BF16),
                pltpu.SemaphoreType.DMA((2, count)),
            ],
        ),
        input_output_aliases={} if previous is None else {len(inputs) - 1: 0},
        compiler_params=params(10),
        cost_estimate=fold_cost(count, rows, orbitals, electrons),
    )(*inputs)


def split_kernel(source, walkers, staying, leaving, order, picked, semaphores):
    per_group = walkers.shape[0]
    half = per_group // 2
    group = lax.axis_index("walk")
    counts = [jnp.int32(0), jnp.int32(0)]
    for slot in range(per_group):
        local = source[group * per_group + slot] - group * per_group
        stays = ((local >= 0) & (local < per_group)).astype(jnp.int32)
        place = jnp.where(stays == 1, counts[0], half + counts[1])
        place = jnp.minimum(place, per_group - 1)
        order[place] = jnp.int32(slot)
        picked[place] = jnp.where(stays == 1, local, 0)
        counts = [counts[0] + stays, counts[1] + 1 - stays]
    sent = jnp.int32(0)
    for slot in range(per_group):
        local = source[(1 - group) * per_group + slot] - group * per_group
        goes = ((local >= 0) & (local < per_group)).astype(jnp.int32)
        place = jnp.where(goes == 1, half + jnp.minimum(sent, half - 1), per_group)
        picked[place] = local
        sent = sent + goes
    copies = []
    for place in range(per_group):
        target = (leaving if place >= half else staying).at[place % half]
        copies.append(
            pltpu.make_async_copy(walkers.at[picked[place]], target, semaphores.at[place])
        )
    for copy in copies[half:] + copies[:half]:
        copy.start()
    for copy in copies:
        copy.wait()


def split_walkers(walkers, source):
    per_group, rows, electrons = walkers.shape
    half = jax.ShapeDtypeStruct((per_group // 2, rows, electrons), walkers.dtype)
    return pl.pallas_call(
        split_kernel,
        out_shape=[half, half, jax.ShapeDtypeStruct((per_group,), jnp.int32)],
        in_specs=[pl.BlockSpec(memory_space=pltpu.SMEM), pl.BlockSpec(memory_space=pl.ANY)],
        out_specs=[pl.BlockSpec(memory_space=pl.ANY)] * 2
        + [pl.BlockSpec(memory_space=pltpu.SMEM)],
        scratch_shapes=[
            pltpu.SMEM((per_group + 1,), jnp.int32),
            pltpu.SemaphoreType.DMA((per_group,)),
        ],
        compiler_params=params(4),
    )(source, walkers)


def ranks(flags):
    count = flags.shape[-1]
    before = jnp.arange(count)[None, :] < jnp.arange(count)[:, None]
    return jnp.sum(jnp.where(before & flags[..., None, :], 1, 0), axis=-1)


def migrate(layout, walkers, source):
    per_group = walkers.shape[0]
    half = per_group // 2
    group = lax.axis_index("walk")
    if layout.walk == 2:
        staying, leaving, order = split_walkers(walkers, source)
        return [staying, lax.ppermute(leaving, "walk", [(0, 1), (1, 0)])], order
    table = source.reshape(layout.walk, per_group)
    incoming = lax.dynamic_index_in_dim(table, group, 0, keepdims=False)
    incoming_groups = incoming // per_group

    def outgoing(distance):
        row = lax.dynamic_index_in_dim(table, (group + distance) % layout.walk, 0, keepdims=False)
        local = row - group * per_group
        here = (local >= 0) & (local < per_group)
        match = here[None, :] & (ranks(here)[None, :] == jnp.arange(half)[:, None])
        return jnp.take(walkers, jnp.sum(jnp.where(match, local[None, :], 0), axis=1), axis=0)

    arrived = [outgoing(0)]
    for distance in range(1, layout.walk):
        pairs = [(g, (g + distance) % layout.walk) for g in range(layout.walk)]
        arrived.append(lax.ppermute(outgoing(distance), "walk", pairs))
    slots = jnp.arange(per_group)
    same = (incoming_groups[:, None] == incoming_groups[None, :]) & (slots[None, :] < slots[:, None])
    rank = jnp.sum(same.astype(jnp.int32), axis=1)
    distance = (group - incoming_groups) % layout.walk
    migrated = jnp.take(jnp.concatenate(arrived, axis=0), distance * half + rank, axis=0)
    return [migrated[:half], migrated[half:]], slots.astype(jnp.int32)


def shards(layout, walkers, trial, cholesky, rotated, fields, source):
    per_group = walkers.shape[0]
    half = per_group // 2
    group = lax.axis_index("walk")

    trial_theirs = layout.shift(trial, db=1)
    theirs = layout.shift(walkers, db=1)
    rot_theirs = layout.shift(rotated, db=1)
    halves, order = migrate(layout, walkers, source)
    places = layout.z == half
    partial = intersections_of(walkers, theirs, trial, trial_theirs, places)
    if places:
        total = partial[0]
        for dz in range(1, half):
            total = total + layout.shift(partial[dz], dz=dz).astype(F32)
        total, halves[1] = lax.optimization_barrier((total, halves[1]))
        other = layout.shift(total.astype(BF16), dy=1)
        inverse = newton_of([total, other])
        inverses = [inverse] + [layout.shift(inverse, dz=dz) for dz in range(1, half)]
    else:
        b = lax.axis_index("chol") % 2
        spread = jnp.zeros((per_group,) + partial[0].shape, F32)
        spread = lax.dynamic_update_slice_in_dim(spread, jnp.stack(partial), b * half, 0)
        summed = lax.dynamic_slice_in_dim(lax.psum(spread, "chol"), b * half, half, 0)
        inverses = [newton_of([summed[index]]) for index in range(half)]
    total = bias_of(walkers, theirs, rotated, rot_theirs, inverses, places)
    distance = layout.z // 2
    while distance:
        total = total + layout.swap(total, distance)
        distance //= 2
    total = total + layout.shift(total, dy=1)
    planes = [layout.gather_plane(piece) for piece in halves]
    total, planes[0] = lax.optimization_barrier((total, planes[0]))
    pieces = []
    for dw in range(layout.walk):
        for db in range(2):
            moved = layout.shift_all(total, dw, db) if dw + db else total
            pieces.append(((dw, db), moved))

    wanted = lax.dynamic_slice_in_dim(source, group * per_group, per_group)[:, None]
    force_bias, potential = potential_of(layout, order, fields, wanted, pieces, cholesky)

    rows = walkers.shape[1]
    bases, seconds = [], []
    for part in range(2):
        both = layout.with_sibling(planes[part], rows)
        rounded, base = first_of(part, potential, both)
        bases.append(base)
        seconds.append(layout.gather_plane(rounded))
    out = None
    for part in range(2):
        both = layout.with_sibling(seconds[part], rows)
        out = second_of(part, potential, bases[part], both, order, out)
    return out, force_bias


def solution(mesh):
    in_specs = (
        P("walk", "chol", None),
        P("chol", None),
        P(None, "chol", None),
        P(None, "chol", None),
        P("walk", None),
        P(),
    )
    out_specs = (P("walk", "chol", None), P("walk", None))
    layout = Layout(mesh.shape["walk"], mesh.shape["chol"])
    return jax.shard_map(
        functools.partial(shards, layout),
        mesh=mesh,
        in_specs=in_specs,
        out_specs=out_specs,
        check_vma=False,
    )
```

```python
import functools

import jax
import jax.numpy as jnp
from jax import lax
from jax.experimental import pallas as pl
from jax.experimental.pallas import tpu as pltpu
from jax.sharding import PartitionSpec as P

ITERS = 3
TAU_ROOT = 0.1
BLOCK = 16
HIGHEST = lax.Precision.HIGHEST
MIB = 1024 * 1024

F32 = jnp.float32
BF16 = jnp.bfloat16


def params(mebibytes):
    return pltpu.CompilerParams(vmem_limit_bytes=mebibytes * MIB)


def vmem_specs(count):
    return [pl.BlockSpec(memory_space=pltpu.VMEM)] * count


class Layout:
    def __init__(self, walk_size, chol_size):
        self.walk = walk_size
        self.chol = chol_size
        self.z = chol_size // 4

    def shift(self, array, dz=0, dy=0, db=0):
        pairs = []
        for index in range(self.chol):
            z, y, b = index // 4, (index // 2) % 2, index % 2
            target = (((z + dz) % self.z) * 2 + (y ^ dy)) * 2 + (b ^ db)
            pairs.append((index, target))
        return lax.ppermute(array, "chol", pairs)

    def shift_all(self, array, dw, db):
        pairs = []
        for group in range(self.walk):
            for index in range(self.chol):
                target = ((group + dw) % self.walk) * self.chol + (index ^ db)
                pairs.append((group * self.chol + index, target))
        return lax.ppermute(array, ("walk", "chol"), pairs)

    def swap(self, array, distance):
        pairs = [(i, (((i // 4) ^ distance) * 4) + i % 4) for i in range(self.chol)]
        return lax.ppermute(array, "chol", pairs)


class Stream:
    def __init__(self, layout, piece, walker=0):
        self.layout = layout
        self.walker = walker
        self.ring = [piece]
        self.across = []

    def advance(self, anchors=()):
        if len(self.across) == self.layout.z:
            return anchors
        latest = self.ring[-1]
        moved = [self.layout.shift(latest, dy=1)]
        last = len(self.ring) == self.layout.z
        if not last:
            moved.append(self.layout.shift(latest, dz=1))
        if anchors or not last:
            anchors, moved = lax.optimization_barrier((anchors, moved))
        self.across.append(moved[0])
        self.ring.extend(moved[1:])
        return anchors

    def pieces(self):
        ring = [(array, self.walker, dz, 0) for dz, array in enumerate(self.ring)]
        return ring + [(array, self.walker, dz, 1) for dz, array in enumerate(self.across)]


def diagonal(shape):
    return lax.broadcasted_iota(jnp.int32, shape, 0) == lax.broadcasted_iota(jnp.int32, shape, 1)


def to_message(total):
    rounded = total.astype(BF16)
    rest = jnp.where(diagonal(total.shape), total - rounded.astype(F32), 0.0)
    rest = jnp.broadcast_to(jnp.sum(rest, axis=0, keepdims=True), (BLOCK, total.shape[1]))
    return jnp.concatenate([rounded, rest.astype(BF16)], axis=0)


def from_message(message):
    size = message.shape[1]
    matrix = message[:size].astype(F32)
    rest = message[size:].astype(F32)[:1]
    return matrix + jnp.where(diagonal(matrix.shape), rest, 0.0)


def intersection_kernel(places, mine, theirs, trial_mine, trial_theirs, *outs):
    count = mine.shape[0] // 2
    first = trial_mine[...].T
    second = trial_theirs[...].T
    index = lax.axis_index("chol")
    z, base = index // 4, lax.rem(index, 2) * count
    for step in range(count):
        walker = base + (lax.rem(z + step, count) if places else step)
        total = jnp.dot(first, mine[walker], preferred_element_type=F32)
        total += jnp.dot(second, theirs[walker], preferred_element_type=F32)
        outs[step][...] = to_message(total) if places and step else total


def intersections_of(mine, theirs, trial_mine, trial_theirs, places):
    per_group, _, electrons = mine.shape
    count = per_group // 2
    whole = jax.ShapeDtypeStruct((electrons, electrons), F32)
    message = jax.ShapeDtypeStruct((electrons + BLOCK, electrons), BF16)
    return pl.pallas_call(
        functools.partial(intersection_kernel, places),
        out_shape=[whole] + [message if places else whole] * (count - 1),
        in_specs=vmem_specs(4),
        out_specs=vmem_specs(count),
        compiler_params=params(8),
    )(mine, theirs, trial_mine, trial_theirs)


def sum_kernel(own, *refs):
    messages, (total_out, message_out) = refs[:-2], refs[-2:]
    total = own[...]
    for message in messages:
        total = total + from_message(message[...])
    total_out[...] = total
    message_out[...] = to_message(total)


def sum_of(own, messages):
    return pl.pallas_call(
        sum_kernel,
        out_shape=[
            jax.ShapeDtypeStruct(own.shape, F32),
            jax.ShapeDtypeStruct(messages[0].shape, BF16),
        ],
        in_specs=vmem_specs(1 + len(messages)),
        out_specs=vmem_specs(2),
        compiler_params=params(8),
    )(own, *messages)


def newton_kernel(own, *refs):
    messages, out = refs[:-1], refs[-1]
    matrix = own[...]
    for message in messages:
        matrix = matrix + from_message(message[...])
    twice = jnp.where(diagonal(matrix.shape), 2.0, 0.0).astype(F32)
    estimate = twice - matrix
    for _ in range(ITERS - 1):
        product = jnp.dot(matrix, estimate, precision=HIGHEST, preferred_element_type=F32)
        estimate = jnp.dot(
            estimate, twice - product, precision=HIGHEST, preferred_element_type=F32
        )
    out[...] = estimate.astype(out.dtype)


def newton_of(own, messages=()):
    return pl.pallas_call(
        newton_kernel,
        out_shape=jax.ShapeDtypeStruct(own.shape, BF16),
        in_specs=vmem_specs(1 + len(messages)),
        out_specs=pl.BlockSpec(memory_space=pltpu.VMEM),
        compiler_params=params(8),
    )(own, *messages)


def bias_kernel(places, mine, theirs, rot_mine, rot_theirs, *refs):
    inverses, out, greens = refs[:-2], refs[-2], refs[-1]
    count = len(inverses)
    rows, electrons = mine.shape[1], mine.shape[2]
    vectors = rot_mine.shape[0]
    index = lax.axis_index("chol")
    z, base = index // 4, lax.rem(index, 2) * count
    for at in range(count):
        walker = base + (lax.rem(z + (count - at), count) if places else at)
        both = jnp.concatenate([mine[walker], theirs[walker]], axis=0)
        product = jnp.dot(both, inverses[at][...], preferred_element_type=F32).astype(BF16)
        greens[:, :, at] = product.reshape(2, rows // BLOCK, BLOCK, electrons)
    total = jnp.zeros((vectors * BLOCK, count * BLOCK), F32)
    for half, rot in enumerate((rot_mine, rot_theirs)):
        for block in range(rows // BLOCK):
            total += lax.dot_general(
                rot[:, block * BLOCK : (block + 1) * BLOCK, :].reshape(vectors * BLOCK, electrons),
                greens[half, block].reshape(count * BLOCK, electrons),
                (((1,), (1,)), ((), ())),
                preferred_element_type=F32,
            )
    same = lax.rem(lax.broadcasted_iota(jnp.int32, total.shape, 0), BLOCK) == lax.rem(
        lax.broadcasted_iota(jnp.int32, total.shape, 1), BLOCK
    )
    summed = jnp.sum(
        jnp.where(same, total, 0.0).reshape(vectors, BLOCK, count * BLOCK), axis=1
    )
    shape = (count, count * BLOCK)
    walker = lax.broadcasted_iota(jnp.int32, shape, 0)
    place = lax.rem(lax.rem(z, count) + (count - walker), count) if places else walker
    pick = (lax.broadcasted_iota(jnp.int32, shape, 1) // BLOCK == place).astype(F32)
    out[...] = lax.dot_general(
        pick, summed, (((1,), (1,)), ((), ())), precision=HIGHEST, preferred_element_type=F32
    )


def bias_of(mine, theirs, rot_mine, rot_theirs, inverses, places):
    _, rows, electrons = mine.shape
    count = len(inverses)
    vectors = rot_mine.shape[0]
    return pl.pallas_call(
        functools.partial(bias_kernel, places),
        out_shape=jax.ShapeDtypeStruct((count, vectors), F32),
        in_specs=vmem_specs(4 + count),
        out_specs=pl.BlockSpec(memory_space=pltpu.VMEM),
        scratch_shapes=[pltpu.VMEM((2, rows // BLOCK, count, BLOCK, electrons), BF16)],
        compiler_params=params(12),
        cost_estimate=pl.CostEstimate(
            flops=4 * count * rows * electrons * (electrons + vectors * BLOCK),
            bytes_accessed=4 * (vectors + count) * rows * electrons,
            transcendentals=0,
        ),
    )(mine, theirs, rot_mine, rot_theirs, *inverses)


def weights_kernel(origins, layout, order, fields, source, *refs):
    pieces, (bias_out, weights) = refs[:-2], refs[-2:]
    per_group, vectors = fields.shape
    half = pieces[0].shape[0]
    group = lax.axis_index("walk")
    b = lax.rem(lax.axis_index("chol"), 2)
    wanted = source[...]
    bias = jnp.zeros((per_group, vectors), F32)
    for (dw, db), piece in zip(origins, pieces):
        from_group = lax.rem(group + (layout.walk - dw), layout.walk)
        from_b = b + db - 2 * b * db
        base = from_group * per_group + from_b * half
        for row in range(half):
            bias += jnp.where(wanted == base + row, piece[row : row + 1, :], 0.0)
    bias = TAU_ROOT * bias
    bias_out[...] = bias
    shifted = (fields[...] - bias).astype(BF16)
    slot = jnp.zeros((per_group * BLOCK, 1), jnp.int32)
    place = lax.broadcasted_iota(jnp.int32, slot.shape, 0) // BLOCK
    for at in range(per_group):
        slot = jnp.where(place == at, order[lax.rem(at + b * half, per_group)], slot)
    tall = (per_group * BLOCK, per_group)
    rows = (lax.broadcasted_iota(jnp.int32, tall, 1) == slot).astype(BF16)
    wide = (vectors, vectors * BLOCK)
    columns = (
        lax.broadcasted_iota(jnp.int32, wide, 1) // BLOCK
        == lax.broadcasted_iota(jnp.int32, wide, 0)
    ).astype(BF16)
    spread = jnp.dot(rows, shifted, preferred_element_type=F32).astype(BF16)
    spread = jnp.dot(spread, columns, preferred_element_type=F32)
    same = lax.rem(lax.broadcasted_iota(jnp.int32, spread.shape, 0), BLOCK) == lax.rem(
        lax.broadcasted_iota(jnp.int32, spread.shape, 1), BLOCK
    )
    weights[...] = jnp.where(same, spread, 0.0).astype(BF16)


def weights_of(layout, order, fields, source, pieces):
    per_group, vectors = fields.shape
    origins = [origin for origin, _ in pieces]
    arrays = [array for _, array in pieces]
    return pl.pallas_call(
        functools.partial(weights_kernel, origins, layout),
        out_shape=[
            jax.ShapeDtypeStruct((per_group, vectors), F32),
            jax.ShapeDtypeStruct((per_group * BLOCK, vectors * BLOCK), BF16),
        ],
        in_specs=[pl.BlockSpec(memory_space=pltpu.SMEM)] + vmem_specs(2 + len(arrays)),
        out_specs=vmem_specs(2),
        compiler_params=params(8),
    )(order, fields, source, *arrays)


def potential_kernel(start, weights, cholesky, kept, sent, blocks, semaphores):
    vectors, orbitals = cholesky.shape[0], cholesky.shape[2]
    half = kept.shape[0]
    copies = []
    for at in range(blocks.shape[0]):
        rows = pl.ds(start + at * BLOCK, BLOCK)
        copies.append(
            pltpu.make_async_copy(cholesky.at[:, rows, :], blocks.at[at], semaphores.at[at])
        )
    for copy in copies:
        copy.start()
    for at, copy in enumerate(copies):
        copy.wait()
        block = blocks[at].reshape(vectors * BLOCK, orbitals)
        result = TAU_ROOT * jnp.dot(weights[...], block, preferred_element_type=F32)
        result = result.astype(BF16).reshape(2 * half, BLOCK, orbitals)
        kept[:, at * BLOCK : (at + 1) * BLOCK, :] = result[:half]
        sent[:, at * BLOCK : (at + 1) * BLOCK, :] = result[half:]


def potential_of(weights, cholesky, part, parts):
    vectors, rows, orbitals = cholesky.shape
    half = weights.shape[0] // BLOCK // 2
    rows = rows // parts
    out = jax.ShapeDtypeStruct((half, rows, orbitals), BF16)
    return pl.pallas_call(
        functools.partial(potential_kernel, part * rows),
        out_shape=[out, out],
        in_specs=vmem_specs(1) + [pl.BlockSpec(memory_space=pltpu.HBM)],
        out_specs=vmem_specs(2),
        scratch_shapes=[
            pltpu.VMEM((rows // BLOCK, vectors, BLOCK, orbitals), BF16),
            pltpu.SemaphoreType.DMA((rows // BLOCK,)),
        ],
        compiler_params=params(48),
    )(weights, cholesky)


def fold(layout, places, kept, theirs, pieces, buffer, walker):
    index = lax.axis_index("chol")
    z, y = index // 4, lax.rem(index // 2, 2)
    for piece, (count, first, dz, dy) in zip(pieces, places):
        if first <= walker < first + count:
            chip = lax.rem(z + (layout.z - dz), layout.z) * 2 + (y + dy - 2 * y * dy)
            buffer[walker, chip] = piece[walker - first]
    rows = jnp.concatenate([part[walker] for part in (*kept, *theirs)], axis=0)
    full = buffer[walker]
    return jnp.dot(rows, full.reshape(-1, full.shape[-1]), preferred_element_type=F32)


def first_kernel(layout, places, parts, sizes, *refs):
    kept, theirs, refs = refs[:parts], refs[parts : 2 * parts], refs[2 * parts :]
    base, buffer = refs[-2:]
    outs = refs[-2 - len(sizes) : -2]
    pieces = refs[: -2 - len(sizes)]
    b = lax.rem(lax.axis_index("chol"), 2)
    own_chip = lax.axis_index("chol") // 2
    number, walker = 0, 0
    for number, size in enumerate(sizes):
        for at in range(size):
            term = fold(layout, places, kept, theirs, pieces, buffer, walker)
            rows = term.shape[0] // 2
            for block, value in ((b, term[:rows]), (1 - b, term[rows:])):
                outs[number][at, block] = value.astype(BF16)
                base[walker, block] = buffer[walker, own_chip, block].astype(F32) + value
            walker += 1


def second_kernel(layout, places, parts, *refs):
    kept, theirs, refs = refs[:parts], refs[parts : 2 * parts], refs[2 * parts :]
    base, pieces, (mine, sent, buffer) = refs[0], refs[1:-3], refs[-3:]
    b = lax.rem(lax.axis_index("chol"), 2)
    for walker in range(base.shape[0]):
        term = fold(layout, places, kept, theirs, pieces, buffer, walker)
        rows = term.shape[0] // 2
        mine[walker] = (base[walker, b] + 0.5 * term[:rows]).astype(BF16)
        sent[walker] = (base[walker, 1 - b] + 0.5 * term[rows:]).astype(BF16)


def operands_of(pieces):
    arrays = [piece[0] for piece in pieces]
    return arrays, [(piece[0].shape[0], *piece[1:]) for piece in pieces]


def fold_cost(half, rows, orbitals, electrons):
    return pl.CostEstimate(
        flops=4 * half * rows * orbitals * electrons,
        bytes_accessed=2 * half * orbitals * (2 * rows + electrons),
        transcendentals=0,
    )


def first_of(layout, kept, theirs, pieces, sizes):
    arrays, places = operands_of(pieces)
    half, _, orbitals = kept[0].shape
    _, rows, electrons = arrays[0].shape[-3:]
    return pl.pallas_call(
        functools.partial(first_kernel, layout, places, len(kept), sizes),
        out_shape=[jax.ShapeDtypeStruct((size, 2, rows, electrons), BF16) for size in sizes]
        + [jax.ShapeDtypeStruct((half, 2, rows, electrons), F32)],
        in_specs=vmem_specs(2 * len(kept) + len(arrays)),
        out_specs=vmem_specs(len(sizes) + 1),
        scratch_shapes=[pltpu.VMEM((half, orbitals // (2 * rows), 2, rows, electrons), BF16)],
        compiler_params=params(16),
        cost_estimate=fold_cost(half, rows, orbitals, electrons),
    )(*kept, *theirs, *arrays)


def second_of(layout, kept, theirs, base, pieces):
    arrays, places = operands_of(pieces)
    half, _, orbitals = kept[0].shape
    _, rows, electrons = arrays[0].shape[-3:]
    out = jax.ShapeDtypeStruct((half, rows, electrons), BF16)
    return pl.pallas_call(
        functools.partial(second_kernel, layout, places, len(kept)),
        out_shape=[out, out],
        in_specs=vmem_specs(2 * len(kept) + 1 + len(arrays)),
        out_specs=vmem_specs(2),
        scratch_shapes=[pltpu.VMEM((half, orbitals // (2 * rows), 2, rows, electrons), BF16)],
        compiler_params=params(16),
        cost_estimate=fold_cost(half, rows, orbitals, electrons),
    )(*kept, *theirs, base, *arrays)


def place_kernel(order, mine, theirs, out):
    half = mine.shape[0]
    b = lax.rem(lax.axis_index("chol"), 2)
    for walker in range(half):
        out[order[b * half + walker]] = mine[walker]
        out[order[(1 - b) * half + walker]] = theirs[walker]


def place(order, mine, theirs):
    half, rows, electrons = mine.shape
    return pl.pallas_call(
        place_kernel,
        out_shape=jax.ShapeDtypeStruct((2 * half, rows, electrons), BF16),
        in_specs=[pl.BlockSpec(memory_space=pltpu.SMEM)] + vmem_specs(2),
        out_specs=pl.BlockSpec(memory_space=pltpu.VMEM),
        compiler_params=params(8),
    )(order, mine, theirs)


def split_kernel(source, walkers, first, second, order, picked, semaphores):
    per_group = walkers.shape[0]
    half = per_group // 2
    group = lax.axis_index("walk")
    b = lax.rem(lax.axis_index("chol"), 2)
    stayed, arrived, sent = jnp.int32(0), jnp.int32(0), jnp.int32(0)
    for slot in range(per_group):
        local = source[group * per_group + slot] - group * per_group
        stays = ((local >= 0) & (local < per_group)).astype(jnp.int32)
        at = jnp.where(stays == 1, jnp.minimum(stayed, half - 1), per_group)
        picked[at] = local
        at = jnp.where(stays == 1, stayed, half + arrived)
        order[jnp.minimum(at, per_group - 1)] = jnp.int32(slot)
        stayed, arrived = stayed + stays, arrived + 1 - stays
        local = source[(1 - group) * per_group + slot] - group * per_group
        goes = ((local >= 0) & (local < per_group)).astype(jnp.int32)
        at = jnp.where(goes == 1, half + jnp.minimum(sent, half - 1), per_group)
        picked[at] = local
        sent = sent + goes
    copies = []
    for target, offset in ((second, (1 - b) * half), (first, b * half)):
        for walker in range(half):
            copies.append(
                pltpu.make_async_copy(
                    walkers.at[picked[offset + walker]],
                    target.at[walker],
                    semaphores.at[len(copies)],
                )
            )
    for copy in copies:
        copy.start()
    for copy in copies:
        copy.wait()


def split_walkers(walkers, source):
    per_group, rows, electrons = walkers.shape
    half = jax.ShapeDtypeStruct((per_group // 2, rows, electrons), walkers.dtype)
    return pl.pallas_call(
        split_kernel,
        out_shape=[half, half, jax.ShapeDtypeStruct((per_group,), jnp.int32)],
        in_specs=[pl.BlockSpec(memory_space=pltpu.SMEM), pl.BlockSpec(memory_space=pltpu.HBM)],
        out_specs=[pl.BlockSpec(memory_space=pl.ANY)] * 2
        + [pl.BlockSpec(memory_space=pltpu.SMEM)],
        scratch_shapes=[
            pltpu.SMEM((per_group + 1,), jnp.int32),
            pltpu.SemaphoreType.DMA((per_group,)),
        ],
        compiler_params=params(4),
    )(source, walkers)


def ranks(flags):
    count = flags.shape[-1]
    before = jnp.arange(count)[None, :] < jnp.arange(count)[:, None]
    return jnp.sum(jnp.where(before & flags[..., None, :], 1, 0), axis=-1)


def migrate(layout, walkers, source):
    per_group = walkers.shape[0]
    half = per_group // 2
    group = lax.axis_index("walk")
    if layout.walk == 2:
        first, second, order = split_walkers(walkers, source)
        near, cross = [], []
        for index in range(2 * layout.chol):
            across = (index + layout.chol) % (2 * layout.chol)
            if index % 2 == 0:
                near.append((index, index))
                cross.append((index, across + 1))
            else:
                near.append((index, across))
                cross.append((index, index - 1))
        axes = ("walk", "chol")
        return lax.ppermute(first, axes, near), lax.ppermute(second, axes, cross), order
    table = source.reshape(layout.walk, per_group)
    incoming = lax.dynamic_index_in_dim(table, group, 0, keepdims=False)
    incoming_groups = incoming // per_group

    def outgoing(distance):
        row = lax.dynamic_index_in_dim(table, (group + distance) % layout.walk, 0, keepdims=False)
        local = row - group * per_group
        here = (local >= 0) & (local < per_group)
        match = here[None, :] & (ranks(here)[None, :] == jnp.arange(half)[:, None])
        return jnp.take(walkers, jnp.sum(jnp.where(match, local[None, :], 0), axis=1), axis=0)

    arrived = [outgoing(0)]
    for distance in range(1, layout.walk):
        pairs = [(g, (g + distance) % layout.walk) for g in range(layout.walk)]
        arrived.append(lax.ppermute(outgoing(distance), "walk", pairs))
    slots = jnp.arange(per_group)
    same = (incoming_groups[:, None] == incoming_groups[None, :]) & (slots[None, :] < slots[:, None])
    rank = jnp.sum(same.astype(jnp.int32), axis=1)
    distance = (group - incoming_groups) % layout.walk
    migrated = jnp.take(jnp.concatenate(arrived, axis=0), distance * half + rank, axis=0)
    b = lax.axis_index("chol") % 2
    mine = lax.dynamic_slice_in_dim(migrated, b * half, half, 0)
    theirs = lax.dynamic_slice_in_dim(migrated, (1 - b) * half, half, 0)
    return mine, layout.shift(theirs, db=1), slots.astype(jnp.int32)


def shards(layout, walkers, trial, cholesky, rotated, fields, source):
    per_group = walkers.shape[0]
    half = per_group // 2
    group = lax.axis_index("walk")
    b = lax.axis_index("chol") % 2
    own, other, order = migrate(layout, walkers, source)
    trial_theirs = layout.shift(trial, db=1)
    theirs = layout.shift(walkers, db=1)
    rot_theirs = layout.shift(rotated, db=1)
    places = layout.z == half
    partial = intersections_of(walkers, theirs, trial, trial_theirs, places)
    if places:
        messages = [layout.shift(partial[dz], dz=dz) for dz in range(1, half)]
        messages, own, other = lax.optimization_barrier((messages, own, other))
        total, message = sum_of(partial[0], messages)
        inverse = newton_of(total, [layout.shift(message, dy=1)])
    chunk = jnp.stack([jnp.where(b == 0, own, other), jnp.where(b == 0, other, own)], axis=1)
    migrated = Stream(layout, chunk)
    if places:
        (inverse,) = migrated.advance((inverse,))
        inverses = [inverse] + [layout.shift(inverse, dz=dz) for dz in range(1, half)]
    else:
        spread = jnp.zeros((per_group,) + partial[0].shape, F32)
        spread = lax.dynamic_update_slice_in_dim(spread, jnp.stack(partial), b * half, 0)
        summed = lax.dynamic_slice_in_dim(lax.psum(spread, "chol"), b * half, half, 0)
        inverses = [newton_of(summed[index]) for index in range(half)]
    inverses = migrated.advance(inverses)

    total = bias_of(walkers, theirs, rotated, rot_theirs, inverses, places)
    distance = layout.z // 2
    while distance:
        total = total + layout.swap(total, distance)
        distance //= 2
    total = total + layout.shift(total, dy=1)
    pieces = []
    for dw in range(layout.walk):
        for db in range(2):
            moved = layout.shift_all(total, dw, db) if dw + db else total
            pieces.append(((dw, db), moved))

    wanted = lax.dynamic_slice_in_dim(source, group * per_group, per_group)[:, None]
    force_bias, weights = weights_of(layout, order, fields, wanted, pieces)
    (weights,) = migrated.advance((weights,))
    kept, received = [], []
    for part in range(2):
        mine, sent = potential_of(weights, cholesky, part, 2)
        kept.append(mine)
        received.append(layout.shift(sent, db=1))

    while len(migrated.across) < layout.z:
        migrated.advance()
    sizes = (half // 2, half - half // 2)
    *firsts, base = first_of(layout, kept, received, migrated.pieces(), sizes)
    streams = [Stream(layout, first, at * sizes[0]) for at, first in enumerate(firsts)]
    for _ in range(layout.z):
        for stream in streams:
            stream.advance()
    gathered = [piece for stream in streams for piece in stream.pieces()]
    mine, sent = second_of(layout, kept, received, base, gathered)
    return place(order, mine, layout.shift(sent, db=1)), force_bias


def solution(mesh):
    in_specs = (
        P("walk", "chol", None),
        P("chol", None),
        P(None, "chol", None),
        P(None, "chol", None),
        P("walk", None),
        P(),
    )
    out_specs = (P("walk", "chol", None), P("walk", None))
    layout = Layout(mesh.shape["walk"], mesh.shape["chol"])
    return jax.shard_map(
        functools.partial(shards, layout),
        mesh=mesh,
        in_specs=in_specs,
        out_specs=out_specs,
        check_vma=False,
    )
```

```python
import functools

import jax
import jax.numpy as jnp
from jax import lax
from jax.experimental import pallas as pl
from jax.experimental.pallas import tpu as pltpu
from jax.sharding import PartitionSpec as P

ITERS = 3
TAU_ROOT = 0.1
BLOCK = 16
HIGHEST = lax.Precision.HIGHEST
MIB = 1024 * 1024

F32 = jnp.float32
BF16 = jnp.bfloat16


def params(mebibytes):
    return pltpu.CompilerParams(vmem_limit_bytes=mebibytes * MIB)


def vmem_specs(count):
    return [pl.BlockSpec(memory_space=pltpu.VMEM)] * count


class Layout:
    def __init__(self, walk_size, chol_size):
        self.walk = walk_size
        self.chol = chol_size
        self.z = chol_size // 4

    def shift(self, array, dz=0, dy=0, db=0):
        pairs = []
        for index in range(self.chol):
            z, y, b = index // 4, (index // 2) % 2, index % 2
            target = (((z + dz) % self.z) * 2 + (y ^ dy)) * 2 + (b ^ db)
            pairs.append((index, target))
        return lax.ppermute(array, "chol", pairs)

    def swap(self, array, distance):
        pairs = [(i, (((i // 4) ^ distance) * 4) + i % 4) for i in range(self.chol)]
        return lax.ppermute(array, "chol", pairs)


class Stream:
    def __init__(self, layout, piece, walker=0):
        self.layout = layout
        self.walker = walker
        self.ring = [piece]
        self.across = []

    def advance(self, anchors=()):
        if len(self.across) == self.layout.z:
            return anchors
        latest = self.ring[-1]
        moved = [self.layout.shift(latest, dy=1)]
        last = len(self.ring) == self.layout.z
        if not last:
            moved.append(self.layout.shift(latest, dz=1))
        if anchors or not last:
            anchors, moved = lax.optimization_barrier((anchors, moved))
        self.across.append(moved[0])
        self.ring.extend(moved[1:])
        return anchors

    def pieces(self):
        ring = [(array, self.walker, dz, 0) for dz, array in enumerate(self.ring)]
        return ring + [(array, self.walker, dz, 1) for dz, array in enumerate(self.across)]


def gathered(layout, dz, dy):
    index = lax.axis_index("chol")
    z, y = index // 4, lax.rem(index // 2, 2)
    return lax.rem(z + (layout.z - dz), layout.z) * 2 + (y + dy - 2 * y * dy)


def transpose_kernel(layout, mine, theirs, out, buffer):
    b = lax.rem(lax.axis_index("chol"), 2)
    for dz in range(layout.z):
        for dy in range(2):
            chip = gathered(layout, dz, dy)
            buffer[chip, b] = mine[dz, dy]
            buffer[chip, 1 - b] = theirs[dz, dy]
    out[...] = buffer[...].reshape(-1, buffer.shape[-1]).T


def transposed(layout, mine, theirs):
    _, _, rows, electrons = mine.shape
    chips = layout.chol // 2
    return pl.pallas_call(
        functools.partial(transpose_kernel, layout),
        out_shape=jax.ShapeDtypeStruct((electrons, layout.chol * rows), BF16),
        in_specs=vmem_specs(2),
        out_specs=pl.BlockSpec(memory_space=pltpu.VMEM),
        scratch_shapes=[pltpu.VMEM((chips, 2, rows, electrons), BF16)],
        compiler_params=params(8),
    )(mine, theirs)


def newton_inverses(matrices):
    shape = matrices[0].shape
    same = lax.broadcasted_iota(jnp.int32, shape, 0) == lax.broadcasted_iota(jnp.int32, shape, 1)
    twice = jnp.where(same, 2.0, 0.0).astype(F32)
    estimates = [twice - matrix for matrix in matrices]
    for _ in range(ITERS - 1):
        products = [
            jnp.dot(matrix, estimate, precision=HIGHEST, preferred_element_type=F32)
            for matrix, estimate in zip(matrices, estimates)
        ]
        estimates = [
            jnp.dot(estimate, twice - product, precision=HIGHEST, preferred_element_type=F32)
            for estimate, product in zip(estimates, products)
        ]
    return estimates


def inverse_kernel(layout, places, trial, *refs):
    pieces, (out, buffer) = refs[:-2], refs[-2:]
    matrices = []
    for walker in range(out.shape[0]):
        for piece, (dz, dy) in zip(pieces, places):
            buffer[walker, gathered(layout, dz, dy)] = piece[walker]
        full = buffer[walker]
        full = full.reshape(-1, full.shape[-1])
        matrices.append(jnp.dot(trial[...], full, preferred_element_type=F32))
    for walker, inverse in enumerate(newton_inverses(matrices)):
        out[walker] = inverse.astype(out.dtype)


def inverses_of(layout, trial, stream):
    arrays = [piece[0] for piece in stream.pieces()]
    places = [piece[2:] for piece in stream.pieces()]
    count, _, rows, electrons = arrays[0].shape
    return pl.pallas_call(
        functools.partial(inverse_kernel, layout, places),
        out_shape=jax.ShapeDtypeStruct((count, electrons, electrons), BF16),
        in_specs=vmem_specs(1 + len(arrays)),
        out_specs=pl.BlockSpec(memory_space=pltpu.VMEM),
        scratch_shapes=[pltpu.VMEM((count, layout.chol // 2, 2, rows, electrons), BF16)],
        compiler_params=params(16),
    )(trial, *arrays)


def bias_kernel(sizes, rot_mine, rot_theirs, *refs):
    streams = len(sizes)
    chunks, inverses, (out, greens) = refs[:streams], refs[streams : 2 * streams], refs[-2:]
    vectors, rows, electrons = rot_mine.shape
    b = lax.rem(lax.axis_index("chol"), 2)
    count = 0
    for chunk, inverse, size in zip(chunks, inverses, sizes):
        for walker in range(size):
            both = chunk[walker].reshape(2 * rows, electrons)
            product = jnp.dot(both, inverse[walker], preferred_element_type=F32).astype(BF16)
            greens[:, :, count] = product.reshape(2, rows // BLOCK, BLOCK, electrons)
            count += 1
    total = jnp.zeros((vectors * BLOCK, count * BLOCK), F32)
    for half, rot in ((b, rot_mine), (1 - b, rot_theirs)):
        for block in range(rows // BLOCK):
            total += lax.dot_general(
                rot[:, block * BLOCK : (block + 1) * BLOCK, :].reshape(vectors * BLOCK, electrons),
                greens[half, block].reshape(count * BLOCK, electrons),
                (((1,), (1,)), ((), ())),
                preferred_element_type=F32,
            )
    same = lax.rem(lax.broadcasted_iota(jnp.int32, total.shape, 0), BLOCK) == lax.rem(
        lax.broadcasted_iota(jnp.int32, total.shape, 1), BLOCK
    )
    summed = jnp.sum(
        jnp.where(same, total, 0.0).reshape(vectors, BLOCK, count * BLOCK), axis=1
    )
    shape = (count, count * BLOCK)
    pick = (
        lax.broadcasted_iota(jnp.int32, shape, 1) // BLOCK
        == lax.broadcasted_iota(jnp.int32, shape, 0)
    ).astype(F32)
    out[...] = lax.dot_general(
        pick, summed, (((1,), (1,)), ((), ())), precision=HIGHEST, preferred_element_type=F32
    )


def bias_of(chunks, inverses, rot_mine, rot_theirs):
    vectors, rows, electrons = rot_mine.shape
    sizes = [chunk.shape[0] for chunk in chunks]
    count = sum(sizes)
    return pl.pallas_call(
        functools.partial(bias_kernel, sizes),
        out_shape=jax.ShapeDtypeStruct((count, vectors), F32),
        in_specs=vmem_specs(2 + 2 * len(sizes)),
        out_specs=pl.BlockSpec(memory_space=pltpu.VMEM),
        scratch_shapes=[pltpu.VMEM((2, rows // BLOCK, count, BLOCK, electrons), BF16)],
        compiler_params=params(12),
        cost_estimate=pl.CostEstimate(
            flops=4 * count * rows * electrons * (electrons + vectors * BLOCK),
            bytes_accessed=4 * (vectors + count) * rows * electrons,
            transcendentals=0,
        ),
    )(rot_mine, rot_theirs, *chunks, *inverses)


def weights_kernel(order, fields, mine, theirs, bias_out, weights):
    per_group, vectors = fields.shape
    half = mine.shape[0]
    b = lax.rem(lax.axis_index("chol"), 2)
    row = lax.broadcasted_iota(jnp.int32, (per_group, vectors), 0)
    bias = jnp.zeros((per_group, vectors), F32)
    for walker in range(half):
        for part, core in ((mine, b), (theirs, 1 - b)):
            slot = order[core * half + walker]
            bias += jnp.where(row == slot, part[walker : walker + 1, :], 0.0)
    bias = TAU_ROOT * bias
    bias_out[...] = bias
    shifted = (fields[...] - bias).astype(BF16)
    slot = jnp.zeros((per_group * BLOCK, 1), jnp.int32)
    place = lax.broadcasted_iota(jnp.int32, slot.shape, 0) // BLOCK
    for at in range(per_group):
        slot = jnp.where(place == at, order[lax.rem(at + b * half, per_group)], slot)
    tall = (per_group * BLOCK, per_group)
    rows = (lax.broadcasted_iota(jnp.int32, tall, 1) == slot).astype(BF16)
    wide = (vectors, vectors * BLOCK)
    columns = (
        lax.broadcasted_iota(jnp.int32, wide, 1) // BLOCK
        == lax.broadcasted_iota(jnp.int32, wide, 0)
    ).astype(BF16)
    spread = jnp.dot(rows, shifted, preferred_element_type=F32).astype(BF16)
    spread = jnp.dot(spread, columns, preferred_element_type=F32)
    same = lax.rem(lax.broadcasted_iota(jnp.int32, spread.shape, 0), BLOCK) == lax.rem(
        lax.broadcasted_iota(jnp.int32, spread.shape, 1), BLOCK
    )
    weights[...] = jnp.where(same, spread, 0.0).astype(BF16)


def weights_of(order, fields, mine, theirs):
    per_group, vectors = fields.shape
    return pl.pallas_call(
        weights_kernel,
        out_shape=[
            jax.ShapeDtypeStruct((per_group, vectors), F32),
            jax.ShapeDtypeStruct((per_group * BLOCK, vectors * BLOCK), BF16),
        ],
        in_specs=[pl.BlockSpec(memory_space=pltpu.SMEM)] + vmem_specs(3),
        out_specs=vmem_specs(2),
        compiler_params=params(8),
    )(order, fields, mine, theirs)


def potential_kernel(start, weights, cholesky, kept, sent, blocks, semaphores):
    vectors, orbitals = cholesky.shape[0], cholesky.shape[2]
    half = kept.shape[0]
    copies = []
    for at in range(blocks.shape[0]):
        rows = pl.ds(start + at * BLOCK, BLOCK)
        copies.append(
            pltpu.make_async_copy(cholesky.at[:, rows, :], blocks.at[at], semaphores.at[at])
        )
    for copy in copies:
        copy.start()
    for at, copy in enumerate(copies):
        copy.wait()
        block = blocks[at].reshape(vectors * BLOCK, orbitals)
        result = TAU_ROOT * jnp.dot(weights[...], block, preferred_element_type=F32)
        result = result.astype(BF16).reshape(2 * half, BLOCK, orbitals)
        kept[:, at * BLOCK : (at + 1) * BLOCK, :] = result[:half]
        sent[:, at * BLOCK : (at + 1) * BLOCK, :] = result[half:]


def potential_of(weights, cholesky, part, parts):
    vectors, rows, orbitals = cholesky.shape
    half = weights.shape[0] // BLOCK // 2
    rows = rows // parts
    out = jax.ShapeDtypeStruct((half, rows, orbitals), BF16)
    return pl.pallas_call(
        functools.partial(potential_kernel, part * rows),
        out_shape=[out, out],
        in_specs=vmem_specs(1) + [pl.BlockSpec(memory_space=pltpu.HBM)],
        out_specs=vmem_specs(2),
        scratch_shapes=[
            pltpu.VMEM((rows // BLOCK, vectors, BLOCK, orbitals), BF16),
            pltpu.SemaphoreType.DMA((rows // BLOCK,)),
        ],
        compiler_params=params(48),
    )(weights, cholesky)


def fold(layout, places, kept, theirs, pieces, buffer, walker):
    for piece, (count, first, dz, dy) in zip(pieces, places):
        if first <= walker < first + count:
            buffer[walker, gathered(layout, dz, dy)] = piece[walker - first]
    rows = jnp.concatenate([part[walker] for part in (*kept, *theirs)], axis=0)
    full = buffer[walker]
    return jnp.dot(rows, full.reshape(-1, full.shape[-1]), preferred_element_type=F32)


def first_kernel(layout, places, parts, sizes, *refs):
    kept, theirs, refs = refs[:parts], refs[parts : 2 * parts], refs[2 * parts :]
    base, buffer = refs[-2:]
    outs = refs[-2 - len(sizes) : -2]
    pieces = refs[: -2 - len(sizes)]
    b = lax.rem(lax.axis_index("chol"), 2)
    own_chip = lax.axis_index("chol") // 2
    number, walker = 0, 0
    for number, size in enumerate(sizes):
        for at in range(size):
            term = fold(layout, places, kept, theirs, pieces, buffer, walker)
            rows = term.shape[0] // 2
            for block, value in ((b, term[:rows]), (1 - b, term[rows:])):
                outs[number][at, block] = value.astype(BF16)
                base[walker, block] = buffer[walker, own_chip, block].astype(F32) + value
            walker += 1


def second_kernel(layout, places, parts, *refs):
    kept, theirs, refs = refs[:parts], refs[parts : 2 * parts], refs[2 * parts :]
    base, pieces, (mine, sent, buffer) = refs[0], refs[1:-3], refs[-3:]
    b = lax.rem(lax.axis_index("chol"), 2)
    for walker in range(base.shape[0]):
        term = fold(layout, places, kept, theirs, pieces, buffer, walker)
        rows = term.shape[0] // 2
        mine[walker] = (base[walker, b] + 0.5 * term[:rows]).astype(BF16)
        sent[walker] = (base[walker, 1 - b] + 0.5 * term[rows:]).astype(BF16)


def operands_of(pieces):
    arrays = [piece[0] for piece in pieces]
    return arrays, [(piece[0].shape[0], *piece[1:]) for piece in pieces]


def fold_cost(half, rows, orbitals, electrons):
    return pl.CostEstimate(
        flops=4 * half * rows * orbitals * electrons,
        bytes_accessed=2 * half * orbitals * (2 * rows + electrons),
        transcendentals=0,
    )


def first_of(layout, kept, theirs, pieces, sizes):
    arrays, places = operands_of(pieces)
    half, _, orbitals = kept[0].shape
    _, rows, electrons = arrays[0].shape[-3:]
    return pl.pallas_call(
        functools.partial(first_kernel, layout, places, len(kept), sizes),
        out_shape=[jax.ShapeDtypeStruct((size, 2, rows, electrons), BF16) for size in sizes]
        + [jax.ShapeDtypeStruct((half, 2, rows, electrons), F32)],
        in_specs=vmem_specs(2 * len(kept) + len(arrays)),
        out_specs=vmem_specs(len(sizes) + 1),
        scratch_shapes=[pltpu.VMEM((half, orbitals // (2 * rows), 2, rows, electrons), BF16)],
        compiler_params=params(16),
        cost_estimate=fold_cost(half, rows, orbitals, electrons),
    )(*kept, *theirs, *arrays)


def second_of(layout, kept, theirs, base, pieces):
    arrays, places = operands_of(pieces)
    half, _, orbitals = kept[0].shape
    _, rows, electrons = arrays[0].shape[-3:]
    out = jax.ShapeDtypeStruct((half, rows, electrons), BF16)
    return pl.pallas_call(
        functools.partial(second_kernel, layout, places, len(kept)),
        out_shape=[out, out],
        in_specs=vmem_specs(2 * len(kept) + 1 + len(arrays)),
        out_specs=vmem_specs(2),
        scratch_shapes=[pltpu.VMEM((half, orbitals // (2 * rows), 2, rows, electrons), BF16)],
        compiler_params=params(16),
        cost_estimate=fold_cost(half, rows, orbitals, electrons),
    )(*kept, *theirs, base, *arrays)


def place_kernel(order, mine, theirs, out):
    half = mine.shape[0]
    b = lax.rem(lax.axis_index("chol"), 2)
    for walker in range(half):
        out[order[b * half + walker]] = mine[walker]
        out[order[(1 - b) * half + walker]] = theirs[walker]


def place(order, mine, theirs):
    half, rows, electrons = mine.shape
    return pl.pallas_call(
        place_kernel,
        out_shape=jax.ShapeDtypeStruct((2 * half, rows, electrons), BF16),
        in_specs=[pl.BlockSpec(memory_space=pltpu.SMEM)] + vmem_specs(2),
        out_specs=pl.BlockSpec(memory_space=pltpu.VMEM),
        compiler_params=params(8),
    )(order, mine, theirs)


def split_kernel(source, walkers, first, second, order, picked, semaphores):
    per_group = walkers.shape[0]
    half = per_group // 2
    group = lax.axis_index("walk")
    b = lax.rem(lax.axis_index("chol"), 2)
    stayed, arrived, sent = jnp.int32(0), jnp.int32(0), jnp.int32(0)
    for slot in range(per_group):
        local = source[group * per_group + slot] - group * per_group
        stays = ((local >= 0) & (local < per_group)).astype(jnp.int32)
        at = jnp.where(stays == 1, jnp.minimum(stayed, half - 1), per_group)
        picked[at] = local
        at = jnp.where(stays == 1, stayed, half + arrived)
        order[jnp.minimum(at, per_group - 1)] = jnp.int32(slot)
        stayed, arrived = stayed + stays, arrived + 1 - stays
        local = source[(1 - group) * per_group + slot] - group * per_group
        goes = ((local >= 0) & (local < per_group)).astype(jnp.int32)
        at = jnp.where(goes == 1, half + jnp.minimum(sent, half - 1), per_group)
        picked[at] = local
        sent = sent + goes
    copies = []
    for target, offset in ((second, (1 - b) * half), (first, b * half)):
        for walker in range(half):
            copies.append(
                pltpu.make_async_copy(
                    walkers.at[picked[offset + walker]],
                    target.at[walker],
                    semaphores.at[len(copies)],
                )
            )
    for copy in copies:
        copy.start()
    for copy in copies:
        copy.wait()


def split_walkers(walkers, source):
    per_group, rows, electrons = walkers.shape
    half = jax.ShapeDtypeStruct((per_group // 2, rows, electrons), walkers.dtype)
    return pl.pallas_call(
        split_kernel,
        out_shape=[half, half, jax.ShapeDtypeStruct((per_group,), jnp.int32)],
        in_specs=[pl.BlockSpec(memory_space=pltpu.SMEM), pl.BlockSpec(memory_space=pltpu.HBM)],
        out_specs=[pl.BlockSpec(memory_space=pl.ANY)] * 2
        + [pl.BlockSpec(memory_space=pltpu.SMEM)],
        scratch_shapes=[
            pltpu.SMEM((per_group + 1,), jnp.int32),
            pltpu.SemaphoreType.DMA((per_group,)),
        ],
        compiler_params=params(4),
    )(source, walkers)


def ranks(flags):
    count = flags.shape[-1]
    before = jnp.arange(count)[None, :] < jnp.arange(count)[:, None]
    return jnp.sum(jnp.where(before & flags[..., None, :], 1, 0), axis=-1)


def migrate(layout, walkers, source):
    per_group = walkers.shape[0]
    half = per_group // 2
    group = lax.axis_index("walk")
    if layout.walk == 2:
        first, second, order = split_walkers(walkers, source)
        near, cross = [], []
        for index in range(2 * layout.chol):
            across = (index + layout.chol) % (2 * layout.chol)
            if index % 2 == 0:
                near.append((index, index))
                cross.append((index, across + 1))
            else:
                near.append((index, across))
                cross.append((index, index - 1))
        axes = ("walk", "chol")
        return lax.ppermute(first, axes, near), lax.ppermute(second, axes, cross), order
    table = source.reshape(layout.walk, per_group)
    incoming = lax.dynamic_index_in_dim(table, group, 0, keepdims=False)
    incoming_groups = incoming // per_group

    def outgoing(distance):
        row = lax.dynamic_index_in_dim(table, (group + distance) % layout.walk, 0, keepdims=False)
        local = row - group * per_group
        here = (local >= 0) & (local < per_group)
        match = here[None, :] & (ranks(here)[None, :] == jnp.arange(half)[:, None])
        return jnp.take(walkers, jnp.sum(jnp.where(match, local[None, :], 0), axis=1), axis=0)

    arrived = [outgoing(0)]
    for distance in range(1, layout.walk):
        pairs = [(g, (g + distance) % layout.walk) for g in range(layout.walk)]
        arrived.append(lax.ppermute(outgoing(distance), "walk", pairs))
    slots = jnp.arange(per_group)
    same = (incoming_groups[:, None] == incoming_groups[None, :]) & (slots[None, :] < slots[:, None])
    rank = jnp.sum(same.astype(jnp.int32), axis=1)
    distance = (group - incoming_groups) % layout.walk
    migrated = jnp.take(jnp.concatenate(arrived, axis=0), distance * half + rank, axis=0)
    b = lax.axis_index("chol") % 2
    mine = lax.dynamic_slice_in_dim(migrated, b * half, half, 0)
    theirs = lax.dynamic_slice_in_dim(migrated, (1 - b) * half, half, 0)
    return mine, layout.shift(theirs, db=1), slots.astype(jnp.int32)


def shards(layout, walkers, trial, cholesky, rotated, fields, source):
    half = walkers.shape[0] // 2
    sizes = (half // 2, half - half // 2)
    b = lax.axis_index("chol") % 2

    pairs = [jnp.stack([trial, layout.shift(trial, dy=1)])]
    own, other, order = migrate(layout, walkers, source)
    for _ in range(layout.z // 2):
        pairs.append(layout.shift(pairs[-1], dz=1))
    own, other, pairs = lax.optimization_barrier((own, other, pairs))
    for _ in range(layout.z - len(pairs)):
        pairs.append(layout.shift(pairs[-1], dz=1))
    chunk = jnp.stack([jnp.where(b == 0, own, other), jnp.where(b == 0, other, own)], axis=1)
    chunks = [chunk[: sizes[0]], chunk[sizes[0] :]]
    streams = [Stream(layout, chunks[0]), Stream(layout, chunks[1], sizes[0])]
    for stage in range(layout.z):
        if stage == 0:
            pairs = streams[0].advance(pairs)
            streams[1].advance()
            planes = jnp.stack(pairs)
            planes_theirs = layout.shift(planes, db=1)
            rot_theirs = layout.shift(rotated, db=1)
        elif stage == 1:
            planes_theirs, rot_theirs = streams[0].advance((planes_theirs, rot_theirs))
            streams[1].advance()
            turned = transposed(layout, planes, planes_theirs)
        elif stage == 2:
            (turned,) = streams[0].advance((turned,))
            streams[1].advance()
        else:
            for stream in streams:
                stream.advance()

    inverses = [inverses_of(layout, turned, stream) for stream in streams]
    total = bias_of(chunks, inverses, rotated, rot_theirs)
    distance = layout.z // 2
    while distance:
        total = total + layout.swap(total, distance)
        distance //= 2
    total = total + layout.shift(total, dy=1)
    force_bias, weights = weights_of(order, fields, total, layout.shift(total, db=1))
    kept, received = [], []
    for part in range(2):
        mine, sent = potential_of(weights, cholesky, part, 2)
        kept.append(mine)
        received.append(layout.shift(sent, db=1))

    pieces = [piece for stream in streams for piece in stream.pieces()]
    *firsts, base = first_of(layout, kept, received, pieces, sizes)
    streams = [Stream(layout, firsts[0]), Stream(layout, firsts[1], sizes[0])]
    for _ in range(layout.z):
        for stream in streams:
            stream.advance()
    pieces = [piece for stream in streams for piece in stream.pieces()]
    mine, sent = second_of(layout, kept, received, base, pieces)
    return place(order, mine, layout.shift(sent, db=1)), force_bias


def solution(mesh):
    in_specs = (
        P("walk", "chol", None),
        P("chol", None),
        P(None, "chol", None),
        P(None, "chol", None),
        P("walk", None),
        P(),
    )
    out_specs = (P("walk", "chol", None), P("walk", None))
    layout = Layout(mesh.shape["walk"], mesh.shape["chol"])
    return jax.shard_map(
        functools.partial(shards, layout),
        mesh=mesh,
        in_specs=in_specs,
        out_specs=out_specs,
        check_vma=False,
    )
```

```python
import functools

import jax
import jax.numpy as jnp
from jax import lax
from jax.experimental import pallas as pl
from jax.experimental.pallas import tpu as pltpu
from jax.sharding import PartitionSpec as P

ITERS = 3
TAU_ROOT = 0.1
BLOCK = 16
HIGHEST = lax.Precision.HIGHEST
MIB = 1024 * 1024

F32 = jnp.float32
BF16 = jnp.bfloat16


def params(mebibytes):
    return pltpu.CompilerParams(vmem_limit_bytes=mebibytes * MIB)


def vmem_specs(count):
    return [pl.BlockSpec(memory_space=pltpu.VMEM)] * count


class Layout:
    def __init__(self, walk_size, chol_size):
        self.walk = walk_size
        self.chol = chol_size
        self.z = chol_size // 4

    def shift(self, array, dz=0, dy=0, db=0):
        pairs = []
        for index in range(self.chol):
            z, y, b = index // 4, (index // 2) % 2, index % 2
            target = (((z + dz) % self.z) * 2 + (y ^ dy)) * 2 + (b ^ db)
            pairs.append((index, target))
        return lax.ppermute(array, "chol", pairs)


class Stream:
    def __init__(self, layout, piece):
        self.layout = layout
        self.ring = [piece]
        self.across = []

    def advance(self, anchors=()):
        if len(self.across) == self.layout.z:
            return anchors
        latest = self.ring[-1]
        moved = [self.layout.shift(latest, dy=1)]
        last = len(self.ring) == self.layout.z
        if not last:
            moved.append(self.layout.shift(latest, dz=1))
        if anchors or not last:
            anchors, moved = lax.optimization_barrier((anchors, moved))
        self.across.append(moved[0])
        self.ring.extend(moved[1:])
        return anchors

    def pieces(self):
        ring = [(array, dz, 0) for dz, array in enumerate(self.ring)]
        return ring + [(array, dz, 1) for dz, array in enumerate(self.across)]


def gathered(layout, dz, dy):
    index = lax.axis_index("chol")
    z, y = index // 4, lax.rem(index // 2, 2)
    return lax.rem(z + (layout.z - dz), layout.z) * 2 + (y + dy - 2 * y * dy)


def transpose_kernel(layout, mine, theirs, out, buffer):
    b = lax.rem(lax.axis_index("chol"), 2)
    for dz in range(layout.z):
        for dy in range(2):
            chip = gathered(layout, dz, dy)
            buffer[chip, b] = mine[dz, dy]
            buffer[chip, 1 - b] = theirs[dz, dy]
    out[...] = buffer[...].reshape(-1, buffer.shape[-1]).T


def transposed(layout, mine, theirs):
    _, _, rows, electrons = mine.shape
    chips = layout.chol // 2
    return pl.pallas_call(
        functools.partial(transpose_kernel, layout),
        out_shape=jax.ShapeDtypeStruct((electrons, layout.chol * rows), BF16),
        in_specs=vmem_specs(2),
        out_specs=pl.BlockSpec(memory_space=pltpu.VMEM),
        scratch_shapes=[pltpu.VMEM((chips, 2, rows, electrons), BF16)],
        compiler_params=params(8),
    )(mine, theirs)


def newton_inverses(matrices):
    shape = matrices[0].shape
    same = lax.broadcasted_iota(jnp.int32, shape, 0) == lax.broadcasted_iota(jnp.int32, shape, 1)
    twice = jnp.where(same, 2.0, 0.0).astype(F32)
    estimates = [twice - matrix for matrix in matrices]
    for _ in range(ITERS - 1):
        products = [
            jnp.dot(matrix, estimate, precision=HIGHEST, preferred_element_type=F32)
            for matrix, estimate in zip(matrices, estimates)
        ]
        estimates = [
            jnp.dot(estimate, twice - product, precision=HIGHEST, preferred_element_type=F32)
            for estimate, product in zip(estimates, products)
        ]
    return estimates


def inverse_kernel(layout, places, trial, *refs):
    pieces, (full, out) = refs[:-2], refs[-2:]
    matrices = []
    for walker in range(out.shape[0]):
        for piece, (dz, dy) in zip(pieces, places):
            full[walker, gathered(layout, dz, dy)] = piece[walker]
        rows = full[walker].reshape(-1, full.shape[-1])
        matrices.append(jnp.dot(trial[...], rows, preferred_element_type=F32))
    for walker, inverse in enumerate(newton_inverses(matrices)):
        out[walker] = inverse.astype(out.dtype)


def inverses_of(layout, trial, stream):
    arrays = [array for array, _, _ in stream.pieces()]
    places = [place for _, *place in stream.pieces()]
    count, _, rows, electrons = arrays[0].shape
    return pl.pallas_call(
        functools.partial(inverse_kernel, layout, places),
        out_shape=[
            jax.ShapeDtypeStruct((count, layout.chol // 2, 2, rows, electrons), BF16),
            jax.ShapeDtypeStruct((count, electrons, electrons), BF16),
        ],
        in_specs=vmem_specs(1 + len(arrays)),
        out_specs=vmem_specs(2),
        compiler_params=params(8),
    )(trial, *arrays)


def bias_kernel(sizes, rot_mine, rot_theirs, *refs):
    streams = len(sizes)
    chunks, inverses, (out, greens) = refs[:streams], refs[streams : 2 * streams], refs[-2:]
    vectors, rows, electrons = rot_mine.shape
    b = lax.rem(lax.axis_index("chol"), 2)
    count = 0
    for chunk, inverse, size in zip(chunks, inverses, sizes):
        for walker in range(size):
            both = chunk[walker].reshape(2 * rows, electrons)
            product = jnp.dot(both, inverse[walker], preferred_element_type=F32).astype(BF16)
            greens[:, :, count] = product.reshape(2, rows // BLOCK, BLOCK, electrons)
            count += 1
    total = jnp.zeros((vectors * BLOCK, count * BLOCK), F32)
    for half, rot in ((b, rot_mine), (1 - b, rot_theirs)):
        for block in range(rows // BLOCK):
            total += lax.dot_general(
                rot[:, block * BLOCK : (block + 1) * BLOCK, :].reshape(vectors * BLOCK, electrons),
                greens[half, block].reshape(count * BLOCK, electrons),
                (((1,), (1,)), ((), ())),
                preferred_element_type=F32,
            )
    same = lax.rem(lax.broadcasted_iota(jnp.int32, total.shape, 0), BLOCK) == lax.rem(
        lax.broadcasted_iota(jnp.int32, total.shape, 1), BLOCK
    )
    summed = jnp.sum(
        jnp.where(same, total, 0.0).reshape(vectors, BLOCK, count * BLOCK), axis=1
    )
    shape = (count, count * BLOCK)
    pick = (
        lax.broadcasted_iota(jnp.int32, shape, 1) // BLOCK
        == lax.broadcasted_iota(jnp.int32, shape, 0)
    ).astype(F32)
    out[...] = lax.dot_general(
        pick, summed, (((1,), (1,)), ((), ())), precision=HIGHEST, preferred_element_type=F32
    )


def bias_of(chunks, inverses, rot_mine, rot_theirs):
    vectors, rows, electrons = rot_mine.shape
    sizes = [chunk.shape[0] for chunk in chunks]
    count = sum(sizes)
    return pl.pallas_call(
        functools.partial(bias_kernel, sizes),
        out_shape=jax.ShapeDtypeStruct((count, vectors), F32),
        in_specs=vmem_specs(2 + 2 * len(sizes)),
        out_specs=pl.BlockSpec(memory_space=pltpu.VMEM),
        scratch_shapes=[pltpu.VMEM((2, rows // BLOCK, count, BLOCK, electrons), BF16)],
        compiler_params=params(12),
        cost_estimate=pl.CostEstimate(
            flops=4 * count * rows * electrons * (electrons + vectors * BLOCK),
            bytes_accessed=4 * (vectors + count) * rows * electrons,
            transcendentals=0,
        ),
    )(rot_mine, rot_theirs, *chunks, *inverses)


def weights_kernel(order, fields, mine, mine_across, theirs, theirs_across, bias_out, weights):
    per_group, vectors = fields.shape
    half = mine.shape[0]
    sums = (mine[...] + mine_across[...], theirs[...] + theirs_across[...])
    b = lax.rem(lax.axis_index("chol"), 2)
    row = lax.broadcasted_iota(jnp.int32, (per_group, vectors), 0)
    bias = jnp.zeros((per_group, vectors), F32)
    for walker in range(half):
        for part, core in zip(sums, (b, 1 - b)):
            slot = order[core * half + walker]
            bias += jnp.where(row == slot, part[walker : walker + 1, :], 0.0)
    bias = TAU_ROOT * bias
    bias_out[...] = bias
    shifted = (fields[...] - bias).astype(BF16)
    slot = jnp.zeros((per_group * BLOCK, 1), jnp.int32)
    place = lax.broadcasted_iota(jnp.int32, slot.shape, 0) // BLOCK
    for at in range(per_group):
        slot = jnp.where(place == at, order[lax.rem(at + b * half, per_group)], slot)
    tall = (per_group * BLOCK, per_group)
    rows = (lax.broadcasted_iota(jnp.int32, tall, 1) == slot).astype(BF16)
    wide = (vectors, vectors * BLOCK)
    columns = (
        lax.broadcasted_iota(jnp.int32, wide, 1) // BLOCK
        == lax.broadcasted_iota(jnp.int32, wide, 0)
    ).astype(BF16)
    spread = jnp.dot(rows, shifted, preferred_element_type=F32).astype(BF16)
    spread = jnp.dot(spread, columns, preferred_element_type=F32)
    same = lax.rem(lax.broadcasted_iota(jnp.int32, spread.shape, 0), BLOCK) == lax.rem(
        lax.broadcasted_iota(jnp.int32, spread.shape, 1), BLOCK
    )
    weights[...] = jnp.where(same, spread, 0.0).astype(BF16)


def weights_of(order, fields, parts):
    per_group, vectors = fields.shape
    return pl.pallas_call(
        weights_kernel,
        out_shape=[
            jax.ShapeDtypeStruct((per_group, vectors), F32),
            jax.ShapeDtypeStruct((per_group * BLOCK, vectors * BLOCK), BF16),
        ],
        in_specs=[pl.BlockSpec(memory_space=pltpu.SMEM)] + vmem_specs(5),
        out_specs=vmem_specs(2),
        compiler_params=params(8),
    )(order, fields, *parts)


def potential_kernel(start, weights, cholesky, kept, sent, blocks, semaphores):
    vectors, orbitals = cholesky.shape[0], cholesky.shape[2]
    half = kept.shape[0]
    copies = []
    for at in range(blocks.shape[0]):
        rows = pl.ds(start + at * BLOCK, BLOCK)
        copies.append(
            pltpu.make_async_copy(cholesky.at[:, rows, :], blocks.at[at], semaphores.at[at])
        )
    for copy in copies:
        copy.start()
    for at, copy in enumerate(copies):
        copy.wait()
        block = blocks[at].reshape(vectors * BLOCK, orbitals)
        result = TAU_ROOT * jnp.dot(weights[...], block, preferred_element_type=F32)
        result = result.astype(BF16).reshape(2 * half, BLOCK, orbitals)
        kept[:, at * BLOCK : (at + 1) * BLOCK, :] = result[:half]
        sent[:, at * BLOCK : (at + 1) * BLOCK, :] = result[half:]


def potential_of(weights, cholesky, part, parts):
    vectors, rows, orbitals = cholesky.shape
    half = weights.shape[0] // BLOCK // 2
    rows = rows // parts
    out = jax.ShapeDtypeStruct((half, rows, orbitals), BF16)
    return pl.pallas_call(
        functools.partial(potential_kernel, part * rows),
        out_shape=[out, out],
        in_specs=vmem_specs(1) + [pl.BlockSpec(memory_space=pltpu.HBM)],
        out_specs=vmem_specs(2),
        scratch_shapes=[
            pltpu.VMEM((rows // BLOCK, vectors, BLOCK, orbitals), BF16),
            pltpu.SemaphoreType.DMA((rows // BLOCK,)),
        ],
        compiler_params=params(48),
    )(weights, cholesky)


def first_kernel(sibling, parts, *refs):
    potential, fulls, (rounded, base) = refs[:parts], refs[parts:-2], refs[-2:]
    b = lax.rem(lax.axis_index("chol"), 2)
    chip = lax.axis_index("chol") // 2
    count = 0
    for full in fulls:
        for walker in range(full.shape[0]):
            rows = jnp.concatenate([part[count] for part in potential], axis=0)
            columns = full[walker].reshape(-1, full.shape[-1])
            term = jnp.dot(rows, columns, preferred_element_type=F32)
            rounded[count] = term.astype(BF16)
            own = full[walker, chip, 1 - b if sibling else b]
            base[count] = own.astype(F32) + term
            count += 1


def first_of(potential, fulls, sibling):
    half, _, orbitals = potential[0].shape
    rows, electrons = fulls[0].shape[-2:]
    shape = (half, rows, electrons)
    return pl.pallas_call(
        functools.partial(first_kernel, sibling, len(potential)),
        out_shape=[jax.ShapeDtypeStruct(shape, BF16), jax.ShapeDtypeStruct(shape, F32)],
        in_specs=vmem_specs(len(potential) + len(fulls)),
        out_specs=vmem_specs(2),
        compiler_params=params(8),
        cost_estimate=pl.CostEstimate(
            flops=2 * half * rows * orbitals * electrons,
            bytes_accessed=2 * half * orbitals * (rows + electrons),
            transcendentals=0,
        ),
    )(*potential, *fulls)


def second_kernel(layout, places, parts, *refs):
    kept, theirs, refs = refs[:parts], refs[parts : 2 * parts], refs[2 * parts :]
    bases, pieces, (mine, sent, buffer) = refs[:2], refs[2:-3], refs[-3:]
    b = lax.rem(lax.axis_index("chol"), 2)
    for walker in range(mine.shape[0]):
        for piece, (sibling, dz, dy) in zip(pieces, places):
            block = 1 - b if sibling else b
            buffer[walker, gathered(layout, dz, dy), block] = piece[walker]
        rows = jnp.concatenate([part[walker] for part in (*kept, *theirs)], axis=0)
        columns = buffer[walker].reshape(-1, buffer.shape[-1])
        term = jnp.dot(rows, columns, preferred_element_type=F32)
        count = term.shape[0] // 2
        mine[walker] = (bases[0][walker] + 0.5 * term[:count]).astype(BF16)
        sent[walker] = (bases[1][walker] + 0.5 * term[count:]).astype(BF16)


def second_of(layout, kept, theirs, bases, streams):
    arrays, places = [], []
    for sibling, stream in enumerate(streams):
        for array, dz, dy in stream.pieces():
            arrays.append(array)
            places.append((sibling, dz, dy))
    orbitals = kept[0].shape[2]
    half, rows, electrons = arrays[0].shape
    out = jax.ShapeDtypeStruct((half, rows, electrons), BF16)
    return pl.pallas_call(
        functools.partial(second_kernel, layout, places, len(kept)),
        out_shape=[out, out],
        in_specs=vmem_specs(2 * len(kept) + 2 + len(arrays)),
        out_specs=vmem_specs(2),
        scratch_shapes=[pltpu.VMEM((half, layout.chol // 2, 2, rows, electrons), BF16)],
        compiler_params=params(16),
        cost_estimate=pl.CostEstimate(
            flops=4 * half * rows * orbitals * electrons,
            bytes_accessed=2 * half * orbitals * (2 * rows + electrons),
            transcendentals=0,
        ),
    )(*kept, *theirs, *bases, *arrays)


def place_kernel(order, mine, theirs, out):
    half = mine.shape[0]
    b = lax.rem(lax.axis_index("chol"), 2)
    for walker in range(half):
        out[order[b * half + walker]] = mine[walker]
        out[order[(1 - b) * half + walker]] = theirs[walker]


def place(order, mine, theirs):
    half, rows, electrons = mine.shape
    return pl.pallas_call(
        place_kernel,
        out_shape=jax.ShapeDtypeStruct((2 * half, rows, electrons), BF16),
        in_specs=[pl.BlockSpec(memory_space=pltpu.SMEM)] + vmem_specs(2),
        out_specs=pl.BlockSpec(memory_space=pltpu.VMEM),
        compiler_params=params(8),
    )(order, mine, theirs)


def split_kernel(source, walkers, first, second, order, picked, semaphores):
    per_group = walkers.shape[0]
    half = per_group // 2
    group = lax.axis_index("walk")
    b = lax.rem(lax.axis_index("chol"), 2)
    stayed, arrived, sent = jnp.int32(0), jnp.int32(0), jnp.int32(0)
    for slot in range(per_group):
        local = source[group * per_group + slot] - group * per_group
        stays = ((local >= 0) & (local < per_group)).astype(jnp.int32)
        at = jnp.where(stays == 1, jnp.minimum(stayed, half - 1), per_group)
        picked[at] = local
        at = jnp.where(stays == 1, stayed, half + arrived)
        order[jnp.minimum(at, per_group - 1)] = jnp.int32(slot)
        stayed, arrived = stayed + stays, arrived + 1 - stays
        local = source[(1 - group) * per_group + slot] - group * per_group
        goes = ((local >= 0) & (local < per_group)).astype(jnp.int32)
        at = jnp.where(goes == 1, half + jnp.minimum(sent, half - 1), per_group)
        picked[at] = local
        sent = sent + goes
    copies = []
    for target, offset in ((second, (1 - b) * half), (first, b * half)):
        for walker in range(half):
            copies.append(
                pltpu.make_async_copy(
                    walkers.at[picked[offset + walker]],
                    target.at[walker],
                    semaphores.at[len(copies)],
                )
            )
    for copy in copies:
        copy.start()
    for copy in copies:
        copy.wait()


def split_walkers(walkers, source):
    per_group, rows, electrons = walkers.shape
    half = jax.ShapeDtypeStruct((per_group // 2, rows, electrons), walkers.dtype)
    return pl.pallas_call(
        split_kernel,
        out_shape=[half, half, jax.ShapeDtypeStruct((per_group,), jnp.int32)],
        in_specs=[pl.BlockSpec(memory_space=pltpu.SMEM), pl.BlockSpec(memory_space=pltpu.HBM)],
        out_specs=[pl.BlockSpec(memory_space=pl.ANY)] * 2
        + [pl.BlockSpec(memory_space=pltpu.SMEM)],
        scratch_shapes=[
            pltpu.SMEM((per_group + 1,), jnp.int32),
            pltpu.SemaphoreType.DMA((per_group,)),
        ],
        compiler_params=params(4),
    )(source, walkers)


def ranks(flags):
    count = flags.shape[-1]
    before = jnp.arange(count)[None, :] < jnp.arange(count)[:, None]
    return jnp.sum(jnp.where(before & flags[..., None, :], 1, 0), axis=-1)


def migrate(layout, walkers, source, trial):
    per_group = walkers.shape[0]
    half = per_group // 2
    group = lax.axis_index("walk")
    if layout.walk == 2:
        first, second, order = split_walkers(walkers, source)
        first, second, trial = lax.optimization_barrier((first, second, trial))
        near, cross = [], []
        for index in range(2 * layout.chol):
            across = (index + layout.chol) % (2 * layout.chol)
            if index % 2 == 0:
                near.append((index, index))
                cross.append((index, across + 1))
            else:
                near.append((index, across))
                cross.append((index, index - 1))
        axes = ("walk", "chol")
        return lax.ppermute(first, axes, near), lax.ppermute(second, axes, cross), order, trial
    table = source.reshape(layout.walk, per_group)
    incoming = lax.dynamic_index_in_dim(table, group, 0, keepdims=False)
    incoming_groups = incoming // per_group

    def outgoing(distance):
        row = lax.dynamic_index_in_dim(table, (group + distance) % layout.walk, 0, keepdims=False)
        local = row - group * per_group
        here = (local >= 0) & (local < per_group)
        match = here[None, :] & (ranks(here)[None, :] == jnp.arange(half)[:, None])
        return jnp.take(walkers, jnp.sum(jnp.where(match, local[None, :], 0), axis=1), axis=0)

    arrived = [outgoing(0)]
    for distance in range(1, layout.walk):
        pairs = [(g, (g + distance) % layout.walk) for g in range(layout.walk)]
        arrived.append(lax.ppermute(outgoing(distance), "walk", pairs))
    slots = jnp.arange(per_group)
    same = (incoming_groups[:, None] == incoming_groups[None, :]) & (slots[None, :] < slots[:, None])
    rank = jnp.sum(same.astype(jnp.int32), axis=1)
    distance = (group - incoming_groups) % layout.walk
    migrated = jnp.take(jnp.concatenate(arrived, axis=0), distance * half + rank, axis=0)
    b = lax.axis_index("chol") % 2
    mine = lax.dynamic_slice_in_dim(migrated, b * half, half, 0)
    theirs = lax.dynamic_slice_in_dim(migrated, (1 - b) * half, half, 0)
    return mine, layout.shift(theirs, db=1), slots.astype(jnp.int32), trial


def shards(layout, walkers, trial, cholesky, rotated, fields, source):
    half = walkers.shape[0] // 2
    sizes = (half // 2, half - half // 2)
    b = lax.axis_index("chol") % 2

    own, other, order, trial = migrate(layout, walkers, source, trial)
    pairs = [jnp.stack([trial, layout.shift(trial, dy=1)])]
    pairs.append(layout.shift(pairs[0], dz=1))
    own, other, pairs = lax.optimization_barrier((own, other, pairs))
    while len(pairs) < layout.z:
        pairs.append(layout.shift(pairs[-1], dz=1))
    chunk = jnp.stack([jnp.where(b == 0, own, other), jnp.where(b == 0, other, own)], axis=1)
    chunks = [chunk[: sizes[0]], chunk[sizes[0] :]]
    streams = [Stream(layout, chunk) for chunk in chunks]
    for stage in range(layout.z):
        if stage == 0:
            pairs[:3] = streams[0].advance(pairs[:3])
            pairs[3:] = streams[1].advance(pairs[3:])
            planes = jnp.stack(pairs)
            planes_theirs = layout.shift(planes, db=1)
            rot_theirs = layout.shift(rotated, db=1)
        elif stage == 1:
            streams[0].advance()
            planes_theirs, rot_theirs = streams[1].advance((planes_theirs, rot_theirs))
            turned = transposed(layout, planes, planes_theirs)
        elif stage == 2:
            (turned,) = streams[0].advance((turned,))
            streams[1].advance()
        else:
            for stream in streams:
                stream.advance()

    fulls, inverses = zip(*[inverses_of(layout, turned, stream) for stream in streams])
    total = bias_of(chunks, inverses, rotated, rot_theirs)
    parts = [total] + [layout.shift(total, dz=dz) for dz in range(1, layout.z)]
    while len(parts) > 1:
        far = len(parts) // 2
        parts = [parts[at] + parts[at + far] for at in range(far)]
    parts = [parts[0]] + [layout.shift(parts[0], dy=dy, db=db) for dy, db in ((1, 0), (0, 1), (1, 1))]
    force_bias, weights = weights_of(order, fields, parts)
    kept, received = [], []
    for part in range(2):
        mine, sent = potential_of(weights, cholesky, part, 2)
        kept.append(mine)
        received.append(layout.shift(sent, db=1))

    rounded, base = first_of(kept, fulls, 0)
    rounded_theirs, base_theirs = first_of(received, fulls, 1)
    streams = [Stream(layout, rounded), Stream(layout, rounded_theirs)]
    for _ in range(layout.z):
        for stream in streams:
            stream.advance()
    mine, sent = second_of(layout, kept, received, (base, base_theirs), streams)
    return place(order, mine, layout.shift(sent, db=1)), force_bias


def solution(mesh):
    in_specs = (
        P("walk", "chol", None),
        P("chol", None),
        P(None, "chol", None),
        P(None, "chol", None),
        P("walk", None),
        P(),
    )
    out_specs = (P("walk", "chol", None), P("walk", None))
    layout = Layout(mesh.shape["walk"], mesh.shape["chol"])
    return jax.shard_map(
        functools.partial(shards, layout),
        mesh=mesh,
        in_specs=in_specs,
        out_specs=out_specs,
        check_vma=False,
    )
```

```python
import functools

import jax
import jax.numpy as jnp
from jax import lax
from jax.experimental import pallas as pl
from jax.experimental.pallas import tpu as pltpu
from jax.sharding import PartitionSpec as P

ITERS = 3
TAU_ROOT = 0.1
BLOCK = 16
HIGHEST = lax.Precision.HIGHEST
MIB = 1024 * 1024

F32 = jnp.float32
BF16 = jnp.bfloat16


def params(mebibytes):
    return pltpu.CompilerParams(vmem_limit_bytes=mebibytes * MIB)


def vmem_specs(count):
    return [pl.BlockSpec(memory_space=pltpu.VMEM)] * count


class Layout:
    def __init__(self, walk_size, chol_size):
        self.walk = walk_size
        self.chol = chol_size
        self.z = chol_size // 4

    def shift(self, array, dz=0, dy=0, db=0):
        pairs = []
        for index in range(self.chol):
            z, y, b = index // 4, (index // 2) % 2, index % 2
            target = (((z + dz) % self.z) * 2 + (y ^ dy)) * 2 + (b ^ db)
            pairs.append((index, target))
        return lax.ppermute(array, "chol", pairs)


class Stream:
    def __init__(self, layout, piece, last_along_z=False):
        self.layout = layout
        self.ring = [piece]
        self.across = []
        self.last_along_z = last_along_z

    def advance(self, anchors=()):
        latest = self.ring[-1]
        last = len(self.ring) == self.layout.z
        if last and self.last_along_z:
            moved = [self.layout.shift(self.across[-1], dz=1)]
        else:
            moved = [self.layout.shift(latest, dy=1)]
        if not last:
            moved.append(self.layout.shift(latest, dz=1))
        if anchors or not last:
            anchors, moved = lax.optimization_barrier((anchors, moved))
        self.across.append(moved[0])
        self.ring.extend(moved[1:])
        return anchors

    def pieces(self):
        ring = [(array, dz, 0) for dz, array in enumerate(self.ring)]
        return ring + [(array, dz, 1) for dz, array in enumerate(self.across)]


class CrossFirst:
    def __init__(self, layout, piece):
        self.layout = layout
        self.piece = piece
        self.ring = []

    def advance(self, anchors=()):
        if self.ring:
            moved = self.layout.shift(self.ring[-1], dz=1)
        else:
            moved = self.layout.shift(self.piece, dy=1)
        anchors, moved = lax.optimization_barrier((anchors, moved))
        self.ring.append(moved if self.ring else jnp.stack([self.piece, moved]))
        return anchors


def gathered(layout, dz, dy):
    index = lax.axis_index("chol")
    z, y = index // 4, lax.rem(index // 2, 2)
    return lax.rem(z + (layout.z - dz), layout.z) * 2 + (y + dy - 2 * y * dy)


def transpose_kernel(layout, mine, theirs, out, buffer):
    b = lax.rem(lax.axis_index("chol"), 2)
    for dz in range(layout.z):
        for dy in range(2):
            chip = gathered(layout, dz, dy)
            buffer[chip, b] = mine[dz, dy]
            buffer[chip, 1 - b] = theirs[dz, dy]
    out[...] = buffer[...].reshape(-1, buffer.shape[-1]).T


def transposed(layout, mine, theirs):
    _, _, rows, electrons = mine.shape
    chips = layout.chol // 2
    return pl.pallas_call(
        functools.partial(transpose_kernel, layout),
        out_shape=jax.ShapeDtypeStruct((electrons, layout.chol * rows), BF16),
        in_specs=vmem_specs(2),
        out_specs=pl.BlockSpec(memory_space=pltpu.VMEM),
        scratch_shapes=[pltpu.VMEM((chips, 2, rows, electrons), BF16)],
        compiler_params=params(8),
    )(mine, theirs)


def product(left, right):
    high, right_high = left.astype(BF16), right.astype(BF16)
    low = (left - high.astype(F32)).astype(BF16)
    right_low = (right - right_high.astype(F32)).astype(BF16)
    return jnp.dot(
        jnp.concatenate([high, high, low], axis=1),
        jnp.concatenate([right_high, right_low, right_high], axis=0),
        preferred_element_type=F32,
    )


def newton_inverses(matrices):
    shape = matrices[0].shape
    same = lax.broadcasted_iota(jnp.int32, shape, 0) == lax.broadcasted_iota(jnp.int32, shape, 1)
    twice = jnp.where(same, 2.0, 0.0).astype(F32)
    estimates = [twice - matrix for matrix in matrices]
    for _ in range(ITERS - 1):
        steps = [twice - product(a, x) for a, x in zip(matrices, estimates)]
        estimates = [product(x, step) for x, step in zip(estimates, steps)]
    return estimates


def inverse_kernel(layout, places, trial, *refs):
    pieces, (full, out) = refs[:-2], refs[-2:]
    matrices = []
    for walker in range(out.shape[0]):
        for piece, (dz, dy) in zip(pieces, places):
            full[walker, gathered(layout, dz, dy)] = piece[:, walker]
        rows = full[walker].reshape(-1, full.shape[-1])
        matrices.append(jnp.dot(trial[...], rows, preferred_element_type=F32))
    for walker, inverse in enumerate(newton_inverses(matrices)):
        out[walker] = inverse.astype(out.dtype)


def inverses_of(layout, trial, stream):
    arrays = [array for array, *_ in stream.pieces()]
    places = [place for _, *place in stream.pieces()]
    _, count, rows, electrons = arrays[0].shape
    return pl.pallas_call(
        functools.partial(inverse_kernel, layout, places),
        out_shape=[
            jax.ShapeDtypeStruct((count, layout.chol // 2, 2, rows, electrons), BF16),
            jax.ShapeDtypeStruct((count, electrons, electrons), BF16),
        ],
        in_specs=vmem_specs(1 + len(arrays)),
        out_specs=vmem_specs(2),
        compiler_params=params(8),
        cost_estimate=pl.CostEstimate(
            flops=2 * count * electrons**2 * (trial.shape[1] + 6 * (ITERS - 1) * electrons),
            bytes_accessed=4 * (count + 1) * trial.shape[1] * electrons,
            transcendentals=0,
        ),
    )(trial, *arrays)


def bias_kernel(sizes, rot_mine, rot_theirs, *refs):
    streams = len(sizes)
    chunks, inverses, (out, greens) = refs[:streams], refs[streams : 2 * streams], refs[-2:]
    vectors, rows, electrons = rot_mine.shape
    b = lax.rem(lax.axis_index("chol"), 2)
    count = 0
    for chunk, inverse, size in zip(chunks, inverses, sizes):
        for walker in range(size):
            both = chunk[:, walker].reshape(2 * rows, electrons)
            product = jnp.dot(both, inverse[walker], preferred_element_type=F32).astype(BF16)
            greens[:, :, count] = product.reshape(2, rows // BLOCK, BLOCK, electrons)
            count += 1
    total = jnp.zeros((vectors * BLOCK, count * BLOCK), F32)
    for half, rot in ((b, rot_mine), (1 - b, rot_theirs)):
        for block in range(rows // BLOCK):
            total += lax.dot_general(
                rot[:, block * BLOCK : (block + 1) * BLOCK, :].reshape(vectors * BLOCK, electrons),
                greens[half, block].reshape(count * BLOCK, electrons),
                (((1,), (1,)), ((), ())),
                preferred_element_type=F32,
            )
    same = lax.rem(lax.broadcasted_iota(jnp.int32, total.shape, 0), BLOCK) == lax.rem(
        lax.broadcasted_iota(jnp.int32, total.shape, 1), BLOCK
    )
    summed = jnp.sum(
        jnp.where(same, total, 0.0).reshape(vectors, BLOCK, count * BLOCK), axis=1
    )
    shape = (count, count * BLOCK)
    pick = (
        lax.broadcasted_iota(jnp.int32, shape, 1) // BLOCK
        == lax.broadcasted_iota(jnp.int32, shape, 0)
    ).astype(F32)
    out[...] = lax.dot_general(
        pick, summed, (((1,), (1,)), ((), ())), precision=HIGHEST, preferred_element_type=F32
    )


def bias_of(chunks, inverses, rot_mine, rot_theirs):
    vectors, rows, electrons = rot_mine.shape
    sizes = [chunk.shape[1] for chunk in chunks]
    count = sum(sizes)
    return pl.pallas_call(
        functools.partial(bias_kernel, sizes),
        out_shape=jax.ShapeDtypeStruct((count, vectors), F32),
        in_specs=vmem_specs(2 + 2 * len(sizes)),
        out_specs=pl.BlockSpec(memory_space=pltpu.VMEM),
        scratch_shapes=[pltpu.VMEM((2, rows // BLOCK, count, BLOCK, electrons), BF16)],
        compiler_params=params(12),
        cost_estimate=pl.CostEstimate(
            flops=4 * count * rows * electrons * (electrons + vectors * BLOCK),
            bytes_accessed=4 * (vectors + count) * rows * electrons,
            transcendentals=0,
        ),
    )(rot_mine, rot_theirs, *chunks, *inverses)


def weights_kernel(order, fields, mine, mine_across, theirs, theirs_across, bias_out, weights):
    per_group, vectors = fields.shape
    half = mine.shape[0]
    sums = (mine[...] + mine_across[...], theirs[...] + theirs_across[...])
    b = lax.rem(lax.axis_index("chol"), 2)
    row = lax.broadcasted_iota(jnp.int32, (per_group, vectors), 0)
    bias = jnp.zeros((per_group, vectors), F32)
    for walker in range(half):
        for part, core in zip(sums, (b, 1 - b)):
            slot = order[core * half + walker]
            bias += jnp.where(row == slot, part[walker : walker + 1, :], 0.0)
    bias = TAU_ROOT * bias
    bias_out[...] = bias
    shifted = (fields[...] - bias).astype(BF16)
    slot = jnp.zeros((per_group * BLOCK, 1), jnp.int32)
    place = lax.broadcasted_iota(jnp.int32, slot.shape, 0) // BLOCK
    for at in range(per_group):
        slot = jnp.where(place == at, order[lax.rem(at + b * half, per_group)], slot)
    tall = (per_group * BLOCK, per_group)
    rows = (lax.broadcasted_iota(jnp.int32, tall, 1) == slot).astype(BF16)
    wide = (vectors, vectors * BLOCK)
    columns = (
        lax.broadcasted_iota(jnp.int32, wide, 1) // BLOCK
        == lax.broadcasted_iota(jnp.int32, wide, 0)
    ).astype(BF16)
    spread = jnp.dot(rows, shifted, preferred_element_type=F32).astype(BF16)
    spread = jnp.dot(spread, columns, preferred_element_type=F32)
    same = lax.rem(lax.broadcasted_iota(jnp.int32, spread.shape, 0), BLOCK) == lax.rem(
        lax.broadcasted_iota(jnp.int32, spread.shape, 1), BLOCK
    )
    weights[...] = jnp.where(same, spread, 0.0).astype(BF16)


def weights_of(order, fields, parts):
    per_group, vectors = fields.shape
    return pl.pallas_call(
        weights_kernel,
        out_shape=[
            jax.ShapeDtypeStruct((per_group, vectors), F32),
            jax.ShapeDtypeStruct((per_group * BLOCK, vectors * BLOCK), BF16),
        ],
        in_specs=[pl.BlockSpec(memory_space=pltpu.SMEM)] + vmem_specs(5),
        out_specs=vmem_specs(2),
        compiler_params=params(8),
    )(order, fields, *parts)


def potential_kernel(weights, cholesky, kept, *sent):
    half, part = kept.shape[0], sent[0].shape[1]
    vectors, rows, orbitals = cholesky.shape
    for at in range(0, rows, BLOCK):
        columns = cholesky[:, at : at + BLOCK, :].reshape(vectors * BLOCK, orbitals)
        result = TAU_ROOT * jnp.dot(weights[...], columns, preferred_element_type=F32)
        result = result.astype(BF16).reshape(2 * half, BLOCK, orbitals)
        kept[:, at : at + BLOCK, :] = result[:half]
        start = at % part
        sent[at // part][:, start : start + BLOCK, :] = result[half:]


def potential_of(weights, cholesky):
    vectors, rows, orbitals = cholesky.shape
    half = weights.shape[0] // BLOCK // 2
    kept = jax.ShapeDtypeStruct((half, rows, orbitals), BF16)
    sent = jax.ShapeDtypeStruct((half, rows // 2, orbitals), BF16)
    return pl.pallas_call(
        potential_kernel,
        out_shape=[kept, sent, sent],
        in_specs=vmem_specs(2),
        out_specs=vmem_specs(3),
        compiler_params=params(12),
    )(weights, cholesky)


def first_kernel(sibling, parts, *refs):
    potential, fulls, (rounded, base) = refs[:parts], refs[parts:-2], refs[-2:]
    b = lax.rem(lax.axis_index("chol"), 2)
    chip = lax.axis_index("chol") // 2
    count = 0
    for full in fulls:
        for walker in range(full.shape[0]):
            rows = jnp.concatenate([part[count] for part in potential], axis=0)
            columns = full[walker].reshape(-1, full.shape[-1])
            term = jnp.dot(rows, columns, preferred_element_type=F32)
            rounded[count] = term.astype(BF16)
            own = full[walker, chip, 1 - b if sibling else b]
            base[count] = own.astype(F32) + term
            count += 1


def first_of(potential, fulls, sibling):
    half, _, orbitals = potential[0].shape
    rows, electrons = fulls[0].shape[-2:]
    shape = (half, rows, electrons)
    return pl.pallas_call(
        functools.partial(first_kernel, sibling, len(potential)),
        out_shape=[jax.ShapeDtypeStruct(shape, BF16), jax.ShapeDtypeStruct(shape, F32)],
        in_specs=vmem_specs(len(potential) + len(fulls)),
        out_specs=vmem_specs(2),
        compiler_params=params(8),
        cost_estimate=pl.CostEstimate(
            flops=2 * half * rows * orbitals * electrons,
            bytes_accessed=2 * half * orbitals * (rows + electrons),
            transcendentals=0,
        ),
    )(*potential, *fulls)


def second_kernel(layout, places, parts, *refs):
    potential, refs = refs[:parts], refs[parts:]
    bases, pieces, (mine, sent, buffer) = refs[:2], refs[2:-3], refs[-3:]
    b = lax.rem(lax.axis_index("chol"), 2)
    for walker in range(mine.shape[0]):
        for piece, (sibling, dz, dy) in zip(pieces, places):
            block = 1 - b if sibling else b
            buffer[walker, gathered(layout, dz, dy), block] = piece[walker]
        rows = jnp.concatenate([part[walker] for part in potential], axis=0)
        columns = buffer[walker].reshape(-1, buffer.shape[-1])
        term = jnp.dot(rows, columns, preferred_element_type=F32)
        count = term.shape[0] // 2
        mine[walker] = (bases[0][walker] + 0.5 * term[:count]).astype(BF16)
        sent[walker] = (bases[1][walker] + 0.5 * term[count:]).astype(BF16)


def second_of(layout, potential, bases, streams):
    arrays, places = [], []
    for sibling, stream in enumerate(streams):
        for array, dz, dy in stream.pieces():
            arrays.append(array)
            places.append((sibling, dz, dy))
    half, rows, orbitals = potential[0].shape
    electrons = arrays[0].shape[-1]
    out = jax.ShapeDtypeStruct((half, rows, electrons), BF16)
    return pl.pallas_call(
        functools.partial(second_kernel, layout, places, len(potential)),
        out_shape=[out, out],
        in_specs=vmem_specs(len(potential) + 2 + len(arrays)),
        out_specs=vmem_specs(2),
        scratch_shapes=[pltpu.VMEM((half, layout.chol // 2, 2, rows, electrons), BF16)],
        compiler_params=params(16),
        cost_estimate=pl.CostEstimate(
            flops=4 * half * rows * orbitals * electrons,
            bytes_accessed=2 * half * orbitals * (2 * rows + electrons),
            transcendentals=0,
        ),
    )(*potential, *bases, *arrays)


def place_kernel(order, mine, theirs, out):
    half = mine.shape[0]
    b = lax.rem(lax.axis_index("chol"), 2)
    for walker in range(half):
        out[order[b * half + walker]] = mine[walker]
        out[order[(1 - b) * half + walker]] = theirs[walker]


def place(order, mine, theirs):
    half, rows, electrons = mine.shape
    return pl.pallas_call(
        place_kernel,
        out_shape=jax.ShapeDtypeStruct((2 * half, rows, electrons), BF16),
        in_specs=[pl.BlockSpec(memory_space=pltpu.SMEM)] + vmem_specs(2),
        out_specs=pl.BlockSpec(memory_space=pltpu.VMEM),
        compiler_params=params(8),
    )(order, mine, theirs)


def split_kernel(source, walkers, *refs):
    targets, (order, picked, semaphores) = refs[:4], refs[4:]
    per_group = walkers.shape[0]
    half = per_group // 2
    share = half // 2
    group = lax.axis_index("walk")
    b = lax.rem(lax.axis_index("chol"), 2)
    stayed, arrived, sent = jnp.int32(0), jnp.int32(0), jnp.int32(0)
    for slot in range(per_group):
        local = source[group * per_group + slot] - group * per_group
        stays = ((local >= 0) & (local < per_group)).astype(jnp.int32)
        picked[jnp.where(stays == 1, jnp.minimum(stayed, half - 1), per_group)] = local
        rank = jnp.minimum(jnp.where(stays == 1, stayed, arrived), half - 1)
        core = rank // share
        order[core * half + (1 - stays) * share + rank - core * share] = jnp.int32(slot)
        stayed, arrived = stayed + stays, arrived + 1 - stays
        local = source[(1 - group) * per_group + slot] - group * per_group
        goes = ((local >= 0) & (local < per_group)).astype(jnp.int32)
        picked[jnp.where(goes == 1, half + jnp.minimum(sent, half - 1), per_group)] = local
        sent = sent + goes
    offsets = (b * share, (1 - b) * share, half + b * share, half + (1 - b) * share)
    copies = []
    for target, offset in reversed(list(zip(targets, offsets))):
        for walker in range(share):
            copies.append(
                pltpu.make_async_copy(
                    walkers.at[picked[offset + walker]],
                    target.at[walker],
                    semaphores.at[len(copies)],
                )
            )
    for copy in copies:
        copy.start()
    for copy in copies:
        copy.wait()


def split_walkers(walkers, source):
    per_group, rows, electrons = walkers.shape
    share = jax.ShapeDtypeStruct((per_group // 4, rows, electrons), walkers.dtype)
    return pl.pallas_call(
        split_kernel,
        out_shape=[share] * 4 + [jax.ShapeDtypeStruct((per_group,), jnp.int32)],
        in_specs=[pl.BlockSpec(memory_space=pltpu.SMEM), pl.BlockSpec(memory_space=pl.ANY)],
        out_specs=[pl.BlockSpec(memory_space=pl.ANY)] * 4
        + [pl.BlockSpec(memory_space=pltpu.SMEM)],
        scratch_shapes=[
            pltpu.SMEM((per_group + 1,), jnp.int32),
            pltpu.SemaphoreType.DMA((per_group,)),
        ],
        compiler_params=params(4),
    )(source, walkers)


def ranks(flags):
    count = flags.shape[-1]
    before = jnp.arange(count)[None, :] < jnp.arange(count)[:, None]
    return jnp.sum(jnp.where(before & flags[..., None, :], 1, 0), axis=-1)


def migrate(layout, walkers, source):
    per_group = walkers.shape[0]
    half = per_group // 2
    group = lax.axis_index("walk")
    if layout.walk == 2 and half % 2 == 0:
        stay, stay_sent, near, cross, order = split_walkers(walkers, source)
        count = 2 * layout.chol
        across = [(index + layout.chol) % count for index in range(count)]
        axes = ("walk", "chol")
        near = lax.ppermute(near, axes, list(enumerate(across)))
        cross = lax.ppermute(cross, axes, [(i, j ^ 1) for i, j in enumerate(across)])
        return [(stay, layout.shift(stay_sent, db=1)), (near, cross)], order
    table = source.reshape(layout.walk, per_group)
    incoming = lax.dynamic_index_in_dim(table, group, 0, keepdims=False)
    incoming_groups = incoming // per_group

    def outgoing(distance):
        row = lax.dynamic_index_in_dim(table, (group + distance) % layout.walk, 0, keepdims=False)
        local = row - group * per_group
        here = (local >= 0) & (local < per_group)
        match = here[None, :] & (ranks(here)[None, :] == jnp.arange(half)[:, None])
        return jnp.take(walkers, jnp.sum(jnp.where(match, local[None, :], 0), axis=1), axis=0)

    arrived = [outgoing(0)]
    for distance in range(1, layout.walk):
        pairs = [(g, (g + distance) % layout.walk) for g in range(layout.walk)]
        arrived.append(lax.ppermute(outgoing(distance), "walk", pairs))
    slots = jnp.arange(per_group)
    same = (incoming_groups[:, None] == incoming_groups[None, :]) & (slots[None, :] < slots[:, None])
    rank = jnp.sum(same.astype(jnp.int32), axis=1)
    distance = (group - incoming_groups) % layout.walk
    migrated = jnp.take(jnp.concatenate(arrived, axis=0), distance * half + rank, axis=0)
    b = lax.axis_index("chol") % 2
    mine = lax.dynamic_slice_in_dim(migrated, b * half, half, 0)
    theirs = lax.dynamic_slice_in_dim(migrated, (1 - b) * half, half, 0)
    theirs = layout.shift(theirs, db=1)
    share = half // 2
    shares = [(mine[:share], theirs[:share]), (mine[share:], theirs[share:])]
    return shares, slots.astype(jnp.int32)


def shards(layout, walkers, trial, cholesky, rotated, fields, source):
    half = walkers.shape[0] // 2
    b = lax.axis_index("chol") % 2
    shares, order = migrate(layout, walkers, source)
    chunks = [
        jnp.stack([jnp.where(b == 0, own, other), jnp.where(b == 0, other, own)])
        for own, other in shares
    ]
    streams = [Stream(layout, chunk) for chunk in chunks]
    pairs = CrossFirst(layout, trial)
    rot_theirs = layout.shift(rotated, db=1)
    for stage in range(layout.z):
        last = stage == layout.z - 1
        if stage < 2:
            pairs.advance()
            streams[0].advance(pairs.ring[-1:])
            if stage == 1:
                while len(pairs.ring) < layout.z:
                    pairs.advance()
            else:
                pairs.advance()
            streams[1].advance(pairs.ring[-1:])
            if stage == 1:
                planes = jnp.stack(pairs.ring)
                planes_theirs = layout.shift(planes, db=1)
        elif stage == 2:
            planes_theirs, rot_theirs = streams[0].advance((planes_theirs, rot_theirs))
            turned = transposed(layout, planes, planes_theirs)
            (turned,) = streams[1].advance((turned,))
        else:
            for stream in streams:
                stream.advance()
    fulls, inverses = zip(*[inverses_of(layout, turned, stream) for stream in streams])
    total = bias_of(chunks, inverses, rotated, rot_theirs)
    parts = [total] + [layout.shift(total, dz=dz) for dz in range(1, layout.z)]
    while len(parts) > 1:
        far = len(parts) // 2
        parts = [parts[at] + parts[at + far] for at in range(far)]
    parts = [parts[0]] + [layout.shift(parts[0], dy=dy, db=db) for dy, db in ((1, 0), (0, 1), (1, 1))]
    force_bias, weights = weights_of(order, fields, parts)
    kept, *sent = potential_of(weights, cholesky)
    received = [layout.shift(part, db=1) for part in sent]

    rounded, base = first_of([kept], fulls, 0)
    rounded_theirs, base_theirs = first_of(received, fulls, 1)
    streams = [Stream(layout, rounded), Stream(layout, rounded_theirs, last_along_z=True)]
    for _ in range(layout.z):
        for stream in streams:
            stream.advance()
    mine, sent = second_of(layout, (kept, *received), (base, base_theirs), streams)
    return place(order, mine, layout.shift(sent, db=1)), force_bias


def solution(mesh):
    in_specs = (
        P("walk", "chol", None),
        P("chol", None),
        P(None, "chol", None),
        P(None, "chol", None),
        P("walk", None),
        P(),
    )
    out_specs = (P("walk", "chol", None), P("walk", None))
    layout = Layout(mesh.shape["walk"], mesh.shape["chol"])
    return jax.shard_map(
        functools.partial(shards, layout),
        mesh=mesh,
        in_specs=in_specs,
        out_specs=out_specs,
        check_vma=False,
    )
```

```python
import functools

import jax
import jax.numpy as jnp
from jax import lax
from jax.experimental import pallas as pl
from jax.experimental.pallas import tpu as pltpu
from jax.sharding import PartitionSpec as P

ITERS = 3
TAU_ROOT = 0.1
BLOCK = 16
HIGHEST = lax.Precision.HIGHEST
MIB = 1024 * 1024

F32 = jnp.float32
BF16 = jnp.bfloat16


def params(mebibytes):
    return pltpu.CompilerParams(vmem_limit_bytes=mebibytes * MIB)


def vmem_specs(count):
    return [pl.BlockSpec(memory_space=pltpu.VMEM)] * count


class Layout:
    def __init__(self, walk_size, chol_size):
        self.walk = walk_size
        self.chol = chol_size
        self.z = chol_size // 4

    def shift(self, array, dz=0, dy=0, db=0):
        pairs = []
        for index in range(self.chol):
            z, y, b = index // 4, (index // 2) % 2, index % 2
            target = (((z + dz) % self.z) * 2 + (y ^ dy)) * 2 + (b ^ db)
            pairs.append((index, target))
        return lax.ppermute(array, "chol", pairs)

    def step(self, array):
        ring = [*range(0, self.z, 2), *reversed(range(1, self.z, 2))]
        target = {z: ring[(at + 1) % self.z] for at, z in enumerate(ring)}
        pairs = [(index, target[index // 4] * 4 + index % 4) for index in range(self.chol)]
        return lax.ppermute(array, "chol", pairs)

    def origin(self, steps, dy):
        index = lax.axis_index("chol")
        z, y = index // 4, lax.rem(index // 2, 2)
        at = jnp.where(lax.rem(z, 2) == 0, z // 2, self.z - (z + 1) // 2)
        at = lax.rem(at + (self.z - steps), self.z)
        z = jnp.where(2 * at < self.z, 2 * at, 2 * (self.z - at) - 1)
        return z * 2 + (y + dy - 2 * y * dy)


class Stream:
    def __init__(self, layout, piece, last_along_z=False):
        self.layout = layout
        self.ring = [piece]
        self.across = []
        self.last_along_z = last_along_z

    def advance(self, anchors=()):
        latest = self.ring[-1]
        last = len(self.ring) == self.layout.z
        if last and self.last_along_z:
            moved = [self.layout.step(self.across[-1])]
        else:
            moved = [self.layout.shift(latest, dy=1)]
        if not last:
            moved.append(self.layout.step(latest))
        if anchors or not last:
            anchors, moved = lax.optimization_barrier((anchors, moved))
        self.across.append(moved[0])
        self.ring.extend(moved[1:])
        return anchors

    def pieces(self):
        ring = [(array, steps, 0) for steps, array in enumerate(self.ring)]
        return ring + [(array, steps, 1) for steps, array in enumerate(self.across)]


def transpose_kernel(layout, places, *refs):
    arrays, theirs, (out, buffer) = refs[: len(places)], refs[len(places) : -2], refs[-2:]
    b = lax.rem(lax.axis_index("chol"), 2)
    slabs = [(part, at) for part in theirs for at in range(part.shape[0])]
    for array, (steps, dy), (part, at) in zip(arrays, places, slabs):
        chip = layout.origin(steps, dy)
        buffer[chip, b] = array[array.shape[0] - 1]
        buffer[chip, 1 - b] = part[at]
    out[...] = buffer[...].reshape(-1, buffer.shape[-1]).T


def transposed(layout, stream, theirs):
    arrays = [array for array, *_ in stream.pieces()]
    places = [place for _, *place in stream.pieces()]
    _, rows, electrons = arrays[0].shape
    return pl.pallas_call(
        functools.partial(transpose_kernel, layout, places),
        out_shape=jax.ShapeDtypeStruct((electrons, layout.chol * rows), BF16),
        in_specs=vmem_specs(len(arrays) + len(theirs)),
        out_specs=pl.BlockSpec(memory_space=pltpu.VMEM),
        scratch_shapes=[pltpu.VMEM((layout.chol // 2, 2, rows, electrons), BF16)],
        compiler_params=params(8),
    )(*arrays, *theirs)


def product(left, right):
    high, right_high = left.astype(BF16), right.astype(BF16)
    low = (left - high.astype(F32)).astype(BF16)
    right_low = (right - right_high.astype(F32)).astype(BF16)
    return jnp.dot(
        jnp.concatenate([high, high, low], axis=1),
        jnp.concatenate([right_high, right_low, right_high], axis=0),
        preferred_element_type=F32,
    )


def newton_inverses(matrices):
    shape = matrices[0].shape
    same = lax.broadcasted_iota(jnp.int32, shape, 0) == lax.broadcasted_iota(jnp.int32, shape, 1)
    twice = jnp.where(same, 2.0, 0.0).astype(F32)
    estimates = [twice - matrix for matrix in matrices]
    for _ in range(ITERS - 1):
        steps = [twice - product(a, x) for a, x in zip(matrices, estimates)]
        estimates = [product(x, step) for x, step in zip(estimates, steps)]
    return estimates


def inverse_kernel(layout, places, trial, *refs):
    pieces, (full, out) = refs[:-2], refs[-2:]
    count = out.shape[0]
    matrices = []
    for walker in range(count):
        for piece, (steps, dy) in zip(pieces, places):
            chip = layout.origin(steps, dy)
            for block in range(2):
                full[walker, chip, block] = piece[block * count + walker]
        rows = full[walker].reshape(-1, full.shape[-1])
        matrices.append(jnp.dot(trial[...], rows, preferred_element_type=F32))
    for walker, inverse in enumerate(newton_inverses(matrices)):
        out[walker] = inverse.astype(out.dtype)


def inverses_of(layout, trial, stream, count):
    arrays = [array for array, *_ in stream.pieces()]
    places = [place for _, *place in stream.pieces()]
    _, rows, electrons = arrays[0].shape
    return pl.pallas_call(
        functools.partial(inverse_kernel, layout, places),
        out_shape=[
            jax.ShapeDtypeStruct((count, layout.chol // 2, 2, rows, electrons), BF16),
            jax.ShapeDtypeStruct((count, electrons, electrons), BF16),
        ],
        in_specs=vmem_specs(1 + len(arrays)),
        out_specs=vmem_specs(2),
        compiler_params=params(8),
        cost_estimate=pl.CostEstimate(
            flops=2 * count * electrons**2 * (trial.shape[1] + 6 * (ITERS - 1) * electrons),
            bytes_accessed=4 * (count + 1) * trial.shape[1] * electrons,
            transcendentals=0,
        ),
    )(trial, *arrays)


def bias_kernel(sizes, rot_mine, rot_theirs, *refs):
    streams = len(sizes)
    chunks, inverses, (out, greens) = refs[:streams], refs[streams : 2 * streams], refs[-2:]
    vectors, rows, electrons = rot_mine.shape
    b = lax.rem(lax.axis_index("chol"), 2)
    count = 0
    for chunk, inverse, size in zip(chunks, inverses, sizes):
        for walker in range(size):
            both = jnp.concatenate([chunk[walker], chunk[size + walker]], axis=0)
            product = jnp.dot(both, inverse[walker], preferred_element_type=F32).astype(BF16)
            greens[:, :, count] = product.reshape(2, rows // BLOCK, BLOCK, electrons)
            count += 1
    total = jnp.zeros((vectors * BLOCK, count * BLOCK), F32)
    for half, rot in ((b, rot_mine), (1 - b, rot_theirs)):
        for block in range(rows // BLOCK):
            total += lax.dot_general(
                rot[:, block * BLOCK : (block + 1) * BLOCK, :].reshape(vectors * BLOCK, electrons),
                greens[half, block].reshape(count * BLOCK, electrons),
                (((1,), (1,)), ((), ())),
                preferred_element_type=F32,
            )
    same = lax.rem(lax.broadcasted_iota(jnp.int32, total.shape, 0), BLOCK) == lax.rem(
        lax.broadcasted_iota(jnp.int32, total.shape, 1), BLOCK
    )
    summed = jnp.sum(
        jnp.where(same, total, 0.0).reshape(vectors, BLOCK, count * BLOCK), axis=1
    )
    shape = (count, count * BLOCK)
    pick = (
        lax.broadcasted_iota(jnp.int32, shape, 1) // BLOCK
        == lax.broadcasted_iota(jnp.int32, shape, 0)
    ).astype(F32)
    out[...] = lax.dot_general(
        pick, summed, (((1,), (1,)), ((), ())), precision=HIGHEST, preferred_element_type=F32
    )


def bias_of(chunks, inverses, rot_mine, rot_theirs):
    vectors, rows, electrons = rot_mine.shape
    sizes = [inverse.shape[0] for inverse in inverses]
    count = sum(sizes)
    return pl.pallas_call(
        functools.partial(bias_kernel, sizes),
        out_shape=jax.ShapeDtypeStruct((count, vectors), F32),
        in_specs=vmem_specs(2 + 2 * len(sizes)),
        out_specs=pl.BlockSpec(memory_space=pltpu.VMEM),
        scratch_shapes=[pltpu.VMEM((2, rows // BLOCK, count, BLOCK, electrons), BF16)],
        compiler_params=params(12),
        cost_estimate=pl.CostEstimate(
            flops=4 * count * rows * electrons * (electrons + vectors * BLOCK),
            bytes_accessed=4 * (vectors + count) * rows * electrons,
            transcendentals=0,
        ),
    )(rot_mine, rot_theirs, *chunks, *inverses)


def potential_kernel(order, fields, mine, mine_across, theirs, theirs_across, cholesky, *refs):
    bias_out, kept, *sent, weights = refs
    per_group, vectors = fields.shape
    half, piece = kept.shape[0], sent[0].shape[1]
    sums = (mine[...] + mine_across[...], theirs[...] + theirs_across[...])
    b = lax.rem(lax.axis_index("chol"), 2)
    row = lax.broadcasted_iota(jnp.int32, (per_group, vectors), 0)
    bias = jnp.zeros((per_group, vectors), F32)
    for walker in range(half):
        for part, core in zip(sums, (b, 1 - b)):
            slot = order[core * half + walker]
            bias += jnp.where(row == slot, part[walker : walker + 1, :], 0.0)
    bias = TAU_ROOT * bias
    bias_out[...] = bias
    shifted = (fields[...] - bias).astype(BF16)
    slot = jnp.zeros((per_group * BLOCK, 1), jnp.int32)
    place = lax.broadcasted_iota(jnp.int32, slot.shape, 0) // BLOCK
    for at in range(per_group):
        slot = jnp.where(place == at, order[lax.rem(at + b * half, per_group)], slot)
    tall = (per_group * BLOCK, per_group)
    rows = (lax.broadcasted_iota(jnp.int32, tall, 1) == slot).astype(BF16)
    wide = (vectors, vectors * BLOCK)
    columns = (
        lax.broadcasted_iota(jnp.int32, wide, 1) // BLOCK
        == lax.broadcasted_iota(jnp.int32, wide, 0)
    ).astype(BF16)
    spread = jnp.dot(rows, shifted, preferred_element_type=F32).astype(BF16)
    spread = jnp.dot(spread, columns, preferred_element_type=F32)
    same = lax.rem(lax.broadcasted_iota(jnp.int32, spread.shape, 0), BLOCK) == lax.rem(
        lax.broadcasted_iota(jnp.int32, spread.shape, 1), BLOCK
    )
    weights[...] = jnp.where(same, spread, 0.0).astype(BF16)
    rows, orbitals = cholesky.shape[1:]
    for at in range(0, rows, BLOCK):
        columns = cholesky[:, at : at + BLOCK, :].reshape(vectors * BLOCK, orbitals)
        result = TAU_ROOT * jnp.dot(weights[...], columns, preferred_element_type=F32)
        result = result.astype(BF16).reshape(2 * half, BLOCK, orbitals)
        kept[:, at : at + BLOCK, :] = result[:half]
        start = at % piece
        sent[at // piece][:, start : start + BLOCK, :] = result[half:]


def potential_of(order, fields, parts, cholesky):
    per_group, vectors = fields.shape
    half = per_group // 2
    _, rows, orbitals = cholesky.shape
    sent = jax.ShapeDtypeStruct((half, rows // 2, orbitals), BF16)
    return pl.pallas_call(
        potential_kernel,
        out_shape=[
            jax.ShapeDtypeStruct((per_group, vectors), F32),
            jax.ShapeDtypeStruct((half, rows, orbitals), BF16),
            sent,
            sent,
        ],
        in_specs=[pl.BlockSpec(memory_space=pltpu.SMEM)] + vmem_specs(6),
        out_specs=vmem_specs(4),
        scratch_shapes=[pltpu.VMEM((per_group * BLOCK, vectors * BLOCK), BF16)],
        compiler_params=params(12),
    )(order, fields, *parts, cholesky)


def first_kernel(sibling, parts, *refs):
    potential, fulls, (rounded, base) = refs[:parts], refs[parts:-2], refs[-2:]
    b = lax.rem(lax.axis_index("chol"), 2)
    chip = lax.axis_index("chol") // 2
    count = 0
    for full in fulls:
        for walker in range(full.shape[0]):
            rows = jnp.concatenate([part[count] for part in potential], axis=0)
            columns = full[walker].reshape(-1, full.shape[-1])
            term = jnp.dot(rows, columns, preferred_element_type=F32)
            rounded[count] = term.astype(BF16)
            own = full[walker, chip, 1 - b if sibling else b]
            base[count] = own.astype(F32) + term
            count += 1


def first_of(potential, fulls, sibling):
    half, _, orbitals = potential[0].shape
    rows, electrons = fulls[0].shape[-2:]
    shape = (half, rows, electrons)
    return pl.pallas_call(
        functools.partial(first_kernel, sibling, len(potential)),
        out_shape=[jax.ShapeDtypeStruct(shape, BF16), jax.ShapeDtypeStruct(shape, F32)],
        in_specs=vmem_specs(len(potential) + len(fulls)),
        out_specs=vmem_specs(2),
        compiler_params=params(8),
        cost_estimate=pl.CostEstimate(
            flops=2 * half * rows * orbitals * electrons,
            bytes_accessed=2 * half * orbitals * (rows + electrons),
            transcendentals=0,
        ),
    )(*potential, *fulls)


def second_kernel(layout, places, parts, *refs):
    potential, base, pieces = refs[:parts], refs[parts], refs[parts + 1 : -2]
    out, full = refs[-2:]
    b = lax.rem(lax.axis_index("chol"), 2)
    for walker in range(out.shape[0]):
        for piece, (sibling, steps, dy) in zip(pieces, places):
            block = 1 - b if sibling else b
            full[walker, layout.origin(steps, dy), block] = piece[walker]
        rows = jnp.concatenate([part[walker] for part in potential], axis=0)
        columns = full[walker].reshape(-1, full.shape[-1])
        term = jnp.dot(rows, columns, preferred_element_type=F32)
        out[walker] = (base[walker] + 0.5 * term).astype(BF16)


def second_of(layout, potential, base, streams):
    arrays, places = [], []
    for sibling, stream in enumerate(streams):
        for array, steps, dy in stream.pieces():
            arrays.append(array)
            places.append((sibling, steps, dy))
    orbitals = potential[0].shape[2]
    half, rows, electrons = base.shape
    return pl.pallas_call(
        functools.partial(second_kernel, layout, places, len(potential)),
        out_shape=[
            jax.ShapeDtypeStruct((half, rows, electrons), BF16),
            jax.ShapeDtypeStruct((half, layout.chol // 2, 2, rows, electrons), BF16),
        ],
        in_specs=vmem_specs(len(potential) + 1 + len(arrays)),
        out_specs=vmem_specs(2),
        compiler_params=params(8),
        cost_estimate=pl.CostEstimate(
            flops=2 * half * rows * orbitals * electrons,
            bytes_accessed=2 * half * orbitals * (rows + 3 * electrons),
            transcendentals=0,
        ),
    )(*potential, base, *arrays)


def finish_kernel(order, potential, base, full, out, results, semaphores):
    half = base.shape[0]
    b = lax.rem(lax.axis_index("chol"), 2)
    copies = []
    for walker in range(half):
        columns = full[walker].reshape(-1, full.shape[-1])
        term = jnp.dot(potential[walker], columns, preferred_element_type=F32)
        results[walker] = (base[walker] + 0.5 * term).astype(BF16)
        copies.append(
            pltpu.make_async_copy(
                results.at[walker], out.at[order[b * half + walker]], semaphores.at[walker]
            )
        )
        copies[-1].start()
    for copy in copies:
        copy.wait()


def finish(order, potential, base, full):
    half, rows, electrons = base.shape
    orbitals = potential.shape[2]
    return pl.pallas_call(
        finish_kernel,
        out_shape=jax.ShapeDtypeStruct((2 * half, rows, electrons), BF16),
        in_specs=[pl.BlockSpec(memory_space=pltpu.SMEM)] + vmem_specs(3),
        out_specs=pl.BlockSpec(memory_space=pl.ANY),
        scratch_shapes=[
            pltpu.VMEM((half, rows, electrons), BF16),
            pltpu.SemaphoreType.DMA((half,)),
        ],
        compiler_params=params(8),
        cost_estimate=pl.CostEstimate(
            flops=2 * half * rows * orbitals * electrons,
            bytes_accessed=2 * half * orbitals * (rows + electrons),
            transcendentals=0,
        ),
    )(order, potential, base, full)


def place_kernel(order, theirs, _, out, semaphores):
    half = theirs.shape[0]
    b = lax.rem(lax.axis_index("chol"), 2)
    copies = [
        pltpu.make_async_copy(
            theirs.at[walker], out.at[order[(1 - b) * half + walker]], semaphores.at[walker]
        )
        for walker in range(half)
    ]
    for copy in copies:
        copy.start()
    for copy in copies:
        copy.wait()


def place(order, theirs, out):
    return pl.pallas_call(
        place_kernel,
        out_shape=jax.ShapeDtypeStruct(out.shape, out.dtype),
        in_specs=[pl.BlockSpec(memory_space=pltpu.SMEM)] + vmem_specs(1)
        + [pl.BlockSpec(memory_space=pl.ANY)],
        out_specs=pl.BlockSpec(memory_space=pl.ANY),
        scratch_shapes=[pltpu.SemaphoreType.DMA((theirs.shape[0],))],
        input_output_aliases={2: 0},
        compiler_params=params(4),
    )(order, theirs, out)


def split_kernel(source, walkers, *refs):
    targets, (order, picked, semaphores) = refs[:4], refs[4:]
    per_group = walkers.shape[0]
    half = per_group // 2
    share = half // 2
    group = lax.axis_index("walk")
    b = lax.rem(lax.axis_index("chol"), 2)
    stayed, arrived, sent = jnp.int32(0), jnp.int32(0), jnp.int32(0)
    for slot in range(per_group):
        local = source[group * per_group + slot] - group * per_group
        stays = ((local >= 0) & (local < per_group)).astype(jnp.int32)
        picked[jnp.where(stays == 1, jnp.minimum(stayed, half - 1), per_group)] = local
        rank = jnp.minimum(jnp.where(stays == 1, stayed, arrived), half - 1)
        core = rank // share
        order[core * half + (1 - stays) * share + rank - core * share] = jnp.int32(slot)
        stayed, arrived = stayed + stays, arrived + 1 - stays
        local = source[(1 - group) * per_group + slot] - group * per_group
        goes = ((local >= 0) & (local < per_group)).astype(jnp.int32)
        picked[jnp.where(goes == 1, half + jnp.minimum(sent, half - 1), per_group)] = local
        sent = sent + goes
    offsets = (b * share, (1 - b) * share, half + b * share, half + (1 - b) * share)
    copies = []
    for target, offset in reversed(list(zip(targets, offsets))):
        for walker in range(share):
            copies.append(
                pltpu.make_async_copy(
                    walkers.at[picked[offset + walker]],
                    target.at[walker],
                    semaphores.at[len(copies)],
                )
            )
    for copy in copies:
        copy.start()
    for copy in copies:
        copy.wait()


def split_walkers(walkers, source):
    per_group, rows, electrons = walkers.shape
    share = jax.ShapeDtypeStruct((per_group // 4, rows, electrons), walkers.dtype)
    return pl.pallas_call(
        split_kernel,
        out_shape=[share] * 4 + [jax.ShapeDtypeStruct((per_group,), jnp.int32)],
        in_specs=[pl.BlockSpec(memory_space=pltpu.SMEM), pl.BlockSpec(memory_space=pl.ANY)],
        out_specs=[pl.BlockSpec(memory_space=pl.ANY)] * 4
        + [pl.BlockSpec(memory_space=pltpu.SMEM)],
        scratch_shapes=[
            pltpu.SMEM((per_group + 1,), jnp.int32),
            pltpu.SemaphoreType.DMA((per_group,)),
        ],
        compiler_params=params(4),
    )(source, walkers)


def ranks(flags):
    count = flags.shape[-1]
    before = jnp.arange(count)[None, :] < jnp.arange(count)[:, None]
    return jnp.sum(jnp.where(before & flags[..., None, :], 1, 0), axis=-1)


def migrate(layout, walkers, source):
    per_group = walkers.shape[0]
    half = per_group // 2
    group = lax.axis_index("walk")
    if layout.walk == 2 and half % 2 == 0:
        stay, stay_sent, near, cross, order = split_walkers(walkers, source)
        count = 2 * layout.chol
        across = [(index + layout.chol) % count for index in range(count)]
        axes = ("walk", "chol")
        near = lax.ppermute(near, axes, list(enumerate(across)))
        cross = lax.ppermute(cross, axes, [(i, j ^ 1) for i, j in enumerate(across)])
        return [(stay, layout.shift(stay_sent, db=1)), (near, cross)], order
    table = source.reshape(layout.walk, per_group)
    incoming = lax.dynamic_index_in_dim(table, group, 0, keepdims=False)
    incoming_groups = incoming // per_group

    def outgoing(distance):
        row = lax.dynamic_index_in_dim(table, (group + distance) % layout.walk, 0, keepdims=False)
        local = row - group * per_group
        here = (local >= 0) & (local < per_group)
        match = here[None, :] & (ranks(here)[None, :] == jnp.arange(half)[:, None])
        return jnp.take(walkers, jnp.sum(jnp.where(match, local[None, :], 0), axis=1), axis=0)

    arrived = [outgoing(0)]
    for distance in range(1, layout.walk):
        pairs = [(g, (g + distance) % layout.walk) for g in range(layout.walk)]
        arrived.append(lax.ppermute(outgoing(distance), "walk", pairs))
    slots = jnp.arange(per_group)
    same = (incoming_groups[:, None] == incoming_groups[None, :]) & (slots[None, :] < slots[:, None])
    rank = jnp.sum(same.astype(jnp.int32), axis=1)
    distance = (group - incoming_groups) % layout.walk
    migrated = jnp.take(jnp.concatenate(arrived, axis=0), distance * half + rank, axis=0)
    b = lax.axis_index("chol") % 2
    mine = lax.dynamic_slice_in_dim(migrated, b * half, half, 0)
    theirs = lax.dynamic_slice_in_dim(migrated, (1 - b) * half, half, 0)
    theirs = layout.shift(theirs, db=1)
    share = half // 2
    shares = [(mine[:share], theirs[:share]), (mine[share:], theirs[share:])]
    return shares, slots.astype(jnp.int32)


def shards(layout, walkers, trial, cholesky, rotated, fields, source):
    b = lax.axis_index("chol") % 2
    shares, order = migrate(layout, walkers, source)
    sizes = [own.shape[0] for own, _ in shares]
    chunks = [
        jnp.concatenate([jnp.where(b == 0, own, other), jnp.where(b == 0, other, own), *extra])
        for (own, other), extra in zip(shares, ([trial[None]], []))
    ]
    streams = [Stream(layout, chunks[0]), Stream(layout, chunks[1], last_along_z=True)]
    rot_theirs = layout.shift(rotated, db=1)
    for stage in range(layout.z):
        if stage == layout.z - 1:
            early = jnp.stack([array[-1] for array, *_ in streams[0].pieces()])
            early, rot_theirs = streams[0].advance((layout.shift(early, db=1), rot_theirs))
        else:
            streams[0].advance()
        streams[1].advance()
    late = layout.shift(streams[0].across[-1][-1:], db=1)
    turned = transposed(layout, streams[0], (early, late))
    fulls, inverses = zip(
        *[inverses_of(layout, turned, stream, size) for stream, size in zip(streams, sizes)]
    )
    total = bias_of(chunks, inverses, rotated, rot_theirs)
    parts = [total] + [layout.shift(total, dz=dz) for dz in range(1, layout.z)]
    while len(parts) > 1:
        far = len(parts) // 2
        parts = [parts[at] + parts[at + far] for at in range(far)]
    parts = [parts[0]] + [layout.shift(parts[0], dy=dy, db=db) for dy, db in ((1, 0), (0, 1), (1, 1))]
    force_bias, kept, *sent = potential_of(order, fields, parts, cholesky)
    received = [layout.shift(part, db=1) for part in sent]

    rounded, base = first_of([kept], fulls, 0)
    rounded_theirs, base_theirs = first_of(received, fulls, 1)
    streams = [Stream(layout, rounded), Stream(layout, rounded_theirs, last_along_z=True)]
    for _ in range(layout.z):
        for stream in streams:
            stream.advance()
    sent, full = second_of(layout, received, base_theirs, streams)
    theirs = layout.shift(sent, db=1)
    return place(order, theirs, finish(order, kept, base, full)), force_bias


def solution(mesh):
    in_specs = (
        P("walk", "chol", None),
        P("chol", None),
        P(None, "chol", None),
        P(None, "chol", None),
        P("walk", None),
        P(),
    )
    out_specs = (P("walk", "chol", None), P("walk", None))
    layout = Layout(mesh.shape["walk"], mesh.shape["chol"])
    return jax.shard_map(
        functools.partial(shards, layout),
        mesh=mesh,
        in_specs=in_specs,
        out_specs=out_specs,
        check_vma=False,
    )
```

```python
import functools

import jax
import jax.numpy as jnp
from jax import lax
from jax.experimental import pallas as pl
from jax.experimental.pallas import tpu as pltpu
from jax.sharding import PartitionSpec as P

ITERS = 3
TAU_ROOT = 0.1
BLOCK = 16
HIGHEST = lax.Precision.HIGHEST
MIB = 1024 * 1024

F32 = jnp.float32
BF16 = jnp.bfloat16


def params(mebibytes):
    return pltpu.CompilerParams(vmem_limit_bytes=mebibytes * MIB)


def vmem_specs(count):
    return [pl.BlockSpec(memory_space=pltpu.VMEM)] * count


class Layout:
    def __init__(self, walk_size, chol_size):
        self.walk = walk_size
        self.chol = chol_size
        self.z = chol_size // 4

    def shift(self, array, dz=0, dy=0, db=0):
        pairs = []
        for index in range(self.chol):
            z, y, b = index // 4, (index // 2) % 2, index % 2
            target = (((z + dz) % self.z) * 2 + (y ^ dy)) * 2 + (b ^ db)
            pairs.append((index, target))
        return lax.ppermute(array, "chol", pairs)

    def step(self, array):
        ring = [*range(0, self.z, 2), *reversed(range(1, self.z, 2))]
        target = {z: ring[(at + 1) % self.z] for at, z in enumerate(ring)}
        pairs = [(index, target[index // 4] * 4 + index % 4) for index in range(self.chol)]
        return lax.ppermute(array, "chol", pairs)

    def origin(self, steps, dy):
        index = lax.axis_index("chol")
        z, y = index // 4, lax.rem(index // 2, 2)
        at = jnp.where(lax.rem(z, 2) == 0, z // 2, self.z - (z + 1) // 2)
        at = lax.rem(at + (self.z - steps), self.z)
        z = jnp.where(2 * at < self.z, 2 * at, 2 * (self.z - at) - 1)
        return z * 2 + (y + dy - 2 * y * dy)


class Stream:
    def __init__(self, layout, piece):
        self.layout = layout
        self.ring = [piece]
        self.across = []
        self.last = []

    def moves(self):
        latest = self.ring[-1]
        if len(self.ring) < self.layout.z:
            return [self.layout.shift(latest, dy=1), self.layout.step(latest)]
        half = (latest.shape[0] + 1) // 2
        return [
            self.layout.shift(latest[:half], dy=1),
            self.layout.step(self.across[-1][half:]),
        ]

    def accept(self, moved):
        if len(self.ring) < self.layout.z:
            self.across.append(moved[0])
            self.ring.append(moved[1])
        else:
            self.last = moved

    def advance(self, anchors=()):
        moved = self.moves()
        if anchors or len(self.ring) < self.layout.z:
            anchors, moved = lax.optimization_barrier((anchors, moved))
        self.accept(moved)
        return anchors

    def pieces(self):
        ring = [(array, 0, steps, 0) for steps, array in enumerate(self.ring)]
        across = [(array, 0, steps, 1) for steps, array in enumerate(self.across)]
        lower, upper = self.last
        steps = self.layout.z - 1
        return ring + across + [(lower, 0, steps, 1), (upper, lower.shape[0], steps, 1)]


def operands(streams):
    arrays, slabs = [], []
    for stream in streams:
        slabs.append([])
        for array, first, steps, dy in stream.pieces():
            for at in range(array.shape[0]):
                slabs[-1].append((len(arrays), at, first + at, steps, dy))
            arrays.append(array)
    return arrays, slabs


def product(left, right):
    high, right_high = left.astype(BF16), right.astype(BF16)
    low = (left - high.astype(F32)).astype(BF16)
    right_low = (right - right_high.astype(F32)).astype(BF16)
    return jnp.dot(
        jnp.concatenate([high, high, low], axis=1),
        jnp.concatenate([right_high, right_low, right_high], axis=0),
        preferred_element_type=F32,
    )


def newton_inverses(matrices):
    shape = matrices[0].shape
    same = lax.broadcasted_iota(jnp.int32, shape, 0) == lax.broadcasted_iota(jnp.int32, shape, 1)
    twice = jnp.where(same, 2.0, 0.0).astype(F32)
    estimates = [twice - matrix for matrix in matrices]
    for _ in range(ITERS - 1):
        steps = [twice - product(a, x) for a, x in zip(matrices, estimates)]
        estimates = [product(x, step) for x, step in zip(estimates, steps)]
    return estimates


def bias_kernel(layout, slabs, counts, rot_mine, rot_theirs, early, late, *refs):
    fulls, (out, buffer, turned, greens) = refs[-4 - len(counts) : -4], refs[-4:]
    pieces = refs[: -4 - len(counts)]
    vectors, rows, electrons = rot_mine.shape
    index = lax.axis_index("chol")
    chip, b = index // 2, lax.rem(index, 2)

    theirs = [(early, at) for at in range(early.shape[0])] + [(late, 0)]
    trial = [slab for slab in slabs[0] if slab[2] == 2 * counts[0]]
    for (operand, at, _, steps, dy), (part, place) in zip(trial, theirs):
        origin = layout.origin(steps, dy)
        buffer[origin, b] = pieces[operand][at]
        buffer[origin, 1 - b] = part[place]
    turned[...] = buffer[...].reshape(-1, electrons).T

    matrices = []
    for full, count, stream in zip(fulls, counts, slabs):
        for operand, at, slab, steps, dy in stream:
            if slab < 2 * count:
                full[slab % count, layout.origin(steps, dy), slab // count] = pieces[operand][at]
        for walker in range(count):
            columns = full[walker].reshape(-1, electrons)
            matrices.append(jnp.dot(turned[...], columns, preferred_element_type=F32))
    inverses = [inverse.astype(BF16) for inverse in newton_inverses(matrices)]

    walkers = [(full, at) for full, count in zip(fulls, counts) for at in range(count)]
    for number, (full, walker) in enumerate(walkers):
        both = full[walker, chip].reshape(2 * rows, electrons)
        green = jnp.dot(both, inverses[number], preferred_element_type=F32).astype(BF16)
        greens[:, :, number] = green.reshape(2, rows // BLOCK, BLOCK, electrons)
    width = len(walkers) * BLOCK
    total = jnp.zeros((vectors * BLOCK, width), F32)
    for half, rot in ((b, rot_mine), (1 - b, rot_theirs)):
        for block in range(rows // BLOCK):
            total += lax.dot_general(
                rot[:, block * BLOCK : (block + 1) * BLOCK, :].reshape(vectors * BLOCK, electrons),
                greens[half, block].reshape(width, electrons),
                (((1,), (1,)), ((), ())),
                preferred_element_type=F32,
            )
    same = lax.rem(lax.broadcasted_iota(jnp.int32, total.shape, 0), BLOCK) == lax.rem(
        lax.broadcasted_iota(jnp.int32, total.shape, 1), BLOCK
    )
    summed = jnp.sum(jnp.where(same, total, 0.0).reshape(vectors, BLOCK, width), axis=1)
    shape = (len(walkers), width)
    pick = (
        lax.broadcasted_iota(jnp.int32, shape, 1) // BLOCK
        == lax.broadcasted_iota(jnp.int32, shape, 0)
    ).astype(F32)
    out[...] = lax.dot_general(
        pick, summed, (((1,), (1,)), ((), ())), precision=HIGHEST, preferred_element_type=F32
    )


def bias_of(layout, streams, counts, early, late, rot_mine, rot_theirs):
    arrays, slabs = operands(streams)
    vectors, rows, electrons = rot_mine.shape
    chips = layout.chol // 2
    total = sum(counts)
    return pl.pallas_call(
        functools.partial(bias_kernel, layout, slabs, counts),
        out_shape=[
            jax.ShapeDtypeStruct((count, chips, 2, rows, electrons), BF16) for count in counts
        ]
        + [jax.ShapeDtypeStruct((total, vectors), F32)],
        in_specs=vmem_specs(4 + len(arrays)),
        out_specs=vmem_specs(len(counts) + 1),
        scratch_shapes=[
            pltpu.VMEM((chips, 2, rows, electrons), BF16),
            pltpu.VMEM((electrons, 2 * chips * rows), BF16),
            pltpu.VMEM((2, rows // BLOCK, total, BLOCK, electrons), BF16),
        ],
        compiler_params=params(20),
        cost_estimate=pl.CostEstimate(
            flops=2 * total * electrons**2 * (2 * chips * rows + 6 * (ITERS - 1) * electrons)
            + 4 * total * rows * electrons * (electrons + vectors * BLOCK),
            bytes_accessed=4 * (vectors + total) * rows * electrons
            + 4 * (total + 1) * 2 * chips * rows * electrons,
            transcendentals=0,
        ),
    )(rot_mine, rot_theirs, early, late, *arrays)


def potential_kernel(order, fields, mine, mine_across, theirs, theirs_across, cholesky, *refs):
    bias_out, kept, *sent, weights = refs
    per_group, vectors = fields.shape
    half, piece = kept.shape[0], sent[0].shape[1]
    sums = (mine[...] + mine_across[...], theirs[...] + theirs_across[...])
    b = lax.rem(lax.axis_index("chol"), 2)
    row = lax.broadcasted_iota(jnp.int32, (per_group, vectors), 0)
    bias = jnp.zeros((per_group, vectors), F32)
    for walker in range(half):
        for part, core in zip(sums, (b, 1 - b)):
            slot = order[core * half + walker]
            bias += jnp.where(row == slot, part[walker : walker + 1, :], 0.0)
    bias = TAU_ROOT * bias
    bias_out[...] = bias
    shifted = (fields[...] - bias).astype(BF16)
    slot = jnp.zeros((per_group * BLOCK, 1), jnp.int32)
    place = lax.broadcasted_iota(jnp.int32, slot.shape, 0) // BLOCK
    for at in range(per_group):
        slot = jnp.where(place == at, order[lax.rem(at + b * half, per_group)], slot)
    tall = (per_group * BLOCK, per_group)
    rows = (lax.broadcasted_iota(jnp.int32, tall, 1) == slot).astype(BF16)
    wide = (vectors, vectors * BLOCK)
    columns = (
        lax.broadcasted_iota(jnp.int32, wide, 1) // BLOCK
        == lax.broadcasted_iota(jnp.int32, wide, 0)
    ).astype(BF16)
    spread = jnp.dot(rows, shifted, preferred_element_type=F32).astype(BF16)
    spread = jnp.dot(spread, columns, preferred_element_type=F32)
    same = lax.rem(lax.broadcasted_iota(jnp.int32, spread.shape, 0), BLOCK) == lax.rem(
        lax.broadcasted_iota(jnp.int32, spread.shape, 1), BLOCK
    )
    weights[...] = jnp.where(same, spread, 0.0).astype(BF16)
    rows, orbitals = cholesky.shape[1:]
    for at in range(0, rows, BLOCK):
        columns = cholesky[:, at : at + BLOCK, :].reshape(vectors * BLOCK, orbitals)
        result = TAU_ROOT * jnp.dot(weights[...], columns, preferred_element_type=F32)
        result = result.astype(BF16).reshape(2 * half, BLOCK, orbitals)
        kept[:, at : at + BLOCK, :] = result[:half]
        start = at % piece
        sent[at // piece][:, start : start + BLOCK, :] = result[half:]


def potential_of(order, fields, parts, cholesky):
    per_group, vectors = fields.shape
    half = per_group // 2
    _, rows, orbitals = cholesky.shape
    sent = jax.ShapeDtypeStruct((half, rows // 2, orbitals), BF16)
    return pl.pallas_call(
        potential_kernel,
        out_shape=[
            jax.ShapeDtypeStruct((per_group, vectors), F32),
            jax.ShapeDtypeStruct((half, rows, orbitals), BF16),
            sent,
            sent,
        ],
        in_specs=[pl.BlockSpec(memory_space=pltpu.SMEM)] + vmem_specs(6),
        out_specs=vmem_specs(4),
        scratch_shapes=[pltpu.VMEM((per_group * BLOCK, vectors * BLOCK), BF16)],
        compiler_params=params(12),
    )(order, fields, *parts, cholesky)


def first_kernel(sibling, parts, *refs):
    potential, fulls, (rounded, base) = refs[:parts], refs[parts:-2], refs[-2:]
    b = lax.rem(lax.axis_index("chol"), 2)
    chip = lax.axis_index("chol") // 2
    count = 0
    for full in fulls:
        for walker in range(full.shape[0]):
            rows = jnp.concatenate([part[count] for part in potential], axis=0)
            columns = full[walker].reshape(-1, full.shape[-1])
            term = jnp.dot(rows, columns, preferred_element_type=F32)
            rounded[count] = term.astype(BF16)
            own = full[walker, chip, 1 - b if sibling else b]
            base[count] = own.astype(F32) + term
            count += 1


def first_of(potential, fulls, sibling):
    half, _, orbitals = potential[0].shape
    rows, electrons = fulls[0].shape[-2:]
    shape = (half, rows, electrons)
    return pl.pallas_call(
        functools.partial(first_kernel, sibling, len(potential)),
        out_shape=[jax.ShapeDtypeStruct(shape, BF16), jax.ShapeDtypeStruct(shape, F32)],
        in_specs=vmem_specs(len(potential) + len(fulls)),
        out_specs=vmem_specs(2),
        compiler_params=params(8),
        cost_estimate=pl.CostEstimate(
            flops=2 * half * rows * orbitals * electrons,
            bytes_accessed=2 * half * orbitals * (rows + electrons),
            transcendentals=0,
        ),
    )(*potential, *fulls)


def second_kernel(layout, slabs, parts, *refs):
    potential, base, pieces = refs[:parts], refs[parts], refs[parts + 1 : -2]
    out, full = refs[-2:]
    b = lax.rem(lax.axis_index("chol"), 2)
    for block, stream in zip((b, 1 - b), slabs):
        for operand, at, walker, steps, dy in stream:
            full[walker, layout.origin(steps, dy), block] = pieces[operand][at]
    for walker in range(out.shape[0]):
        rows = jnp.concatenate([part[walker] for part in potential], axis=0)
        columns = full[walker].reshape(-1, full.shape[-1])
        term = jnp.dot(rows, columns, preferred_element_type=F32)
        out[walker] = (base[walker] + 0.5 * term).astype(BF16)


def second_of(layout, potential, base, streams):
    arrays, slabs = operands(streams)
    orbitals = potential[0].shape[2]
    half, rows, electrons = base.shape
    return pl.pallas_call(
        functools.partial(second_kernel, layout, slabs, len(potential)),
        out_shape=[
            jax.ShapeDtypeStruct((half, rows, electrons), BF16),
            jax.ShapeDtypeStruct((half, layout.chol // 2, 2, rows, electrons), BF16),
        ],
        in_specs=vmem_specs(len(potential) + 1 + len(arrays)),
        out_specs=vmem_specs(2),
        compiler_params=params(8),
        cost_estimate=pl.CostEstimate(
            flops=2 * half * rows * orbitals * electrons,
            bytes_accessed=2 * half * orbitals * (rows + 3 * electrons),
            transcendentals=0,
        ),
    )(*potential, base, *arrays)


def finish_kernel(order, potential, base, full, out, results, semaphores):
    half = base.shape[0]
    b = lax.rem(lax.axis_index("chol"), 2)
    copies = []
    for walker in range(half):
        columns = full[walker].reshape(-1, full.shape[-1])
        term = jnp.dot(potential[walker], columns, preferred_element_type=F32)
        results[walker] = (base[walker] + 0.5 * term).astype(BF16)
        copies.append(
            pltpu.make_async_copy(
                results.at[walker], out.at[order[b * half + walker]], semaphores.at[walker]
            )
        )
        copies[-1].start()
    for copy in copies:
        copy.wait()


def finish(order, potential, base, full):
    half, rows, electrons = base.shape
    orbitals = potential.shape[2]
    return pl.pallas_call(
        finish_kernel,
        out_shape=jax.ShapeDtypeStruct((2 * half, rows, electrons), BF16),
        in_specs=[pl.BlockSpec(memory_space=pltpu.SMEM)] + vmem_specs(3),
        out_specs=pl.BlockSpec(memory_space=pl.ANY),
        scratch_shapes=[
            pltpu.VMEM((half, rows, electrons), BF16),
            pltpu.SemaphoreType.DMA((half,)),
        ],
        compiler_params=params(8),
        cost_estimate=pl.CostEstimate(
            flops=2 * half * rows * orbitals * electrons,
            bytes_accessed=2 * half * orbitals * (rows + electrons),
            transcendentals=0,
        ),
    )(order, potential, base, full)


def place_kernel(order, theirs, _, out, semaphores):
    half = theirs.shape[0]
    b = lax.rem(lax.axis_index("chol"), 2)
    copies = [
        pltpu.make_async_copy(
            theirs.at[walker], out.at[order[(1 - b) * half + walker]], semaphores.at[walker]
        )
        for walker in range(half)
    ]
    for copy in copies:
        copy.start()
    for copy in copies:
        copy.wait()


def place(order, theirs, out):
    return pl.pallas_call(
        place_kernel,
        out_shape=jax.ShapeDtypeStruct(out.shape, out.dtype),
        in_specs=[pl.BlockSpec(memory_space=pltpu.SMEM)] + vmem_specs(1)
        + [pl.BlockSpec(memory_space=pl.ANY)],
        out_specs=pl.BlockSpec(memory_space=pl.ANY),
        scratch_shapes=[pltpu.SemaphoreType.DMA((theirs.shape[0],))],
        input_output_aliases={2: 0},
        compiler_params=params(4),
    )(order, theirs, out)


def split_kernel(source, walkers, *refs):
    targets, (order, picked, semaphores) = refs[:4], refs[4:]
    per_group = walkers.shape[0]
    half = per_group // 2
    share = half // 2
    group = lax.axis_index("walk")
    b = lax.rem(lax.axis_index("chol"), 2)
    stayed, arrived, sent = jnp.int32(0), jnp.int32(0), jnp.int32(0)
    for slot in range(per_group):
        local = source[group * per_group + slot] - group * per_group
        stays = ((local >= 0) & (local < per_group)).astype(jnp.int32)
        picked[jnp.where(stays == 1, jnp.minimum(stayed, half - 1), per_group)] = local
        rank = jnp.minimum(jnp.where(stays == 1, stayed, arrived), half - 1)
        core = rank // share
        order[core * half + (1 - stays) * share + rank - core * share] = jnp.int32(slot)
        stayed, arrived = stayed + stays, arrived + 1 - stays
        local = source[(1 - group) * per_group + slot] - group * per_group
        goes = ((local >= 0) & (local < per_group)).astype(jnp.int32)
        picked[jnp.where(goes == 1, half + jnp.minimum(sent, half - 1), per_group)] = local
        sent = sent + goes
    offsets = (b * share, (1 - b) * share, half + b * share, half + (1 - b) * share)
    copies = []
    for target, offset in reversed(list(zip(targets, offsets))):
        for walker in range(share):
            copies.append(
                pltpu.make_async_copy(
                    walkers.at[picked[offset + walker]],
                    target.at[walker],
                    semaphores.at[len(copies)],
                )
            )
    for copy in copies:
        copy.start()
    for copy in copies:
        copy.wait()


def split_walkers(walkers, source):
    per_group, rows, electrons = walkers.shape
    share = jax.ShapeDtypeStruct((per_group // 4, rows, electrons), walkers.dtype)
    return pl.pallas_call(
        split_kernel,
        out_shape=[share] * 4 + [jax.ShapeDtypeStruct((per_group,), jnp.int32)],
        in_specs=[pl.BlockSpec(memory_space=pltpu.SMEM), pl.BlockSpec(memory_space=pl.ANY)],
        out_specs=[pl.BlockSpec(memory_space=pl.ANY)] * 4
        + [pl.BlockSpec(memory_space=pltpu.SMEM)],
        scratch_shapes=[
            pltpu.SMEM((per_group + 1,), jnp.int32),
            pltpu.SemaphoreType.DMA((per_group,)),
        ],
        compiler_params=params(4),
    )(source, walkers)


def ranks(flags):
    count = flags.shape[-1]
    before = jnp.arange(count)[None, :] < jnp.arange(count)[:, None]
    return jnp.sum(jnp.where(before & flags[..., None, :], 1, 0), axis=-1)


def migrate(layout, walkers, source):
    per_group = walkers.shape[0]
    half = per_group // 2
    group = lax.axis_index("walk")
    if layout.walk == 2 and half % 2 == 0:
        stay, stay_sent, near, cross, order = split_walkers(walkers, source)
        count = 2 * layout.chol
        across = [(index + layout.chol) % count for index in range(count)]
        axes = ("walk", "chol")
        near = lax.ppermute(near, axes, list(enumerate(across)))
        cross = lax.ppermute(cross, axes, [(i, j ^ 1) for i, j in enumerate(across)])
        return [(stay, layout.shift(stay_sent, db=1)), (near, cross)], order
    table = source.reshape(layout.walk, per_group)
    incoming = lax.dynamic_index_in_dim(table, group, 0, keepdims=False)
    incoming_groups = incoming // per_group

    def outgoing(distance):
        row = lax.dynamic_index_in_dim(table, (group + distance) % layout.walk, 0, keepdims=False)
        local = row - group * per_group
        here = (local >= 0) & (local < per_group)
        match = here[None, :] & (ranks(here)[None, :] == jnp.arange(half)[:, None])
        return jnp.take(walkers, jnp.sum(jnp.where(match, local[None, :], 0), axis=1), axis=0)

    arrived = [outgoing(0)]
    for distance in range(1, layout.walk):
        pairs = [(g, (g + distance) % layout.walk) for g in range(layout.walk)]
        arrived.append(lax.ppermute(outgoing(distance), "walk", pairs))
    slots = jnp.arange(per_group)
    same = (incoming_groups[:, None] == incoming_groups[None, :]) & (slots[None, :] < slots[:, None])
    rank = jnp.sum(same.astype(jnp.int32), axis=1)
    distance = (group - incoming_groups) % layout.walk
    migrated = jnp.take(jnp.concatenate(arrived, axis=0), distance * half + rank, axis=0)
    b = lax.axis_index("chol") % 2
    mine = lax.dynamic_slice_in_dim(migrated, b * half, half, 0)
    theirs = lax.dynamic_slice_in_dim(migrated, (1 - b) * half, half, 0)
    theirs = layout.shift(theirs, db=1)
    share = half // 2
    shares = [(mine[:share], theirs[:share]), (mine[share:], theirs[share:])]
    return shares, slots.astype(jnp.int32)


def shards(layout, walkers, trial, cholesky, rotated, fields, source):
    b = lax.axis_index("chol") % 2
    shares, order = migrate(layout, walkers, source)
    sizes = [own.shape[0] for own, _ in shares]
    chunks = [
        jnp.concatenate([jnp.where(b == 0, own, other), jnp.where(b == 0, other, own), *extra])
        for (own, other), extra in zip(shares, ([trial[None]], []))
    ]
    streams = [Stream(layout, chunk) for chunk in chunks]
    rot_theirs = layout.shift(rotated, db=1)
    moved = lax.optimization_barrier([stream.moves() for stream in streams])
    for stream, arrays in zip(streams, moved):
        stream.accept(arrays)
    for _ in range(layout.z - 2):
        for stream in streams:
            stream.advance()
    slabs = [array[-1:] for array in (*streams[0].ring, *streams[0].across)]
    early = layout.shift(jnp.concatenate(slabs), db=1)
    late = layout.shift(early[layout.z - 1 : layout.z], dy=1)
    early, rot_theirs = streams[0].advance((early, rot_theirs))
    streams[1].advance()
    *fulls, total = bias_of(layout, streams, sizes, early, late, rotated, rot_theirs)
    parts = [total] + [layout.shift(total, dz=dz) for dz in range(1, layout.z)]
    while len(parts) > 1:
        far = len(parts) // 2
        parts = [parts[at] + parts[at + far] for at in range(far)]
    parts = [parts[0]] + [layout.shift(parts[0], dy=dy, db=db) for dy, db in ((1, 0), (0, 1), (1, 1))]
    force_bias, kept, *sent = potential_of(order, fields, parts, cholesky)
    received = [layout.shift(part, db=1) for part in sent]

    rounded, base = first_of([kept], fulls, 0)
    rounded_theirs, base_theirs = first_of(received, fulls, 1)
    streams = [Stream(layout, rounded), Stream(layout, rounded_theirs)]
    for _ in range(layout.z):
        for stream in streams:
            stream.advance()
    sent, full = second_of(layout, received, base_theirs, streams)
    theirs = layout.shift(sent, db=1)
    return place(order, theirs, finish(order, kept, base, full)), force_bias


def solution(mesh):
    in_specs = (
        P("walk", "chol", None),
        P("chol", None),
        P(None, "chol", None),
        P(None, "chol", None),
        P("walk", None),
        P(),
    )
    out_specs = (P("walk", "chol", None), P("walk", None))
    layout = Layout(mesh.shape["walk"], mesh.shape["chol"])
    return jax.shard_map(
        functools.partial(shards, layout),
        mesh=mesh,
        in_specs=in_specs,
        out_specs=out_specs,
        check_vma=False,
    )
```

```python
import functools

import jax
import jax.numpy as jnp
from jax import lax
from jax.experimental import pallas as pl
from jax.experimental.pallas import tpu as pltpu
from jax.sharding import PartitionSpec as P

ITERS = 3
TAU_ROOT = 0.1
BLOCK = 16
HIGHEST = lax.Precision.HIGHEST
MIB = 1024 * 1024

F32 = jnp.float32
BF16 = jnp.bfloat16


def params(mebibytes):
    return pltpu.CompilerParams(vmem_limit_bytes=mebibytes * MIB)


def vmem_specs(count):
    return [pl.BlockSpec(memory_space=pltpu.VMEM)] * count


class Layout:
    def __init__(self, walk_size, chol_size):
        self.walk = walk_size
        self.chol = chol_size
        self.z = chol_size // 4

    def shift(self, array, dz=0, dy=0, db=0):
        pairs = []
        for index in range(self.chol):
            z, y, b = index // 4, (index // 2) % 2, index % 2
            target = (((z + dz) % self.z) * 2 + (y ^ dy)) * 2 + (b ^ db)
            pairs.append((index, target))
        return lax.ppermute(array, "chol", pairs)

    def flip(self, array, mask):
        return lax.ppermute(array, "chol", [(i, i ^ mask) for i in range(self.chol)])

    def step(self, array):
        ring = [*range(0, self.z, 2), *reversed(range(1, self.z, 2))]
        target = {z: ring[(at + 1) % self.z] for at, z in enumerate(ring)}
        pairs = [(index, target[index // 4] * 4 + index % 4) for index in range(self.chol)]
        return lax.ppermute(array, "chol", pairs)

    def origin(self, steps, dy):
        index = lax.axis_index("chol")
        z, y = index // 4, lax.rem(index // 2, 2)
        at = jnp.where(lax.rem(z, 2) == 0, z // 2, self.z - (z + 1) // 2)
        at = lax.rem(at + (self.z - steps), self.z)
        z = jnp.where(2 * at < self.z, 2 * at, 2 * (self.z - at) - 1)
        return z * 2 + (y + dy - 2 * y * dy)


class Stream:
    def __init__(self, layout, piece):
        self.layout = layout
        self.ring = [piece]
        self.across = []
        self.last = []

    def moves(self):
        latest = self.ring[-1]
        if len(self.ring) < self.layout.z:
            return [self.layout.shift(latest, dy=1), self.layout.step(latest)]
        half = (latest.shape[0] + 1) // 2
        return [
            self.layout.shift(latest[:half], dy=1),
            self.layout.step(self.across[-1][half:]),
        ]

    def accept(self, moved):
        if len(self.ring) < self.layout.z:
            self.across.append(moved[0])
            self.ring.append(moved[1])
        else:
            self.last = moved

    def advance(self, anchors=()):
        moved = self.moves()
        if anchors or len(self.ring) < self.layout.z:
            anchors, moved = lax.optimization_barrier((anchors, moved))
        self.accept(moved)
        return anchors

    def pieces(self):
        ring = [(array, 0, steps, 0) for steps, array in enumerate(self.ring)]
        across = [(array, 0, steps, 1) for steps, array in enumerate(self.across)]
        lower, upper = self.last
        steps = self.layout.z - 1
        return ring + across + [(lower, 0, steps, 1), (upper, lower.shape[0], steps, 1)]


def operands(streams):
    arrays, slabs = [], []
    for stream in streams:
        slabs.append([])
        for array, first, steps, dy in stream.pieces():
            for at in range(array.shape[0]):
                slabs[-1].append((len(arrays), at, first + at, steps, dy))
            arrays.append(array)
    return arrays, slabs


def product(left, right):
    high, right_high = left.astype(BF16), right.astype(BF16)
    low = (left - high.astype(F32)).astype(BF16)
    right_low = (right - right_high.astype(F32)).astype(BF16)
    return jnp.dot(
        jnp.concatenate([high, high, low], axis=1),
        jnp.concatenate([right_high, right_low, right_high], axis=0),
        preferred_element_type=F32,
    )


def newton_inverses(matrices):
    shape = matrices[0].shape
    same = lax.broadcasted_iota(jnp.int32, shape, 0) == lax.broadcasted_iota(jnp.int32, shape, 1)
    twice = jnp.where(same, 2.0, 0.0).astype(F32)
    estimates = [twice - matrix for matrix in matrices]
    for _ in range(ITERS - 1):
        steps = [twice - product(a, x) for a, x in zip(matrices, estimates)]
        estimates = [product(x, step) for x, step in zip(estimates, steps)]
    return estimates


def transpose_kernel(matrix, out):
    out[...] = matrix[...].T


def transposed(matrix):
    return pl.pallas_call(
        transpose_kernel,
        out_shape=jax.ShapeDtypeStruct(matrix.shape[::-1], matrix.dtype),
        in_specs=vmem_specs(1),
        out_specs=pl.BlockSpec(memory_space=pltpu.VMEM),
        compiler_params=params(8),
    )(matrix)


def bias_kernel(layout, slabs, counts, rot_mine, rot_theirs, trial, *refs):
    fulls, (out, greens) = refs[-2 - len(counts) : -2], refs[-2:]
    pieces = refs[: -2 - len(counts)]
    vectors, rows, electrons = rot_mine.shape
    index = lax.axis_index("chol")
    chip, b = index // 2, lax.rem(index, 2)

    matrices = []
    for full, count, stream in zip(fulls, counts, slabs):
        for operand, at, slab, steps, dy in stream:
            full[slab % count, layout.origin(steps, dy), slab // count] = pieces[operand][at]
        for walker in range(count):
            columns = full[walker].reshape(-1, electrons)
            matrices.append(jnp.dot(trial[...], columns, preferred_element_type=F32))
    inverses = [inverse.astype(BF16) for inverse in newton_inverses(matrices)]

    walkers = [(full, at) for full, count in zip(fulls, counts) for at in range(count)]
    for number, (full, walker) in enumerate(walkers):
        both = full[walker, chip].reshape(2 * rows, electrons)
        green = jnp.dot(both, inverses[number], preferred_element_type=F32).astype(BF16)
        greens[:, :, number] = green.reshape(2, rows // BLOCK, BLOCK, electrons)
    width = len(walkers) * BLOCK
    total = jnp.zeros((vectors * BLOCK, width), F32)
    for half, rot in ((b, rot_mine), (1 - b, rot_theirs)):
        for block in range(rows // BLOCK):
            total += lax.dot_general(
                rot[:, block * BLOCK : (block + 1) * BLOCK, :].reshape(vectors * BLOCK, electrons),
                greens[half, block].reshape(width, electrons),
                (((1,), (1,)), ((), ())),
                preferred_element_type=F32,
            )
    same = lax.rem(lax.broadcasted_iota(jnp.int32, total.shape, 0), BLOCK) == lax.rem(
        lax.broadcasted_iota(jnp.int32, total.shape, 1), BLOCK
    )
    summed = jnp.sum(jnp.where(same, total, 0.0).reshape(vectors, BLOCK, width), axis=1)
    shape = (len(walkers), width)
    pick = (
        lax.broadcasted_iota(jnp.int32, shape, 1) // BLOCK
        == lax.broadcasted_iota(jnp.int32, shape, 0)
    ).astype(F32)
    out[...] = lax.dot_general(
        pick, summed, (((1,), (1,)), ((), ())), precision=HIGHEST, preferred_element_type=F32
    )


def bias_of(layout, streams, counts, trial, rot_mine, rot_theirs):
    arrays, slabs = operands(streams)
    vectors, rows, electrons = rot_mine.shape
    chips = layout.chol // 2
    total = sum(counts)
    return pl.pallas_call(
        functools.partial(bias_kernel, layout, slabs, counts),
        out_shape=[
            jax.ShapeDtypeStruct((count, chips, 2, rows, electrons), BF16) for count in counts
        ]
        + [jax.ShapeDtypeStruct((total, vectors), F32)],
        in_specs=vmem_specs(3 + len(arrays)),
        out_specs=vmem_specs(len(counts) + 1),
        scratch_shapes=[
            pltpu.VMEM((2, rows // BLOCK, total, BLOCK, electrons), BF16),
        ],
        compiler_params=params(12),
        cost_estimate=pl.CostEstimate(
            flops=2 * total * electrons**2 * (2 * chips * rows + 6 * (ITERS - 1) * electrons)
            + 4 * total * rows * electrons * (electrons + vectors * BLOCK),
            bytes_accessed=4 * (vectors + total) * rows * electrons
            + 4 * (total + 1) * 2 * chips * rows * electrons,
            transcendentals=0,
        ),
    )(rot_mine, rot_theirs, trial, *arrays)


def potential_kernel(order, fields, mine, mine_across, theirs, theirs_across, cholesky, *refs):
    bias_out, kept, *sent, weights = refs
    per_group, vectors = fields.shape
    half, piece = kept.shape[0], sent[0].shape[1]
    sums = (mine[...] + mine_across[...], theirs[...] + theirs_across[...])
    b = lax.rem(lax.axis_index("chol"), 2)
    row = lax.broadcasted_iota(jnp.int32, (per_group, vectors), 0)
    bias = jnp.zeros((per_group, vectors), F32)
    for walker in range(half):
        for part, core in zip(sums, (b, 1 - b)):
            slot = order[core * half + walker]
            bias += jnp.where(row == slot, part[walker : walker + 1, :], 0.0)
    bias = TAU_ROOT * bias
    bias_out[...] = bias
    shifted = (fields[...] - bias).astype(BF16)
    slot = jnp.zeros((per_group * BLOCK, 1), jnp.int32)
    place = lax.broadcasted_iota(jnp.int32, slot.shape, 0) // BLOCK
    for at in range(per_group):
        slot = jnp.where(place == at, order[lax.rem(at + b * half, per_group)], slot)
    tall = (per_group * BLOCK, per_group)
    rows = (lax.broadcasted_iota(jnp.int32, tall, 1) == slot).astype(BF16)
    wide = (vectors, vectors * BLOCK)
    columns = (
        lax.broadcasted_iota(jnp.int32, wide, 1) // BLOCK
        == lax.broadcasted_iota(jnp.int32, wide, 0)
    ).astype(BF16)
    spread = jnp.dot(rows, shifted, preferred_element_type=F32).astype(BF16)
    spread = jnp.dot(spread, columns, preferred_element_type=F32)
    same = lax.rem(lax.broadcasted_iota(jnp.int32, spread.shape, 0), BLOCK) == lax.rem(
        lax.broadcasted_iota(jnp.int32, spread.shape, 1), BLOCK
    )
    weights[...] = jnp.where(same, spread, 0.0).astype(BF16)
    rows, orbitals = cholesky.shape[1:]
    for at in range(0, rows, BLOCK):
        columns = cholesky[:, at : at + BLOCK, :].reshape(vectors * BLOCK, orbitals)
        result = TAU_ROOT * jnp.dot(weights[...], columns, preferred_element_type=F32)
        result = result.astype(BF16).reshape(2 * half, BLOCK, orbitals)
        kept[:, at : at + BLOCK, :] = result[:half]
        start = at % piece
        sent[at // piece][:, start : start + BLOCK, :] = result[half:]


def potential_of(order, fields, parts, cholesky):
    per_group, vectors = fields.shape
    half = per_group // 2
    _, rows, orbitals = cholesky.shape
    sent = jax.ShapeDtypeStruct((half, rows // 2, orbitals), BF16)
    return pl.pallas_call(
        potential_kernel,
        out_shape=[
            jax.ShapeDtypeStruct((per_group, vectors), F32),
            jax.ShapeDtypeStruct((half, rows, orbitals), BF16),
            sent,
            sent,
        ],
        in_specs=[pl.BlockSpec(memory_space=pltpu.SMEM)] + vmem_specs(6),
        out_specs=vmem_specs(4),
        scratch_shapes=[pltpu.VMEM((per_group * BLOCK, vectors * BLOCK), BF16)],
        compiler_params=params(12),
    )(order, fields, *parts, cholesky)


def first_kernel(sibling, parts, *refs):
    potential, fulls, (rounded, base) = refs[:parts], refs[parts:-2], refs[-2:]
    b = lax.rem(lax.axis_index("chol"), 2)
    chip = lax.axis_index("chol") // 2
    count = 0
    for full in fulls:
        for walker in range(full.shape[0]):
            rows = jnp.concatenate([part[count] for part in potential], axis=0)
            columns = full[walker].reshape(-1, full.shape[-1])
            term = jnp.dot(rows, columns, preferred_element_type=F32)
            rounded[count] = term.astype(BF16)
            own = full[walker, chip, 1 - b if sibling else b]
            base[count] = own.astype(F32) + term
            count += 1


def first_of(potential, fulls, sibling):
    half, _, orbitals = potential[0].shape
    rows, electrons = fulls[0].shape[-2:]
    shape = (half, rows, electrons)
    return pl.pallas_call(
        functools.partial(first_kernel, sibling, len(potential)),
        out_shape=[jax.ShapeDtypeStruct(shape, BF16), jax.ShapeDtypeStruct(shape, F32)],
        in_specs=vmem_specs(len(potential) + len(fulls)),
        out_specs=vmem_specs(2),
        compiler_params=params(8),
        cost_estimate=pl.CostEstimate(
            flops=2 * half * rows * orbitals * electrons,
            bytes_accessed=2 * half * orbitals * (rows + electrons),
            transcendentals=0,
        ),
    )(*potential, *fulls)


def second_kernel(layout, slabs, parts, *refs):
    potential, base, pieces = refs[:parts], refs[parts], refs[parts + 1 : -2]
    out, full = refs[-2:]
    b = lax.rem(lax.axis_index("chol"), 2)
    for block, stream in zip((b, 1 - b), slabs):
        for operand, at, walker, steps, dy in stream:
            full[walker, layout.origin(steps, dy), block] = pieces[operand][at]
    for walker in range(out.shape[0]):
        rows = jnp.concatenate([part[walker] for part in potential], axis=0)
        columns = full[walker].reshape(-1, full.shape[-1])
        term = jnp.dot(rows, columns, preferred_element_type=F32)
        out[walker] = (base[walker] + 0.5 * term).astype(BF16)


def second_of(layout, potential, base, streams):
    arrays, slabs = operands(streams)
    orbitals = potential[0].shape[2]
    half, rows, electrons = base.shape
    return pl.pallas_call(
        functools.partial(second_kernel, layout, slabs, len(potential)),
        out_shape=[
            jax.ShapeDtypeStruct((half, rows, electrons), BF16),
            jax.ShapeDtypeStruct((half, layout.chol // 2, 2, rows, electrons), BF16),
        ],
        in_specs=vmem_specs(len(potential) + 1 + len(arrays)),
        out_specs=vmem_specs(2),
        compiler_params=params(8),
        cost_estimate=pl.CostEstimate(
            flops=2 * half * rows * orbitals * electrons,
            bytes_accessed=2 * half * orbitals * (rows + 3 * electrons),
            transcendentals=0,
        ),
    )(*potential, base, *arrays)


def finish_kernel(order, potential, base, full, out, results, semaphores):
    half = base.shape[0]
    b = lax.rem(lax.axis_index("chol"), 2)
    copies = []
    for walker in range(half):
        columns = full[walker].reshape(-1, full.shape[-1])
        term = jnp.dot(potential[walker], columns, preferred_element_type=F32)
        results[walker] = (base[walker] + 0.5 * term).astype(BF16)
        copies.append(
            pltpu.make_async_copy(
                results.at[walker], out.at[order[b * half + walker]], semaphores.at[walker]
            )
        )
        copies[-1].start()
    for copy in copies:
        copy.wait()


def finish(order, potential, base, full):
    half, rows, electrons = base.shape
    orbitals = potential.shape[2]
    return pl.pallas_call(
        finish_kernel,
        out_shape=jax.ShapeDtypeStruct((2 * half, rows, electrons), BF16),
        in_specs=[pl.BlockSpec(memory_space=pltpu.SMEM)] + vmem_specs(3),
        out_specs=pl.BlockSpec(memory_space=pl.ANY),
        scratch_shapes=[
            pltpu.VMEM((half, rows, electrons), BF16),
            pltpu.SemaphoreType.DMA((half,)),
        ],
        compiler_params=params(8),
        cost_estimate=pl.CostEstimate(
            flops=2 * half * rows * orbitals * electrons,
            bytes_accessed=2 * half * orbitals * (rows + electrons),
            transcendentals=0,
        ),
    )(order, potential, base, full)


def place_kernel(order, theirs, _, out, semaphores):
    half = theirs.shape[0]
    b = lax.rem(lax.axis_index("chol"), 2)
    copies = [
        pltpu.make_async_copy(
            theirs.at[walker], out.at[order[(1 - b) * half + walker]], semaphores.at[walker]
        )
        for walker in range(half)
    ]
    for copy in copies:
        copy.start()
    for copy in copies:
        copy.wait()


def place(order, theirs, out):
    return pl.pallas_call(
        place_kernel,
        out_shape=jax.ShapeDtypeStruct(out.shape, out.dtype),
        in_specs=[pl.BlockSpec(memory_space=pltpu.SMEM)] + vmem_specs(1)
        + [pl.BlockSpec(memory_space=pl.ANY)],
        out_specs=pl.BlockSpec(memory_space=pl.ANY),
        scratch_shapes=[pltpu.SemaphoreType.DMA((theirs.shape[0],))],
        input_output_aliases={2: 0},
        compiler_params=params(4),
    )(order, theirs, out)


def split_kernel(source, walkers, *refs):
    targets, (order, picked, semaphores) = refs[:4], refs[4:]
    per_group = walkers.shape[0]
    half = per_group // 2
    share = half // 2
    group = lax.axis_index("walk")
    b = lax.rem(lax.axis_index("chol"), 2)
    stayed, arrived, sent = jnp.int32(0), jnp.int32(0), jnp.int32(0)
    for slot in range(per_group):
        local = source[group * per_group + slot] - group * per_group
        stays = ((local >= 0) & (local < per_group)).astype(jnp.int32)
        picked[jnp.where(stays == 1, jnp.minimum(stayed, half - 1), per_group)] = local
        rank = jnp.minimum(jnp.where(stays == 1, stayed, arrived), half - 1)
        core = rank // share
        order[core * half + (1 - stays) * share + rank - core * share] = jnp.int32(slot)
        stayed, arrived = stayed + stays, arrived + 1 - stays
        local = source[(1 - group) * per_group + slot] - group * per_group
        goes = ((local >= 0) & (local < per_group)).astype(jnp.int32)
        picked[jnp.where(goes == 1, half + jnp.minimum(sent, half - 1), per_group)] = local
        sent = sent + goes
    offsets = (b * share, (1 - b) * share, half + b * share, half + (1 - b) * share)
    copies = []
    for target, offset in reversed(list(zip(targets, offsets))):
        for walker in range(share):
            copies.append(
                pltpu.make_async_copy(
                    walkers.at[picked[offset + walker]],
                    target.at[walker],
                    semaphores.at[len(copies)],
                )
            )
    for copy in copies:
        copy.start()
    for copy in copies:
        copy.wait()


def split_walkers(walkers, source):
    per_group, rows, electrons = walkers.shape
    share = jax.ShapeDtypeStruct((per_group // 4, rows, electrons), walkers.dtype)
    return pl.pallas_call(
        split_kernel,
        out_shape=[share] * 4 + [jax.ShapeDtypeStruct((per_group,), jnp.int32)],
        in_specs=[pl.BlockSpec(memory_space=pltpu.SMEM), pl.BlockSpec(memory_space=pl.ANY)],
        out_specs=[pl.BlockSpec(memory_space=pl.ANY)] * 4
        + [pl.BlockSpec(memory_space=pltpu.SMEM)],
        scratch_shapes=[
            pltpu.SMEM((per_group + 1,), jnp.int32),
            pltpu.SemaphoreType.DMA((per_group,)),
        ],
        compiler_params=params(4),
    )(source, walkers)


def ranks(flags):
    count = flags.shape[-1]
    before = jnp.arange(count)[None, :] < jnp.arange(count)[:, None]
    return jnp.sum(jnp.where(before & flags[..., None, :], 1, 0), axis=-1)


def migrate(layout, walkers, source):
    per_group = walkers.shape[0]
    half = per_group // 2
    group = lax.axis_index("walk")
    if layout.walk == 2 and half % 2 == 0:
        stay, stay_sent, near, cross, order = split_walkers(walkers, source)
        count = 2 * layout.chol
        across = [(index + layout.chol) % count for index in range(count)]
        axes = ("walk", "chol")
        near = lax.ppermute(near, axes, list(enumerate(across)))
        cross = lax.ppermute(cross, axes, [(i, j ^ 1) for i, j in enumerate(across)])
        return [(stay, layout.shift(stay_sent, db=1)), (near, cross)], order
    table = source.reshape(layout.walk, per_group)
    incoming = lax.dynamic_index_in_dim(table, group, 0, keepdims=False)
    incoming_groups = incoming // per_group

    def outgoing(distance):
        row = lax.dynamic_index_in_dim(table, (group + distance) % layout.walk, 0, keepdims=False)
        local = row - group * per_group
        here = (local >= 0) & (local < per_group)
        match = here[None, :] & (ranks(here)[None, :] == jnp.arange(half)[:, None])
        return jnp.take(walkers, jnp.sum(jnp.where(match, local[None, :], 0), axis=1), axis=0)

    arrived = [outgoing(0)]
    for distance in range(1, layout.walk):
        pairs = [(g, (g + distance) % layout.walk) for g in range(layout.walk)]
        arrived.append(lax.ppermute(outgoing(distance), "walk", pairs))
    slots = jnp.arange(per_group)
    same = (incoming_groups[:, None] == incoming_groups[None, :]) & (slots[None, :] < slots[:, None])
    rank = jnp.sum(same.astype(jnp.int32), axis=1)
    distance = (group - incoming_groups) % layout.walk
    migrated = jnp.take(jnp.concatenate(arrived, axis=0), distance * half + rank, axis=0)
    b = lax.axis_index("chol") % 2
    mine = lax.dynamic_slice_in_dim(migrated, b * half, half, 0)
    theirs = lax.dynamic_slice_in_dim(migrated, (1 - b) * half, half, 0)
    theirs = layout.shift(theirs, db=1)
    share = half // 2
    shares = [(mine[:share], theirs[:share]), (mine[share:], theirs[share:])]
    return shares, slots.astype(jnp.int32)


def shards(layout, walkers, trial, cholesky, rotated, fields, source):
    b = lax.axis_index("chol") % 2
    shares, order = migrate(layout, walkers, source)
    sizes = [own.shape[0] for own, _ in shares]
    chunks = [
        jnp.concatenate([jnp.where(b == 0, own, other), jnp.where(b == 0, other, own)])
        for own, other in shares
    ]
    streams = [Stream(layout, chunk) for chunk in chunks]
    rot_theirs = layout.shift(rotated, db=1)
    turned = transposed(lax.all_gather(trial, "chol", axis=0, tiled=True))
    moved = lax.optimization_barrier([stream.moves() for stream in reversed(streams)])
    for stream, arrays in zip(reversed(streams), moved):
        stream.accept(arrays)
    for _ in range(layout.z - 2):
        for stream in streams:
            stream.advance()
    turned, rot_theirs = streams[0].advance((turned, rot_theirs))
    streams[1].advance()
    *fulls, total = bias_of(layout, streams, sizes, turned, rotated, rot_theirs)
    bits = [2] + [4 << at for at in range(layout.z.bit_length() - 1)]
    while len(bits) > 1:
        first, second, *rest = bits if len(bits) % 2 else (bits[0], 0, *bits[1:])
        sums = [total + layout.flip(total, first)]
        if second:
            sums.append(layout.flip(total, second) + layout.flip(total, first + second))
        total = sum(sums[1:], sums[0])
        bits = rest
    parts = [total] + [layout.flip(total, mask) for mask in (bits[0], 1, bits[0] + 1)]
    force_bias, kept, *sent = potential_of(order, fields, parts, cholesky)
    received = [layout.shift(part, db=1) for part in sent]

    rounded, base = first_of([kept], fulls, 0)
    rounded_theirs, base_theirs = first_of(received, fulls, 1)
    streams = [Stream(layout, rounded), Stream(layout, rounded_theirs)]
    for _ in range(layout.z):
        for stream in streams:
            stream.advance()
    sent, full = second_of(layout, received, base_theirs, streams)
    theirs = layout.shift(sent, db=1)
    return place(order, theirs, finish(order, kept, base, full)), force_bias


def solution(mesh):
    in_specs = (
        P("walk", "chol", None),
        P("chol", None),
        P(None, "chol", None),
        P(None, "chol", None),
        P("walk", None),
        P(),
    )
    out_specs = (P("walk", "chol", None), P("walk", None))
    layout = Layout(mesh.shape["walk"], mesh.shape["chol"])
    return jax.shard_map(
        functools.partial(shards, layout),
        mesh=mesh,
        in_specs=in_specs,
        out_specs=out_specs,
        check_vma=False,
    )
```

```python
import functools

import jax
import jax.numpy as jnp
from jax import lax
from jax.experimental import pallas as pl
from jax.experimental.pallas import tpu as pltpu
from jax.sharding import PartitionSpec as P

ITERS = 3
TAU_ROOT = 0.1
BLOCK = 16
HIGHEST = lax.Precision.HIGHEST
MIB = 1024 * 1024

F32 = jnp.float32
BF16 = jnp.bfloat16


def params(mebibytes):
    return pltpu.CompilerParams(vmem_limit_bytes=mebibytes * MIB)


def vmem_specs(count):
    return [pl.BlockSpec(memory_space=pltpu.VMEM)] * count


class Layout:
    def __init__(self, walk_size, chol_size):
        self.walk = walk_size
        self.chol = chol_size
        self.z = chol_size // 4

    def shift(self, array, dz=0, dy=0, db=0):
        pairs = []
        for index in range(self.chol):
            z, y, b = index // 4, (index // 2) % 2, index % 2
            target = (((z + dz) % self.z) * 2 + (y ^ dy)) * 2 + (b ^ db)
            pairs.append((index, target))
        return lax.ppermute(array, "chol", pairs)

    def flip(self, array, mask):
        return lax.ppermute(array, "chol", [(i, i ^ mask) for i in range(self.chol)])

    def step(self, array):
        ring = [*range(0, self.z, 2), *reversed(range(1, self.z, 2))]
        target = {z: ring[(at + 1) % self.z] for at, z in enumerate(ring)}
        pairs = [(index, target[index // 4] * 4 + index % 4) for index in range(self.chol)]
        return lax.ppermute(array, "chol", pairs)

    def origin(self, steps, dy):
        index = lax.axis_index("chol")
        z, y = index // 4, lax.rem(index // 2, 2)
        at = jnp.where(lax.rem(z, 2) == 0, z // 2, self.z - (z + 1) // 2)
        at = lax.rem(at + (self.z - steps), self.z)
        z = jnp.where(2 * at < self.z, 2 * at, 2 * (self.z - at) - 1)
        return z * 2 + (y + dy - 2 * y * dy)


class Stream:
    def __init__(self, layout, piece):
        self.layout = layout
        self.ring = [piece]
        self.across = []
        self.last = []

    def moves(self):
        latest = self.ring[-1]
        if len(self.ring) < self.layout.z:
            return [self.layout.shift(latest, dy=1), self.layout.step(latest)]
        half = (latest.shape[0] + 1) // 2
        return [
            self.layout.shift(latest[:half], dy=1),
            self.layout.step(self.across[-1][half:]),
        ]

    def accept(self, moved):
        if len(self.ring) < self.layout.z:
            self.across.append(moved[0])
            self.ring.append(moved[1])
        else:
            self.last = moved

    def advance(self, anchors=()):
        moved = self.moves()
        if anchors or len(self.ring) < self.layout.z:
            anchors, moved = lax.optimization_barrier((anchors, moved))
        self.accept(moved)
        return anchors

    def pieces(self):
        ring = [(array, 0, steps, 0) for steps, array in enumerate(self.ring)]
        across = [(array, 0, steps, 1) for steps, array in enumerate(self.across)]
        lower, upper = self.last
        steps = self.layout.z - 1
        return ring + across + [(lower, 0, steps, 1), (upper, lower.shape[0], steps, 1)]


def operands(streams):
    arrays, slabs = [], []
    for stream in streams:
        slabs.append([])
        for array, first, steps, dy in stream.pieces():
            for at in range(array.shape[0]):
                slabs[-1].append((len(arrays), at, first + at, steps, dy))
            arrays.append(array)
    return arrays, slabs


def product(left, right):
    high, right_high = left.astype(BF16), right.astype(BF16)
    low = (left - high.astype(F32)).astype(BF16)
    right_low = (right - right_high.astype(F32)).astype(BF16)
    return jnp.dot(
        jnp.concatenate([high, high, low], axis=1),
        jnp.concatenate([right_high, right_low, right_high], axis=0),
        preferred_element_type=F32,
    )


def newton_inverses(matrices):
    shape = matrices[0].shape
    same = lax.broadcasted_iota(jnp.int32, shape, 0) == lax.broadcasted_iota(jnp.int32, shape, 1)
    twice = jnp.where(same, 2.0, 0.0).astype(F32)
    estimates = [twice - matrix for matrix in matrices]
    for _ in range(ITERS - 1):
        steps = [twice - product(a, x) for a, x in zip(matrices, estimates)]
        estimates = [product(x, step) for x, step in zip(estimates, steps)]
    return estimates


def inverse_kernel(layout, slabs, counts, early, late, *refs):
    fulls, (out, buffer, turned) = refs[-3 - len(counts) : -3], refs[-3:]
    pieces = refs[: -3 - len(counts)]
    electrons = early.shape[-1]
    b = lax.rem(lax.axis_index("chol"), 2)

    theirs = [(early, at) for at in range(early.shape[0])] + [(late, 0)]
    trial = [slab for slab in slabs[0] if slab[2] == 2 * counts[0]]
    for (operand, at, _, steps, dy), (part, place) in zip(trial, theirs):
        origin = layout.origin(steps, dy)
        buffer[origin, b] = pieces[operand][at]
        buffer[origin, 1 - b] = part[place]
    turned[...] = buffer[...].reshape(-1, electrons).T

    matrices = []
    for full, count, stream in zip(fulls, counts, slabs):
        for operand, at, slab, steps, dy in stream:
            if slab < 2 * count:
                full[slab % count, layout.origin(steps, dy), slab // count] = pieces[operand][at]
        for walker in range(count):
            columns = full[walker].reshape(-1, electrons)
            matrices.append(jnp.dot(turned[...], columns, preferred_element_type=F32))
    for number, inverse in enumerate(newton_inverses(matrices)):
        out[number] = inverse.astype(BF16)


def inverses_of(layout, streams, counts, early, late):
    arrays, slabs = operands(streams)
    _, rows, electrons = early.shape
    chips = layout.chol // 2
    total = sum(counts)
    return pl.pallas_call(
        functools.partial(inverse_kernel, layout, slabs, counts),
        out_shape=[
            jax.ShapeDtypeStruct((count, chips, 2, rows, electrons), BF16) for count in counts
        ]
        + [jax.ShapeDtypeStruct((total, electrons, electrons), BF16)],
        in_specs=vmem_specs(2 + len(arrays)),
        out_specs=vmem_specs(len(counts) + 1),
        scratch_shapes=[
            pltpu.VMEM((chips, 2, rows, electrons), BF16),
            pltpu.VMEM((electrons, 2 * chips * rows), BF16),
        ],
        compiler_params=params(8),
        cost_estimate=pl.CostEstimate(
            flops=2 * total * electrons**2 * (2 * chips * rows + 6 * (ITERS - 1) * electrons),
            bytes_accessed=4 * (total + 1) * 2 * chips * rows * electrons,
            transcendentals=0,
        ),
    )(early, late, *arrays)


def bias_kernel(counts, rot_mine, rot_theirs, inverses, *refs):
    fulls, (out, greens) = refs[:-2], refs[-2:]
    vectors, rows, electrons = rot_mine.shape
    index = lax.axis_index("chol")
    chip, b = index // 2, lax.rem(index, 2)
    walkers = [(full, at) for full, count in zip(fulls, counts) for at in range(count)]
    for number, (full, walker) in enumerate(walkers):
        both = full[walker, chip].reshape(2 * rows, electrons)
        green = jnp.dot(both, inverses[number], preferred_element_type=F32).astype(BF16)
        greens[:, :, number] = green.reshape(2, rows // BLOCK, BLOCK, electrons)
    width = len(walkers) * BLOCK
    total = jnp.zeros((vectors * BLOCK, width), F32)
    for half, rot in ((b, rot_mine), (1 - b, rot_theirs)):
        for block in range(rows // BLOCK):
            total += lax.dot_general(
                rot[:, block * BLOCK : (block + 1) * BLOCK, :].reshape(vectors * BLOCK, electrons),
                greens[half, block].reshape(width, electrons),
                (((1,), (1,)), ((), ())),
                preferred_element_type=F32,
            )
    same = lax.rem(lax.broadcasted_iota(jnp.int32, total.shape, 0), BLOCK) == lax.rem(
        lax.broadcasted_iota(jnp.int32, total.shape, 1), BLOCK
    )
    summed = jnp.sum(jnp.where(same, total, 0.0).reshape(vectors, BLOCK, width), axis=1)
    shape = (len(walkers), width)
    pick = (
        lax.broadcasted_iota(jnp.int32, shape, 1) // BLOCK
        == lax.broadcasted_iota(jnp.int32, shape, 0)
    ).astype(F32)
    out[...] = lax.dot_general(
        pick, summed, (((1,), (1,)), ((), ())), precision=HIGHEST, preferred_element_type=F32
    )


def bias_of(fulls, inverses, rot_mine, rot_theirs):
    vectors, rows, electrons = rot_mine.shape
    counts = [full.shape[0] for full in fulls]
    total = sum(counts)
    return pl.pallas_call(
        functools.partial(bias_kernel, counts),
        out_shape=jax.ShapeDtypeStruct((total, vectors), F32),
        in_specs=vmem_specs(3 + len(fulls)),
        out_specs=pl.BlockSpec(memory_space=pltpu.VMEM),
        scratch_shapes=[pltpu.VMEM((2, rows // BLOCK, total, BLOCK, electrons), BF16)],
        compiler_params=params(8),
        cost_estimate=pl.CostEstimate(
            flops=4 * total * rows * electrons * (electrons + vectors * BLOCK),
            bytes_accessed=4 * (vectors + total) * rows * electrons,
            transcendentals=0,
        ),
    )(rot_mine, rot_theirs, inverses, *fulls)


def potential_kernel(order, fields, mine, mine_across, theirs, theirs_across, cholesky, *refs):
    bias_out, kept, *sent, weights = refs
    per_group, vectors = fields.shape
    half, piece = kept.shape[0], sent[0].shape[1]
    sums = (mine[...] + mine_across[...], theirs[...] + theirs_across[...])
    b = lax.rem(lax.axis_index("chol"), 2)
    row = lax.broadcasted_iota(jnp.int32, (per_group, vectors), 0)
    bias = jnp.zeros((per_group, vectors), F32)
    for walker in range(half):
        for part, core in zip(sums, (b, 1 - b)):
            slot = order[core * half + walker]
            bias += jnp.where(row == slot, part[walker : walker + 1, :], 0.0)
    bias = TAU_ROOT * bias
    bias_out[...] = bias
    shifted = (fields[...] - bias).astype(BF16)
    slot = jnp.zeros((per_group * BLOCK, 1), jnp.int32)
    place = lax.broadcasted_iota(jnp.int32, slot.shape, 0) // BLOCK
    for at in range(per_group):
        slot = jnp.where(place == at, order[lax.rem(at + b * half, per_group)], slot)
    tall = (per_group * BLOCK, per_group)
    rows = (lax.broadcasted_iota(jnp.int32, tall, 1) == slot).astype(BF16)
    wide = (vectors, vectors * BLOCK)
    columns = (
        lax.broadcasted_iota(jnp.int32, wide, 1) // BLOCK
        == lax.broadcasted_iota(jnp.int32, wide, 0)
    ).astype(BF16)
    spread = jnp.dot(rows, shifted, preferred_element_type=F32).astype(BF16)
    spread = jnp.dot(spread, columns, preferred_element_type=F32)
    same = lax.rem(lax.broadcasted_iota(jnp.int32, spread.shape, 0), BLOCK) == lax.rem(
        lax.broadcasted_iota(jnp.int32, spread.shape, 1), BLOCK
    )
    weights[...] = jnp.where(same, spread, 0.0).astype(BF16)
    rows, orbitals = cholesky.shape[1:]
    for at in range(0, rows, BLOCK):
        columns = cholesky[:, at : at + BLOCK, :].reshape(vectors * BLOCK, orbitals)
        result = TAU_ROOT * jnp.dot(weights[...], columns, preferred_element_type=F32)
        result = result.astype(BF16).reshape(2 * half, BLOCK, orbitals)
        kept[:, at : at + BLOCK, :] = result[:half]
        start = at % piece
        sent[at // piece][:, start : start + BLOCK, :] = result[half:]


def potential_of(order, fields, parts, cholesky):
    per_group, vectors = fields.shape
    half = per_group // 2
    _, rows, orbitals = cholesky.shape
    sent = jax.ShapeDtypeStruct((half, rows // 2, orbitals), BF16)
    return pl.pallas_call(
        potential_kernel,
        out_shape=[
            jax.ShapeDtypeStruct((per_group, vectors), F32),
            jax.ShapeDtypeStruct((half, rows, orbitals), BF16),
            sent,
            sent,
        ],
        in_specs=[pl.BlockSpec(memory_space=pltpu.SMEM)] + vmem_specs(6),
        out_specs=vmem_specs(4),
        scratch_shapes=[pltpu.VMEM((per_group * BLOCK, vectors * BLOCK), BF16)],
        compiler_params=params(12),
    )(order, fields, *parts, cholesky)


def first_kernel(sibling, parts, *refs):
    potential, fulls, (rounded, base) = refs[:parts], refs[parts:-2], refs[-2:]
    b = lax.rem(lax.axis_index("chol"), 2)
    chip = lax.axis_index("chol") // 2
    count = 0
    for full in fulls:
        for walker in range(full.shape[0]):
            rows = jnp.concatenate([part[count] for part in potential], axis=0)
            columns = full[walker].reshape(-1, full.shape[-1])
            term = jnp.dot(rows, columns, preferred_element_type=F32)
            rounded[count] = term.astype(BF16)
            own = full[walker, chip, 1 - b if sibling else b]
            base[count] = own.astype(F32) + term
            count += 1


def first_of(potential, fulls, sibling):
    half, _, orbitals = potential[0].shape
    rows, electrons = fulls[0].shape[-2:]
    shape = (half, rows, electrons)
    return pl.pallas_call(
        functools.partial(first_kernel, sibling, len(potential)),
        out_shape=[jax.ShapeDtypeStruct(shape, BF16), jax.ShapeDtypeStruct(shape, F32)],
        in_specs=vmem_specs(len(potential) + len(fulls)),
        out_specs=vmem_specs(2),
        compiler_params=params(8),
        cost_estimate=pl.CostEstimate(
            flops=2 * half * rows * orbitals * electrons,
            bytes_accessed=2 * half * orbitals * (rows + electrons),
            transcendentals=0,
        ),
    )(*potential, *fulls)


def second_kernel(layout, slabs, parts, *refs):
    potential, base, pieces = refs[:parts], refs[parts], refs[parts + 1 : -2]
    out, full = refs[-2:]
    b = lax.rem(lax.axis_index("chol"), 2)
    for block, stream in zip((b, 1 - b), slabs):
        for operand, at, walker, steps, dy in stream:
            full[walker, layout.origin(steps, dy), block] = pieces[operand][at]
    for walker in range(out.shape[0]):
        rows = jnp.concatenate([part[walker] for part in potential], axis=0)
        columns = full[walker].reshape(-1, full.shape[-1])
        term = jnp.dot(rows, columns, preferred_element_type=F32)
        out[walker] = (base[walker] + 0.5 * term).astype(BF16)


def second_of(layout, potential, base, streams):
    arrays, slabs = operands(streams)
    orbitals = potential[0].shape[2]
    half, rows, electrons = base.shape
    return pl.pallas_call(
        functools.partial(second_kernel, layout, slabs, len(potential)),
        out_shape=[
            jax.ShapeDtypeStruct((half, rows, electrons), BF16),
            jax.ShapeDtypeStruct((half, layout.chol // 2, 2, rows, electrons), BF16),
        ],
        in_specs=vmem_specs(len(potential) + 1 + len(arrays)),
        out_specs=vmem_specs(2),
        compiler_params=params(8),
        cost_estimate=pl.CostEstimate(
            flops=2 * half * rows * orbitals * electrons,
            bytes_accessed=2 * half * orbitals * (rows + 3 * electrons),
            transcendentals=0,
        ),
    )(*potential, base, *arrays)


def finish_kernel(order, potential, base, full, out, results, semaphores):
    half = base.shape[0]
    b = lax.rem(lax.axis_index("chol"), 2)
    copies = []
    for walker in range(half):
        columns = full[walker].reshape(-1, full.shape[-1])
        term = jnp.dot(potential[walker], columns, preferred_element_type=F32)
        results[walker] = (base[walker] + 0.5 * term).astype(BF16)
        copies.append(
            pltpu.make_async_copy(
                results.at[walker], out.at[order[b * half + walker]], semaphores.at[walker]
            )
        )
        copies[-1].start()
    for copy in copies:
        copy.wait()


def finish(order, potential, base, full):
    half, rows, electrons = base.shape
    orbitals = potential.shape[2]
    return pl.pallas_call(
        finish_kernel,
        out_shape=jax.ShapeDtypeStruct((2 * half, rows, electrons), BF16),
        in_specs=[pl.BlockSpec(memory_space=pltpu.SMEM)] + vmem_specs(3),
        out_specs=pl.BlockSpec(memory_space=pl.ANY),
        scratch_shapes=[
            pltpu.VMEM((half, rows, electrons), BF16),
            pltpu.SemaphoreType.DMA((half,)),
        ],
        compiler_params=params(8),
        cost_estimate=pl.CostEstimate(
            flops=2 * half * rows * orbitals * electrons,
            bytes_accessed=2 * half * orbitals * (rows + electrons),
            transcendentals=0,
        ),
    )(order, potential, base, full)


def place_kernel(order, theirs, _, out, semaphores):
    half = theirs.shape[0]
    b = lax.rem(lax.axis_index("chol"), 2)
    copies = [
        pltpu.make_async_copy(
            theirs.at[walker], out.at[order[(1 - b) * half + walker]], semaphores.at[walker]
        )
        for walker in range(half)
    ]
    for copy in copies:
        copy.start()
    for copy in copies:
        copy.wait()


def place(order, theirs, out):
    return pl.pallas_call(
        place_kernel,
        out_shape=jax.ShapeDtypeStruct(out.shape, out.dtype),
        in_specs=[pl.BlockSpec(memory_space=pltpu.SMEM)] + vmem_specs(1)
        + [pl.BlockSpec(memory_space=pl.ANY)],
        out_specs=pl.BlockSpec(memory_space=pl.ANY),
        scratch_shapes=[pltpu.SemaphoreType.DMA((theirs.shape[0],))],
        input_output_aliases={2: 0},
        compiler_params=params(4),
    )(order, theirs, out)


def split_kernel(source, walkers, *refs):
    targets, (order, picked, semaphores) = refs[:4], refs[4:]
    per_group = walkers.shape[0]
    half = per_group // 2
    share = half // 2
    group = lax.axis_index("walk")
    b = lax.rem(lax.axis_index("chol"), 2)
    stayed, arrived, sent = jnp.int32(0), jnp.int32(0), jnp.int32(0)
    for slot in range(per_group):
        local = source[group * per_group + slot] - group * per_group
        stays = ((local >= 0) & (local < per_group)).astype(jnp.int32)
        picked[jnp.where(stays == 1, jnp.minimum(stayed, half - 1), per_group)] = local
        rank = jnp.minimum(jnp.where(stays == 1, stayed, arrived), half - 1)
        core = rank // share
        order[core * half + (1 - stays) * share + rank - core * share] = jnp.int32(slot)
        stayed, arrived = stayed + stays, arrived + 1 - stays
        local = source[(1 - group) * per_group + slot] - group * per_group
        goes = ((local >= 0) & (local < per_group)).astype(jnp.int32)
        picked[jnp.where(goes == 1, half + jnp.minimum(sent, half - 1), per_group)] = local
        sent = sent + goes
    offsets = (b * share, (1 - b) * share, half + b * share, half + (1 - b) * share)
    copies = []
    for target, offset in reversed(list(zip(targets, offsets))):
        for walker in range(share):
            copies.append(
                pltpu.make_async_copy(
                    walkers.at[picked[offset + walker]],
                    target.at[walker],
                    semaphores.at[len(copies)],
                )
            )
    for copy in copies:
        copy.start()
    for copy in copies:
        copy.wait()


def split_walkers(walkers, source):
    per_group, rows, electrons = walkers.shape
    share = jax.ShapeDtypeStruct((per_group // 4, rows, electrons), walkers.dtype)
    return pl.pallas_call(
        split_kernel,
        out_shape=[share] * 4 + [jax.ShapeDtypeStruct((per_group,), jnp.int32)],
        in_specs=[pl.BlockSpec(memory_space=pltpu.SMEM), pl.BlockSpec(memory_space=pl.ANY)],
        out_specs=[pl.BlockSpec(memory_space=pl.ANY)] * 4
        + [pl.BlockSpec(memory_space=pltpu.SMEM)],
        scratch_shapes=[
            pltpu.SMEM((per_group + 1,), jnp.int32),
            pltpu.SemaphoreType.DMA((per_group,)),
        ],
        compiler_params=params(4),
    )(source, walkers)


def ranks(flags):
    count = flags.shape[-1]
    before = jnp.arange(count)[None, :] < jnp.arange(count)[:, None]
    return jnp.sum(jnp.where(before & flags[..., None, :], 1, 0), axis=-1)


def migrate(layout, walkers, source):
    per_group = walkers.shape[0]
    half = per_group // 2
    group = lax.axis_index("walk")
    if layout.walk == 2 and half % 2 == 0:
        stay, stay_sent, near, cross, order = split_walkers(walkers, source)
        count = 2 * layout.chol
        across = [(index + layout.chol) % count for index in range(count)]
        axes = ("walk", "chol")
        near = lax.ppermute(near, axes, list(enumerate(across)))
        cross = lax.ppermute(cross, axes, [(i, j ^ 1) for i, j in enumerate(across)])
        return [(stay, layout.shift(stay_sent, db=1)), (near, cross)], order
    table = source.reshape(layout.walk, per_group)
    incoming = lax.dynamic_index_in_dim(table, group, 0, keepdims=False)
    incoming_groups = incoming // per_group

    def outgoing(distance):
        row = lax.dynamic_index_in_dim(table, (group + distance) % layout.walk, 0, keepdims=False)
        local = row - group * per_group
        here = (local >= 0) & (local < per_group)
        match = here[None, :] & (ranks(here)[None, :] == jnp.arange(half)[:, None])
        return jnp.take(walkers, jnp.sum(jnp.where(match, local[None, :], 0), axis=1), axis=0)

    arrived = [outgoing(0)]
    for distance in range(1, layout.walk):
        pairs = [(g, (g + distance) % layout.walk) for g in range(layout.walk)]
        arrived.append(lax.ppermute(outgoing(distance), "walk", pairs))
    slots = jnp.arange(per_group)
    same = (incoming_groups[:, None] == incoming_groups[None, :]) & (slots[None, :] < slots[:, None])
    rank = jnp.sum(same.astype(jnp.int32), axis=1)
    distance = (group - incoming_groups) % layout.walk
    migrated = jnp.take(jnp.concatenate(arrived, axis=0), distance * half + rank, axis=0)
    b = lax.axis_index("chol") % 2
    mine = lax.dynamic_slice_in_dim(migrated, b * half, half, 0)
    theirs = lax.dynamic_slice_in_dim(migrated, (1 - b) * half, half, 0)
    theirs = layout.shift(theirs, db=1)
    share = half // 2
    shares = [(mine[:share], theirs[:share]), (mine[share:], theirs[share:])]
    return shares, slots.astype(jnp.int32)


def shards(layout, walkers, trial, cholesky, rotated, fields, source):
    b = lax.axis_index("chol") % 2
    shares, order = migrate(layout, walkers, source)
    sizes = [own.shape[0] for own, _ in shares]
    chunks = [
        jnp.concatenate([jnp.where(b == 0, own, other), jnp.where(b == 0, other, own), *extra])
        for (own, other), extra in zip(shares, ([trial[None]], []))
    ]
    streams = [Stream(layout, chunk) for chunk in chunks]
    rot_theirs = layout.shift(rotated, db=1)
    moved = lax.optimization_barrier([stream.moves() for stream in streams])
    for stream, arrays in zip(streams, moved):
        stream.accept(arrays)
    for _ in range(layout.z - 2):
        for stream in streams:
            stream.advance()
    slabs = [array[-1:] for array in (*streams[0].ring, *streams[0].across)]
    early = layout.shift(jnp.concatenate(slabs), db=1)
    late = layout.shift(early[layout.z - 1 : layout.z], dy=1)
    early, rot_theirs = streams[0].advance((early, rot_theirs))
    streams[1].advance()
    *fulls, inverses = inverses_of(layout, streams, sizes, early, late)
    total = bias_of(fulls, inverses, rotated, rot_theirs)
    bits = [2] + [4 << at for at in range(layout.z.bit_length() - 1)]
    while len(bits) > 1:
        first, second, *rest = bits if len(bits) % 2 else (bits[0], 0, *bits[1:])
        sums = [total + layout.flip(total, first)]
        if second:
            sums.append(layout.flip(total, second) + layout.flip(total, first + second))
        total = sum(sums[1:], sums[0])
        bits = rest
    parts = [total] + [layout.flip(total, mask) for mask in (bits[0], 1, bits[0] + 1)]
    force_bias, kept, *sent = potential_of(order, fields, parts, cholesky)
    received = [layout.shift(part, db=1) for part in sent]

    rounded, base = first_of([kept], fulls, 0)
    rounded_theirs, base_theirs = first_of(received, fulls, 1)
    streams = [Stream(layout, rounded), Stream(layout, rounded_theirs)]
    for _ in range(layout.z):
        for stream in streams:
            stream.advance()
    sent, full = second_of(layout, received, base_theirs, streams)
    theirs = layout.shift(sent, db=1)
    return place(order, theirs, finish(order, kept, base, full)), force_bias


def solution(mesh):
    in_specs = (
        P("walk", "chol", None),
        P("chol", None),
        P(None, "chol", None),
        P(None, "chol", None),
        P("walk", None),
        P(),
    )
    out_specs = (P("walk", "chol", None), P("walk", None))
    layout = Layout(mesh.shape["walk"], mesh.shape["chol"])
    return jax.shard_map(
        functools.partial(shards, layout),
        mesh=mesh,
        in_specs=in_specs,
        out_specs=out_specs,
        check_vma=False,
    )
```

```python
import functools

import jax
import jax.numpy as jnp
from jax import lax
from jax.experimental import pallas as pl
from jax.experimental.pallas import tpu as pltpu
from jax.sharding import PartitionSpec as P

ITERS = 3
TAU_ROOT = 0.1
BLOCK = 16
HIGHEST = lax.Precision.HIGHEST
MIB = 1024 * 1024

F32 = jnp.float32
BF16 = jnp.bfloat16


def params(mebibytes):
    return pltpu.CompilerParams(vmem_limit_bytes=mebibytes * MIB)


def vmem_specs(count):
    return [pl.BlockSpec(memory_space=pltpu.VMEM)] * count


class Layout:
    def __init__(self, walk_size, chol_size):
        self.walk = walk_size
        self.chol = chol_size
        self.z = chol_size // 4

    def shift(self, array, dz=0, dy=0, db=0):
        pairs = []
        for index in range(self.chol):
            z, y, b = index // 4, (index // 2) % 2, index % 2
            target = (((z + dz) % self.z) * 2 + (y ^ dy)) * 2 + (b ^ db)
            pairs.append((index, target))
        return lax.ppermute(array, "chol", pairs)

    def flip(self, array, mask):
        return lax.ppermute(array, "chol", [(i, i ^ mask) for i in range(self.chol)])

    def step(self, array):
        ring = [*range(0, self.z, 2), *reversed(range(1, self.z, 2))]
        target = {z: ring[(at + 1) % self.z] for at, z in enumerate(ring)}
        pairs = [(index, target[index // 4] * 4 + index % 4) for index in range(self.chol)]
        return lax.ppermute(array, "chol", pairs)

    def origin(self, steps, dy):
        index = lax.axis_index("chol")
        z, y = index // 4, lax.rem(index // 2, 2)
        at = jnp.where(lax.rem(z, 2) == 0, z // 2, self.z - (z + 1) // 2)
        at = lax.rem(at + (self.z - steps), self.z)
        z = jnp.where(2 * at < self.z, 2 * at, 2 * (self.z - at) - 1)
        return z * 2 + (y + dy - 2 * y * dy)


class Stream:
    def __init__(self, layout, piece):
        self.layout = layout
        self.ring = [piece]
        self.across = []
        self.last = []

    def moves(self):
        latest = self.ring[-1]
        if len(self.ring) < self.layout.z:
            return [self.layout.shift(latest, dy=1), self.layout.step(latest)]
        half = (latest.shape[0] + 1) // 2
        return [
            self.layout.shift(latest[:half], dy=1),
            self.layout.step(self.across[-1][half:]),
        ]

    def accept(self, moved):
        if len(self.ring) < self.layout.z:
            self.across.append(moved[0])
            self.ring.append(moved[1])
        else:
            self.last = moved

    def advance(self, anchors=()):
        moved = self.moves()
        if anchors or len(self.ring) < self.layout.z:
            anchors, moved = lax.optimization_barrier((anchors, moved))
        self.accept(moved)
        return anchors

    def pieces(self):
        ring = [(array, 0, steps, 0) for steps, array in enumerate(self.ring)]
        across = [(array, 0, steps, 1) for steps, array in enumerate(self.across)]
        lower, upper = self.last
        steps = self.layout.z - 1
        return ring + across + [(lower, 0, steps, 1), (upper, lower.shape[0], steps, 1)]


def operands(streams):
    arrays, slabs = [], []
    for stream in streams:
        slabs.append([])
        for array, first, steps, dy in stream.pieces():
            for at in range(array.shape[0]):
                slabs[-1].append((len(arrays), at, first + at, steps, dy))
            arrays.append(array)
    return arrays, slabs


def product(left, right):
    high, right_high = left.astype(BF16), right.astype(BF16)
    low = (left - high.astype(F32)).astype(BF16)
    right_low = (right - right_high.astype(F32)).astype(BF16)
    return jnp.dot(
        jnp.concatenate([high, high, low], axis=1),
        jnp.concatenate([right_high, right_low, right_high], axis=0),
        preferred_element_type=F32,
    )


def newton_inverses(matrices):
    shape = matrices[0].shape
    same = lax.broadcasted_iota(jnp.int32, shape, 0) == lax.broadcasted_iota(jnp.int32, shape, 1)
    twice = jnp.where(same, 2.0, 0.0).astype(F32)
    estimates = [twice - matrix for matrix in matrices]
    for _ in range(ITERS - 1):
        steps = [twice - product(a, x) for a, x in zip(matrices, estimates)]
        estimates = [product(x, step) for x, step in zip(estimates, steps)]
    return estimates


def inverse_kernel(layout, slabs, counts, *refs):
    streams = len(counts)
    early, late, refs = refs[:streams], refs[streams : 2 * streams], refs[2 * streams :]
    fulls, (out, buffer, turned) = refs[-3 - streams : -3], refs[-3:]
    pieces = refs[: -3 - streams]
    rows, electrons = early[0].shape[1:]
    b = lax.rem(lax.axis_index("chol"), 2)

    for half, stream in enumerate(slabs):
        place = slice(half * rows, (half + 1) * rows)
        theirs = [(early[half], at) for at in range(early[half].shape[0])] + [(late[half], 0)]
        trial = [slab for slab in stream if slab[2] == 4 * counts[half]]
        for (operand, at, _, steps, dy), (part, number) in zip(trial, theirs):
            origin = layout.origin(steps, dy)
            buffer[origin, b, place] = pieces[operand][at]
            buffer[origin, 1 - b, place] = part[number]
    turned[...] = buffer[...].reshape(-1, electrons).T

    matrices = []
    for full, count, stream in zip(fulls, counts, slabs):
        for operand, at, slab, steps, dy in stream:
            if slab < 4 * count:
                block, walker, half = slab // (2 * count), slab // 2 % count, slab % 2
                place = slice(half * rows, (half + 1) * rows)
                full[walker, layout.origin(steps, dy), block, place] = pieces[operand][at]
        for walker in range(count):
            columns = full[walker].reshape(-1, electrons)
            matrices.append(jnp.dot(turned[...], columns, preferred_element_type=F32))
    for number, inverse in enumerate(newton_inverses(matrices)):
        out[number] = inverse.astype(BF16)


def inverses_of(layout, streams, counts, early, late):
    arrays, slabs = operands(streams)
    _, rows, electrons = early[0].shape
    rows = 2 * rows
    chips = layout.chol // 2
    total = sum(counts)
    return pl.pallas_call(
        functools.partial(inverse_kernel, layout, slabs, counts),
        out_shape=[
            jax.ShapeDtypeStruct((count, chips, 2, rows, electrons), BF16) for count in counts
        ]
        + [jax.ShapeDtypeStruct((total, electrons, electrons), BF16)],
        in_specs=vmem_specs(2 * len(counts) + len(arrays)),
        out_specs=vmem_specs(len(counts) + 1),
        scratch_shapes=[
            pltpu.VMEM((chips, 2, rows, electrons), BF16),
            pltpu.VMEM((electrons, 2 * chips * rows), BF16),
        ],
        compiler_params=params(8),
        cost_estimate=pl.CostEstimate(
            flops=2 * total * electrons**2 * (2 * chips * rows + 6 * (ITERS - 1) * electrons),
            bytes_accessed=4 * (total + 1) * 2 * chips * rows * electrons,
            transcendentals=0,
        ),
    )(*early, *late, *arrays)


def bias_kernel(counts, rot_mine, rot_theirs, inverses, *refs):
    fulls, (out, greens) = refs[:-2], refs[-2:]
    vectors, rows, electrons = rot_mine.shape
    index = lax.axis_index("chol")
    chip, b = index // 2, lax.rem(index, 2)
    walkers = [(full, at) for full, count in zip(fulls, counts) for at in range(count)]
    for number, (full, walker) in enumerate(walkers):
        both = full[walker, chip].reshape(2 * rows, electrons)
        green = jnp.dot(both, inverses[number], preferred_element_type=F32).astype(BF16)
        greens[:, :, number] = green.reshape(2, rows // BLOCK, BLOCK, electrons)
    width = len(walkers) * BLOCK
    total = jnp.zeros((vectors * BLOCK, width), F32)
    for half, rot in ((b, rot_mine), (1 - b, rot_theirs)):
        for block in range(rows // BLOCK):
            total += lax.dot_general(
                rot[:, block * BLOCK : (block + 1) * BLOCK, :].reshape(vectors * BLOCK, electrons),
                greens[half, block].reshape(width, electrons),
                (((1,), (1,)), ((), ())),
                preferred_element_type=F32,
            )
    same = lax.rem(lax.broadcasted_iota(jnp.int32, total.shape, 0), BLOCK) == lax.rem(
        lax.broadcasted_iota(jnp.int32, total.shape, 1), BLOCK
    )
    summed = jnp.sum(jnp.where(same, total, 0.0).reshape(vectors, BLOCK, width), axis=1)
    shape = (len(walkers), width)
    pick = (
        lax.broadcasted_iota(jnp.int32, shape, 1) // BLOCK
        == lax.broadcasted_iota(jnp.int32, shape, 0)
    ).astype(F32)
    out[...] = lax.dot_general(
        pick, summed, (((1,), (1,)), ((), ())), precision=HIGHEST, preferred_element_type=F32
    )


def bias_of(fulls, inverses, rot_mine, rot_theirs):
    vectors, rows, electrons = rot_mine.shape
    counts = [full.shape[0] for full in fulls]
    total = sum(counts)
    return pl.pallas_call(
        functools.partial(bias_kernel, counts),
        out_shape=jax.ShapeDtypeStruct((total, vectors), F32),
        in_specs=vmem_specs(3 + len(fulls)),
        out_specs=pl.BlockSpec(memory_space=pltpu.VMEM),
        scratch_shapes=[pltpu.VMEM((2, rows // BLOCK, total, BLOCK, electrons), BF16)],
        compiler_params=params(8),
        cost_estimate=pl.CostEstimate(
            flops=4 * total * rows * electrons * (electrons + vectors * BLOCK),
            bytes_accessed=4 * (vectors + total) * rows * electrons,
            transcendentals=0,
        ),
    )(rot_mine, rot_theirs, inverses, *fulls)


def potential_kernel(order, fields, mine, theirs, cholesky, *refs):
    bias_out, kept, *sent, weights = refs
    per_group, vectors = fields.shape
    half, piece = kept.shape[0], sent[0].shape[1]
    b = lax.rem(lax.axis_index("chol"), 2)
    row = lax.broadcasted_iota(jnp.int32, (per_group, vectors), 0)
    bias = jnp.zeros((per_group, vectors), F32)
    for walker in range(half):
        for part, core in ((mine, b), (theirs, 1 - b)):
            slot = order[core * half + walker]
            bias += jnp.where(row == slot, part[walker : walker + 1, :], 0.0)
    bias = TAU_ROOT * bias
    bias_out[...] = bias
    shifted = (fields[...] - bias).astype(BF16)
    slot = jnp.zeros((per_group * BLOCK, 1), jnp.int32)
    place = lax.broadcasted_iota(jnp.int32, slot.shape, 0) // BLOCK
    for at in range(per_group):
        slot = jnp.where(place == at, order[lax.rem(at + b * half, per_group)], slot)
    tall = (per_group * BLOCK, per_group)
    rows = (lax.broadcasted_iota(jnp.int32, tall, 1) == slot).astype(BF16)
    wide = (vectors, vectors * BLOCK)
    columns = (
        lax.broadcasted_iota(jnp.int32, wide, 1) // BLOCK
        == lax.broadcasted_iota(jnp.int32, wide, 0)
    ).astype(BF16)
    spread = jnp.dot(rows, shifted, preferred_element_type=F32).astype(BF16)
    spread = jnp.dot(spread, columns, preferred_element_type=F32)
    same = lax.rem(lax.broadcasted_iota(jnp.int32, spread.shape, 0), BLOCK) == lax.rem(
        lax.broadcasted_iota(jnp.int32, spread.shape, 1), BLOCK
    )
    weights[...] = jnp.where(same, spread, 0.0).astype(BF16)
    rows, orbitals = cholesky.shape[1:]
    for at in range(0, rows, BLOCK):
        columns = cholesky[:, at : at + BLOCK, :].reshape(vectors * BLOCK, orbitals)
        result = TAU_ROOT * jnp.dot(weights[...], columns, preferred_element_type=F32)
        result = result.astype(BF16).reshape(2 * half, BLOCK, orbitals)
        kept[:, at : at + BLOCK, :] = result[:half]
        start = at % piece
        sent[at // piece][:, start : start + BLOCK, :] = result[half:]


def potential_of(order, fields, parts, cholesky):
    per_group, vectors = fields.shape
    half = per_group // 2
    _, rows, orbitals = cholesky.shape
    sent = jax.ShapeDtypeStruct((half, rows // 2, orbitals), BF16)
    return pl.pallas_call(
        potential_kernel,
        out_shape=[
            jax.ShapeDtypeStruct((per_group, vectors), F32),
            jax.ShapeDtypeStruct((half, rows, orbitals), BF16),
            sent,
            sent,
        ],
        in_specs=[pl.BlockSpec(memory_space=pltpu.SMEM)] + vmem_specs(4),
        out_specs=vmem_specs(4),
        scratch_shapes=[pltpu.VMEM((per_group * BLOCK, vectors * BLOCK), BF16)],
        compiler_params=params(12),
    )(order, fields, *parts, cholesky)


def first_kernel(sibling, parts, *refs):
    potential, fulls, (rounded, base) = refs[:parts], refs[parts:-2], refs[-2:]
    b = lax.rem(lax.axis_index("chol"), 2)
    chip = lax.axis_index("chol") // 2
    count = 0
    for full in fulls:
        for walker in range(full.shape[0]):
            rows = jnp.concatenate([part[count] for part in potential], axis=0)
            columns = full[walker].reshape(-1, full.shape[-1])
            term = jnp.dot(rows, columns, preferred_element_type=F32)
            rounded[count] = term.astype(BF16)
            own = full[walker, chip, 1 - b if sibling else b]
            base[count] = own.astype(F32) + term
            count += 1


def first_of(potential, fulls, sibling):
    half, _, orbitals = potential[0].shape
    rows, electrons = fulls[0].shape[-2:]
    shape = (half, rows, electrons)
    return pl.pallas_call(
        functools.partial(first_kernel, sibling, len(potential)),
        out_shape=[jax.ShapeDtypeStruct(shape, BF16), jax.ShapeDtypeStruct(shape, F32)],
        in_specs=vmem_specs(len(potential) + len(fulls)),
        out_specs=vmem_specs(2),
        compiler_params=params(8),
        cost_estimate=pl.CostEstimate(
            flops=2 * half * rows * orbitals * electrons,
            bytes_accessed=2 * half * orbitals * (rows + electrons),
            transcendentals=0,
        ),
    )(*potential, *fulls)


def second_kernel(layout, slabs, parts, *refs):
    potential, base, pieces = refs[:parts], refs[parts], refs[parts + 1 : -2]
    out, full = refs[-2:]
    b = lax.rem(lax.axis_index("chol"), 2)
    for block, stream in zip((b, 1 - b), slabs):
        for operand, at, walker, steps, dy in stream:
            full[walker, layout.origin(steps, dy), block] = pieces[operand][at]
    for walker in range(out.shape[0]):
        rows = jnp.concatenate([part[walker] for part in potential], axis=0)
        columns = full[walker].reshape(-1, full.shape[-1])
        term = jnp.dot(rows, columns, preferred_element_type=F32)
        out[walker] = (base[walker] + 0.5 * term).astype(BF16)


def second_of(layout, potential, base, streams):
    arrays, slabs = operands(streams)
    orbitals = potential[0].shape[2]
    half, rows, electrons = base.shape
    return pl.pallas_call(
        functools.partial(second_kernel, layout, slabs, len(potential)),
        out_shape=[
            jax.ShapeDtypeStruct((half, rows, electrons), BF16),
            jax.ShapeDtypeStruct((half, layout.chol // 2, 2, rows, electrons), BF16),
        ],
        in_specs=vmem_specs(len(potential) + 1 + len(arrays)),
        out_specs=vmem_specs(2),
        compiler_params=params(8),
        cost_estimate=pl.CostEstimate(
            flops=2 * half * rows * orbitals * electrons,
            bytes_accessed=2 * half * orbitals * (rows + 3 * electrons),
            transcendentals=0,
        ),
    )(*potential, base, *arrays)


def finish_kernel(order, potential, base, full, out, results, semaphores):
    half = base.shape[0]
    b = lax.rem(lax.axis_index("chol"), 2)
    copies = []
    for walker in range(half):
        columns = full[walker].reshape(-1, full.shape[-1])
        term = jnp.dot(potential[walker], columns, preferred_element_type=F32)
        results[walker] = (base[walker] + 0.5 * term).astype(BF16)
        copies.append(
            pltpu.make_async_copy(
                results.at[walker], out.at[order[b * half + walker]], semaphores.at[walker]
            )
        )
        copies[-1].start()
    for copy in copies:
        copy.wait()


def finish(order, potential, base, full):
    half, rows, electrons = base.shape
    orbitals = potential.shape[2]
    return pl.pallas_call(
        finish_kernel,
        out_shape=jax.ShapeDtypeStruct((2 * half, rows, electrons), BF16),
        in_specs=[pl.BlockSpec(memory_space=pltpu.SMEM)] + vmem_specs(3),
        out_specs=pl.BlockSpec(memory_space=pl.ANY),
        scratch_shapes=[
            pltpu.VMEM((half, rows, electrons), BF16),
            pltpu.SemaphoreType.DMA((half,)),
        ],
        compiler_params=params(8),
        cost_estimate=pl.CostEstimate(
            flops=2 * half * rows * orbitals * electrons,
            bytes_accessed=2 * half * orbitals * (rows + electrons),
            transcendentals=0,
        ),
    )(order, potential, base, full)


def place_kernel(order, theirs, _, out, semaphores):
    half = theirs.shape[0]
    b = lax.rem(lax.axis_index("chol"), 2)
    copies = [
        pltpu.make_async_copy(
            theirs.at[walker], out.at[order[(1 - b) * half + walker]], semaphores.at[walker]
        )
        for walker in range(half)
    ]
    for copy in copies:
        copy.start()
    for copy in copies:
        copy.wait()


def place(order, theirs, out):
    return pl.pallas_call(
        place_kernel,
        out_shape=jax.ShapeDtypeStruct(out.shape, out.dtype),
        in_specs=[pl.BlockSpec(memory_space=pltpu.SMEM)] + vmem_specs(1)
        + [pl.BlockSpec(memory_space=pl.ANY)],
        out_specs=pl.BlockSpec(memory_space=pl.ANY),
        scratch_shapes=[pltpu.SemaphoreType.DMA((theirs.shape[0],))],
        input_output_aliases={2: 0},
        compiler_params=params(4),
    )(order, theirs, out)


def split_kernel(source, walkers, *refs):
    targets, (order, picked, semaphores) = refs[:4], refs[4:]
    per_group = walkers.shape[0]
    half = per_group // 2
    share = half // 2
    group = lax.axis_index("walk")
    b = lax.rem(lax.axis_index("chol"), 2)
    stayed, arrived, sent = jnp.int32(0), jnp.int32(0), jnp.int32(0)
    for slot in range(per_group):
        local = source[group * per_group + slot] - group * per_group
        stays = ((local >= 0) & (local < per_group)).astype(jnp.int32)
        picked[jnp.where(stays == 1, jnp.minimum(stayed, half - 1), per_group)] = local
        rank = jnp.minimum(jnp.where(stays == 1, stayed, arrived), half - 1)
        core = rank // share
        order[core * half + (1 - stays) * share + rank - core * share] = jnp.int32(slot)
        stayed, arrived = stayed + stays, arrived + 1 - stays
        local = source[(1 - group) * per_group + slot] - group * per_group
        goes = ((local >= 0) & (local < per_group)).astype(jnp.int32)
        picked[jnp.where(goes == 1, half + jnp.minimum(sent, half - 1), per_group)] = local
        sent = sent + goes
    offsets = (b * share, (1 - b) * share, half + b * share, half + (1 - b) * share)
    copies = []
    for target, offset in reversed(list(zip(targets, offsets))):
        for walker in range(share):
            copies.append(
                pltpu.make_async_copy(
                    walkers.at[picked[offset + walker]],
                    target.at[walker],
                    semaphores.at[len(copies)],
                )
            )
    for copy in copies:
        copy.start()
    for copy in copies:
        copy.wait()


def split_walkers(walkers, source):
    per_group, rows, electrons = walkers.shape
    share = jax.ShapeDtypeStruct((per_group // 4, rows, electrons), walkers.dtype)
    return pl.pallas_call(
        split_kernel,
        out_shape=[share] * 4 + [jax.ShapeDtypeStruct((per_group,), jnp.int32)],
        in_specs=[pl.BlockSpec(memory_space=pltpu.SMEM), pl.BlockSpec(memory_space=pl.ANY)],
        out_specs=[pl.BlockSpec(memory_space=pl.ANY)] * 4
        + [pl.BlockSpec(memory_space=pltpu.SMEM)],
        scratch_shapes=[
            pltpu.SMEM((per_group + 1,), jnp.int32),
            pltpu.SemaphoreType.DMA((per_group,)),
        ],
        compiler_params=params(4),
    )(source, walkers)


def ranks(flags):
    count = flags.shape[-1]
    before = jnp.arange(count)[None, :] < jnp.arange(count)[:, None]
    return jnp.sum(jnp.where(before & flags[..., None, :], 1, 0), axis=-1)


def migrate(layout, walkers, source):
    per_group = walkers.shape[0]
    half = per_group // 2
    group = lax.axis_index("walk")
    if layout.walk == 2 and half % 2 == 0:
        stay, stay_sent, near, cross, order = split_walkers(walkers, source)
        count = 2 * layout.chol
        across = [(index + layout.chol) % count for index in range(count)]
        axes = ("walk", "chol")
        near = lax.ppermute(near, axes, list(enumerate(across)))
        cross = lax.ppermute(cross, axes, [(i, j ^ 1) for i, j in enumerate(across)])
        return [(stay, layout.shift(stay_sent, db=1)), (near, cross)], order
    table = source.reshape(layout.walk, per_group)
    incoming = lax.dynamic_index_in_dim(table, group, 0, keepdims=False)
    incoming_groups = incoming // per_group

    def outgoing(distance):
        row = lax.dynamic_index_in_dim(table, (group + distance) % layout.walk, 0, keepdims=False)
        local = row - group * per_group
        here = (local >= 0) & (local < per_group)
        match = here[None, :] & (ranks(here)[None, :] == jnp.arange(half)[:, None])
        return jnp.take(walkers, jnp.sum(jnp.where(match, local[None, :], 0), axis=1), axis=0)

    arrived = [outgoing(0)]
    for distance in range(1, layout.walk):
        pairs = [(g, (g + distance) % layout.walk) for g in range(layout.walk)]
        arrived.append(lax.ppermute(outgoing(distance), "walk", pairs))
    slots = jnp.arange(per_group)
    same = (incoming_groups[:, None] == incoming_groups[None, :]) & (slots[None, :] < slots[:, None])
    rank = jnp.sum(same.astype(jnp.int32), axis=1)
    distance = (group - incoming_groups) % layout.walk
    migrated = jnp.take(jnp.concatenate(arrived, axis=0), distance * half + rank, axis=0)
    b = lax.axis_index("chol") % 2
    mine = lax.dynamic_slice_in_dim(migrated, b * half, half, 0)
    theirs = lax.dynamic_slice_in_dim(migrated, (1 - b) * half, half, 0)
    theirs = layout.shift(theirs, db=1)
    share = half // 2
    shares = [(mine[:share], theirs[:share]), (mine[share:], theirs[share:])]
    return shares, slots.astype(jnp.int32)


def shards(layout, walkers, trial, cholesky, rotated, fields, source):
    b = lax.axis_index("chol") % 2
    shares, order = migrate(layout, walkers, source)
    sizes = [own.shape[0] for own, _ in shares]
    halves = trial.reshape(2, -1, trial.shape[1])
    streams = []
    for at, (own, other) in enumerate(shares):
        both = (jnp.where(b == 0, own, other), jnp.where(b == 0, other, own))
        slabs = jnp.concatenate(both).reshape(-1, *halves.shape[1:])
        streams.append(Stream(layout, jnp.concatenate([slabs, halves[at : at + 1]])))
    rot_theirs = layout.shift(rotated, db=1)
    moved = lax.optimization_barrier([stream.moves() for stream in reversed(streams)])
    for stream, arrays in zip(reversed(streams), moved):
        stream.accept(arrays)
    for _ in range(layout.z - 2):
        for stream in streams:
            stream.advance()
    early, late = [], []
    for at, stream in enumerate(streams):
        slabs = [array[-1:] for array in (*stream.ring, *stream.across)]
        received = layout.shift(jnp.concatenate(slabs), db=1)
        if at == 0:
            (received,) = stream.advance((received,))
        else:
            stream.advance()
        early.append(received)
        late.append(layout.shift(received[layout.z - 1 : layout.z], dy=1))
    *fulls, inverses = inverses_of(layout, streams, sizes, early, late)
    total = bias_of(fulls, inverses, rotated, rot_theirs)
    bits = [2] + [4 << at for at in range(layout.z.bit_length() - 1)]
    while bits:
        masks = [0]
        for bit in bits[:3]:
            masks += [mask + bit for mask in masks]
        sums = [layout.flip(total, mask) if mask else total for mask in masks]
        while len(sums) > 1:
            sums = [one + two for one, two in zip(sums[::2], sums[1::2])]
        total, bits = sums[0], bits[3:]
    parts = [total, layout.flip(total, 1)]
    force_bias, kept, *sent = potential_of(order, fields, parts, cholesky)
    received = [layout.shift(part, db=1) for part in sent]

    rounded, base = first_of([kept], fulls, 0)
    rounded_theirs, base_theirs = first_of(received, fulls, 1)
    streams = [Stream(layout, rounded), Stream(layout, rounded_theirs)]
    for _ in range(layout.z):
        for stream in streams:
            stream.advance()
    sent, full = second_of(layout, received, base_theirs, streams)
    theirs = layout.shift(sent, db=1)
    return place(order, theirs, finish(order, kept, base, full)), force_bias


def solution(mesh):
    in_specs = (
        P("walk", "chol", None),
        P("chol", None),
        P(None, "chol", None),
        P(None, "chol", None),
        P("walk", None),
        P(),
    )
    out_specs = (P("walk", "chol", None), P("walk", None))
    layout = Layout(mesh.shape["walk"], mesh.shape["chol"])
    return jax.shard_map(
        functools.partial(shards, layout),
        mesh=mesh,
        in_specs=in_specs,
        out_specs=out_specs,
        check_vma=False,
    )
```

```python
import functools

import jax
import jax.numpy as jnp
from jax import lax
from jax.experimental import pallas as pl
from jax.experimental.pallas import tpu as pltpu
from jax.sharding import PartitionSpec as P

ITERS = 3
TAU_ROOT = 0.1
BLOCK = 16
HIGHEST = lax.Precision.HIGHEST
MIB = 1024 * 1024

F32 = jnp.float32
BF16 = jnp.bfloat16


def params(mebibytes):
    return pltpu.CompilerParams(vmem_limit_bytes=mebibytes * MIB)


def vmem_specs(count):
    return [pl.BlockSpec(memory_space=pltpu.VMEM)] * count


class Layout:
    def __init__(self, walk_size, chol_size):
        self.walk = walk_size
        self.chol = chol_size
        self.z = chol_size // 4

    def shift(self, array, dz=0, dy=0, db=0):
        pairs = []
        for index in range(self.chol):
            z, y, b = index // 4, (index // 2) % 2, index % 2
            target = (((z + dz) % self.z) * 2 + (y ^ dy)) * 2 + (b ^ db)
            pairs.append((index, target))
        return lax.ppermute(array, "chol", pairs)

    def flip(self, array, mask):
        return lax.ppermute(array, "chol", [(i, i ^ mask) for i in range(self.chol)])

    def step(self, array):
        ring = [*range(0, self.z, 2), *reversed(range(1, self.z, 2))]
        target = {z: ring[(at + 1) % self.z] for at, z in enumerate(ring)}
        pairs = [(index, target[index // 4] * 4 + index % 4) for index in range(self.chol)]
        return lax.ppermute(array, "chol", pairs)

    def origin(self, steps, dy):
        index = lax.axis_index("chol")
        z, y = index // 4, lax.rem(index // 2, 2)
        at = jnp.where(lax.rem(z, 2) == 0, z // 2, self.z - (z + 1) // 2)
        at = lax.rem(at + (self.z - steps), self.z)
        z = jnp.where(2 * at < self.z, 2 * at, 2 * (self.z - at) - 1)
        return z * 2 + (y + dy - 2 * y * dy)


class Stream:
    def __init__(self, layout, piece):
        self.layout = layout
        self.ring = [piece]
        self.across = []
        self.last = []

    def moves(self):
        latest = self.ring[-1]
        if len(self.ring) < self.layout.z:
            return [self.layout.shift(latest, dy=1), self.layout.step(latest)]
        half = (latest.shape[0] + 1) // 2
        return [
            self.layout.shift(latest[:half], dy=1),
            self.layout.step(self.across[-1][half:]),
        ]

    def accept(self, moved):
        if len(self.ring) < self.layout.z:
            self.across.append(moved[0])
            self.ring.append(moved[1])
        else:
            self.last = moved

    def advance(self, anchors=()):
        moved = self.moves()
        if anchors or len(self.ring) < self.layout.z:
            anchors, moved = lax.optimization_barrier((anchors, moved))
        self.accept(moved)
        return anchors

    def pieces(self):
        ring = [(array, 0, steps, 0) for steps, array in enumerate(self.ring)]
        across = [(array, 0, steps, 1) for steps, array in enumerate(self.across)]
        lower, upper = self.last
        steps = self.layout.z - 1
        return ring + across + [(lower, 0, steps, 1), (upper, lower.shape[0], steps, 1)]


def operands(streams):
    arrays, slabs = [], []
    for stream in streams:
        slabs.append([])
        for array, first, steps, dy in stream.pieces():
            for at in range(array.shape[0]):
                slabs[-1].append((len(arrays), at, first + at, steps, dy))
            arrays.append(array)
    return arrays, slabs


def product(left, right):
    high, right_high = left.astype(BF16), right.astype(BF16)
    low = (left - high.astype(F32)).astype(BF16)
    right_low = (right - right_high.astype(F32)).astype(BF16)
    return jnp.dot(
        jnp.concatenate([high, high, low], axis=1),
        jnp.concatenate([right_high, right_low, right_high], axis=0),
        preferred_element_type=F32,
    )


def newton_inverses(matrices):
    shape = matrices[0].shape
    same = lax.broadcasted_iota(jnp.int32, shape, 0) == lax.broadcasted_iota(jnp.int32, shape, 1)
    twice = jnp.where(same, 2.0, 0.0).astype(F32)
    estimates = [twice - matrix for matrix in matrices]
    for _ in range(ITERS - 1):
        steps = [twice - product(a, x) for a, x in zip(matrices, estimates)]
        estimates = [product(x, step) for x, step in zip(estimates, steps)]
    return estimates


def inverse_kernel(layout, slabs, counts, *refs):
    streams = len(counts)
    early, late, refs = refs[:streams], refs[streams : 2 * streams], refs[2 * streams :]
    fulls, (out, buffer, turned) = refs[-3 - streams : -3], refs[-3:]
    pieces = refs[: -3 - streams]
    rows, electrons = early[0].shape[1:]
    b = lax.rem(lax.axis_index("chol"), 2)

    for half, stream in enumerate(slabs):
        place = slice(half * rows, (half + 1) * rows)
        theirs = [(early[half], at) for at in range(early[half].shape[0])] + [(late[half], 0)]
        trial = [slab for slab in stream if slab[2] == 4 * counts[half]]
        for (operand, at, _, steps, dy), (part, number) in zip(trial, theirs):
            origin = layout.origin(steps, dy)
            buffer[origin, b, place] = pieces[operand][at]
            buffer[origin, 1 - b, place] = part[number]
    turned[...] = buffer[...].reshape(-1, electrons).T

    matrices = []
    for full, count, stream in zip(fulls, counts, slabs):
        for operand, at, slab, steps, dy in stream:
            if slab < 4 * count:
                block, walker, half = slab // (2 * count), slab // 2 % count, slab % 2
                place = slice(half * rows, (half + 1) * rows)
                full[walker, layout.origin(steps, dy), block, place] = pieces[operand][at]
        for walker in range(count):
            columns = full[walker].reshape(-1, electrons)
            matrices.append(jnp.dot(turned[...], columns, preferred_element_type=F32))
    for number, inverse in enumerate(newton_inverses(matrices)):
        out[number] = inverse.astype(BF16)


def inverses_of(layout, streams, counts, early, late):
    arrays, slabs = operands(streams)
    _, rows, electrons = early[0].shape
    rows = 2 * rows
    chips = layout.chol // 2
    total = sum(counts)
    return pl.pallas_call(
        functools.partial(inverse_kernel, layout, slabs, counts),
        out_shape=[
            jax.ShapeDtypeStruct((count, chips, 2, rows, electrons), BF16) for count in counts
        ]
        + [jax.ShapeDtypeStruct((total, electrons, electrons), BF16)],
        in_specs=vmem_specs(2 * len(counts) + len(arrays)),
        out_specs=vmem_specs(len(counts) + 1),
        scratch_shapes=[
            pltpu.VMEM((chips, 2, rows, electrons), BF16),
            pltpu.VMEM((electrons, 2 * chips * rows), BF16),
        ],
        compiler_params=params(8),
        cost_estimate=pl.CostEstimate(
            flops=2 * total * electrons**2 * (2 * chips * rows + 6 * (ITERS - 1) * electrons),
            bytes_accessed=4 * (total + 1) * 2 * chips * rows * electrons,
            transcendentals=0,
        ),
    )(*early, *late, *arrays)


def bias_kernel(counts, rot_mine, rot_theirs, inverses, *refs):
    fulls, (out, greens) = refs[:-2], refs[-2:]
    vectors, rows, electrons = rot_mine.shape
    index = lax.axis_index("chol")
    chip, b = index // 2, lax.rem(index, 2)
    walkers = [(full, at) for full, count in zip(fulls, counts) for at in range(count)]
    for number, (full, walker) in enumerate(walkers):
        both = full[walker, chip].reshape(2 * rows, electrons)
        green = jnp.dot(both, inverses[number], preferred_element_type=F32).astype(BF16)
        greens[:, :, number] = green.reshape(2, rows // BLOCK, BLOCK, electrons)
    width = len(walkers) * BLOCK
    total = jnp.zeros((vectors * BLOCK, width), F32)
    for half, rot in ((b, rot_mine), (1 - b, rot_theirs)):
        for block in range(rows // BLOCK):
            total += lax.dot_general(
                rot[:, block * BLOCK : (block + 1) * BLOCK, :].reshape(vectors * BLOCK, electrons),
                greens[half, block].reshape(width, electrons),
                (((1,), (1,)), ((), ())),
                preferred_element_type=F32,
            )
    same = lax.rem(lax.broadcasted_iota(jnp.int32, total.shape, 0), BLOCK) == lax.rem(
        lax.broadcasted_iota(jnp.int32, total.shape, 1), BLOCK
    )
    summed = jnp.sum(jnp.where(same, total, 0.0).reshape(vectors, BLOCK, width), axis=1)
    shape = (len(walkers), width)
    pick = (
        lax.broadcasted_iota(jnp.int32, shape, 1) // BLOCK
        == lax.broadcasted_iota(jnp.int32, shape, 0)
    ).astype(F32)
    out[...] = lax.dot_general(
        pick, summed, (((1,), (1,)), ((), ())), precision=HIGHEST, preferred_element_type=F32
    )


def bias_of(fulls, inverses, rot_mine, rot_theirs):
    vectors, rows, electrons = rot_mine.shape
    counts = [full.shape[0] for full in fulls]
    total = sum(counts)
    return pl.pallas_call(
        functools.partial(bias_kernel, counts),
        out_shape=jax.ShapeDtypeStruct((total, vectors), F32),
        in_specs=vmem_specs(3 + len(fulls)),
        out_specs=pl.BlockSpec(memory_space=pltpu.VMEM),
        scratch_shapes=[pltpu.VMEM((2, rows // BLOCK, total, BLOCK, electrons), BF16)],
        compiler_params=params(8),
        cost_estimate=pl.CostEstimate(
            flops=4 * total * rows * electrons * (electrons + vectors * BLOCK),
            bytes_accessed=4 * (vectors + total) * rows * electrons,
            transcendentals=0,
        ),
    )(rot_mine, rot_theirs, inverses, *fulls)


def potential_kernel(order, fields, parts, cholesky, *refs):
    bias_out, kept, *sent, weights = refs
    per_group, vectors = fields.shape
    half, piece = kept.shape[0], sent[0].shape[1]
    b = lax.rem(lax.axis_index("chol"), 2)
    row = lax.broadcasted_iota(jnp.int32, (per_group, vectors), 0)
    bias = jnp.zeros((per_group, vectors), F32)
    for core in range(2):
        total = parts[core]
        for index in range(core + 2, parts.shape[0], 2):
            total = total + parts[index]
        for walker in range(half):
            slot = order[core * half + walker]
            bias += jnp.where(row == slot, total[walker : walker + 1, :], 0.0)
    bias = TAU_ROOT * bias
    bias_out[...] = bias
    shifted = (fields[...] - bias).astype(BF16)
    slot = jnp.zeros((per_group * BLOCK, 1), jnp.int32)
    place = lax.broadcasted_iota(jnp.int32, slot.shape, 0) // BLOCK
    for at in range(per_group):
        slot = jnp.where(place == at, order[lax.rem(at + b * half, per_group)], slot)
    tall = (per_group * BLOCK, per_group)
    rows = (lax.broadcasted_iota(jnp.int32, tall, 1) == slot).astype(BF16)
    wide = (vectors, vectors * BLOCK)
    columns = (
        lax.broadcasted_iota(jnp.int32, wide, 1) // BLOCK
        == lax.broadcasted_iota(jnp.int32, wide, 0)
    ).astype(BF16)
    spread = jnp.dot(rows, shifted, preferred_element_type=F32).astype(BF16)
    spread = jnp.dot(spread, columns, preferred_element_type=F32)
    same = lax.rem(lax.broadcasted_iota(jnp.int32, spread.shape, 0), BLOCK) == lax.rem(
        lax.broadcasted_iota(jnp.int32, spread.shape, 1), BLOCK
    )
    weights[...] = jnp.where(same, spread, 0.0).astype(BF16)
    rows, orbitals = cholesky.shape[1:]
    for at in range(0, rows, BLOCK):
        columns = cholesky[:, at : at + BLOCK, :].reshape(vectors * BLOCK, orbitals)
        result = TAU_ROOT * jnp.dot(weights[...], columns, preferred_element_type=F32)
        result = result.astype(BF16).reshape(2 * half, BLOCK, orbitals)
        kept[:, at : at + BLOCK, :] = result[:half]
        start = at % piece
        sent[at // piece][:, start : start + BLOCK, :] = result[half:]


def potential_of(order, fields, parts, cholesky):
    per_group, vectors = fields.shape
    half = per_group // 2
    _, rows, orbitals = cholesky.shape
    sent = jax.ShapeDtypeStruct((half, rows // 2, orbitals), BF16)
    return pl.pallas_call(
        potential_kernel,
        out_shape=[
            jax.ShapeDtypeStruct((per_group, vectors), F32),
            jax.ShapeDtypeStruct((half, rows, orbitals), BF16),
            sent,
            sent,
        ],
        in_specs=[pl.BlockSpec(memory_space=pltpu.SMEM)] + vmem_specs(3),
        out_specs=vmem_specs(4),
        scratch_shapes=[pltpu.VMEM((per_group * BLOCK, vectors * BLOCK), BF16)],
        compiler_params=params(12),
    )(order, fields, parts, cholesky)


def first_kernel(sibling, parts, *refs):
    potential, fulls, (rounded, base) = refs[:parts], refs[parts:-2], refs[-2:]
    b = lax.rem(lax.axis_index("chol"), 2)
    chip = lax.axis_index("chol") // 2
    count = 0
    for full in fulls:
        for walker in range(full.shape[0]):
            rows = jnp.concatenate([part[count] for part in potential], axis=0)
            columns = full[walker].reshape(-1, full.shape[-1])
            term = jnp.dot(rows, columns, preferred_element_type=F32)
            rounded[count] = term.astype(BF16)
            own = full[walker, chip, 1 - b if sibling else b]
            base[count] = own.astype(F32) + term
            count += 1


def first_of(potential, fulls, sibling):
    half, _, orbitals = potential[0].shape
    rows, electrons = fulls[0].shape[-2:]
    shape = (half, rows, electrons)
    return pl.pallas_call(
        functools.partial(first_kernel, sibling, len(potential)),
        out_shape=[jax.ShapeDtypeStruct(shape, BF16), jax.ShapeDtypeStruct(shape, F32)],
        in_specs=vmem_specs(len(potential) + len(fulls)),
        out_specs=vmem_specs(2),
        compiler_params=params(8),
        cost_estimate=pl.CostEstimate(
            flops=2 * half * rows * orbitals * electrons,
            bytes_accessed=2 * half * orbitals * (rows + electrons),
            transcendentals=0,
        ),
    )(*potential, *fulls)


def second_kernel(layout, slabs, parts, *refs):
    potential, base, pieces = refs[:parts], refs[parts], refs[parts + 1 : -2]
    out, full = refs[-2:]
    b = lax.rem(lax.axis_index("chol"), 2)
    for block, stream in zip((b, 1 - b), slabs):
        for operand, at, walker, steps, dy in stream:
            full[walker, layout.origin(steps, dy), block] = pieces[operand][at]
    for walker in range(out.shape[0]):
        rows = jnp.concatenate([part[walker] for part in potential], axis=0)
        columns = full[walker].reshape(-1, full.shape[-1])
        term = jnp.dot(rows, columns, preferred_element_type=F32)
        out[walker] = (base[walker] + 0.5 * term).astype(BF16)


def second_of(layout, potential, base, streams):
    arrays, slabs = operands(streams)
    orbitals = potential[0].shape[2]
    half, rows, electrons = base.shape
    return pl.pallas_call(
        functools.partial(second_kernel, layout, slabs, len(potential)),
        out_shape=[
            jax.ShapeDtypeStruct((half, rows, electrons), BF16),
            jax.ShapeDtypeStruct((half, layout.chol // 2, 2, rows, electrons), BF16),
        ],
        in_specs=vmem_specs(len(potential) + 1 + len(arrays)),
        out_specs=vmem_specs(2),
        compiler_params=params(8),
        cost_estimate=pl.CostEstimate(
            flops=2 * half * rows * orbitals * electrons,
            bytes_accessed=2 * half * orbitals * (rows + 3 * electrons),
            transcendentals=0,
        ),
    )(*potential, base, *arrays)


def finish_kernel(order, potential, base, full, out, results, semaphores):
    half = base.shape[0]
    b = lax.rem(lax.axis_index("chol"), 2)
    copies = []
    for walker in range(half):
        columns = full[walker].reshape(-1, full.shape[-1])
        term = jnp.dot(potential[walker], columns, preferred_element_type=F32)
        results[walker] = (base[walker] + 0.5 * term).astype(BF16)
        copies.append(
            pltpu.make_async_copy(
                results.at[walker], out.at[order[b * half + walker]], semaphores.at[walker]
            )
        )
        copies[-1].start()
    for copy in copies:
        copy.wait()


def finish(order, potential, base, full):
    half, rows, electrons = base.shape
    orbitals = potential.shape[2]
    return pl.pallas_call(
        finish_kernel,
        out_shape=jax.ShapeDtypeStruct((2 * half, rows, electrons), BF16),
        in_specs=[pl.BlockSpec(memory_space=pltpu.SMEM)] + vmem_specs(3),
        out_specs=pl.BlockSpec(memory_space=pl.ANY),
        scratch_shapes=[
            pltpu.VMEM((half, rows, electrons), BF16),
            pltpu.SemaphoreType.DMA((half,)),
        ],
        compiler_params=params(8),
        cost_estimate=pl.CostEstimate(
            flops=2 * half * rows * orbitals * electrons,
            bytes_accessed=2 * half * orbitals * (rows + electrons),
            transcendentals=0,
        ),
    )(order, potential, base, full)


def place_kernel(order, theirs, _, out, semaphores):
    half = theirs.shape[0]
    b = lax.rem(lax.axis_index("chol"), 2)
    copies = [
        pltpu.make_async_copy(
            theirs.at[walker], out.at[order[(1 - b) * half + walker]], semaphores.at[walker]
        )
        for walker in range(half)
    ]
    for copy in copies:
        copy.start()
    for copy in copies:
        copy.wait()


def place(order, theirs, out):
    return pl.pallas_call(
        place_kernel,
        out_shape=jax.ShapeDtypeStruct(out.shape, out.dtype),
        in_specs=[pl.BlockSpec(memory_space=pltpu.SMEM)] + vmem_specs(1)
        + [pl.BlockSpec(memory_space=pl.ANY)],
        out_specs=pl.BlockSpec(memory_space=pl.ANY),
        scratch_shapes=[pltpu.SemaphoreType.DMA((theirs.shape[0],))],
        input_output_aliases={2: 0},
        compiler_params=params(4),
    )(order, theirs, out)


def split_kernel(source, walkers, *refs):
    targets, (order, picked, semaphores) = refs[:4], refs[4:]
    per_group = walkers.shape[0]
    half = per_group // 2
    share = half // 2
    group = lax.axis_index("walk")
    b = lax.rem(lax.axis_index("chol"), 2)
    stayed, arrived, sent = jnp.int32(0), jnp.int32(0), jnp.int32(0)
    for slot in range(per_group):
        local = source[group * per_group + slot] - group * per_group
        stays = ((local >= 0) & (local < per_group)).astype(jnp.int32)
        picked[jnp.where(stays == 1, jnp.minimum(stayed, half - 1), per_group)] = local
        rank = jnp.minimum(jnp.where(stays == 1, stayed, arrived), half - 1)
        core = rank // share
        order[core * half + stays * share + rank - core * share] = jnp.int32(slot)
        stayed, arrived = stayed + stays, arrived + 1 - stays
        local = source[(1 - group) * per_group + slot] - group * per_group
        goes = ((local >= 0) & (local < per_group)).astype(jnp.int32)
        picked[jnp.where(goes == 1, half + jnp.minimum(sent, half - 1), per_group)] = local
        sent = sent + goes
    offsets = (b * share, (1 - b) * share, half + b * share, half + (1 - b) * share)
    copies = []
    for target, offset in reversed(list(zip(targets, offsets))):
        for walker in range(share):
            copies.append(
                pltpu.make_async_copy(
                    walkers.at[picked[offset + walker]],
                    target.at[walker],
                    semaphores.at[len(copies)],
                )
            )
    for copy in copies:
        copy.start()
    for copy in copies:
        copy.wait()


def split_walkers(walkers, source):
    per_group, rows, electrons = walkers.shape
    share = jax.ShapeDtypeStruct((per_group // 4, rows, electrons), walkers.dtype)
    return pl.pallas_call(
        split_kernel,
        out_shape=[share] * 4 + [jax.ShapeDtypeStruct((per_group,), jnp.int32)],
        in_specs=[pl.BlockSpec(memory_space=pltpu.SMEM), pl.BlockSpec(memory_space=pl.ANY)],
        out_specs=[pl.BlockSpec(memory_space=pl.ANY)] * 4
        + [pl.BlockSpec(memory_space=pltpu.SMEM)],
        scratch_shapes=[
            pltpu.SMEM((per_group + 1,), jnp.int32),
            pltpu.SemaphoreType.DMA((per_group,)),
        ],
        compiler_params=params(4),
    )(source, walkers)


def ranks(flags):
    count = flags.shape[-1]
    before = jnp.arange(count)[None, :] < jnp.arange(count)[:, None]
    return jnp.sum(jnp.where(before & flags[..., None, :], 1, 0), axis=-1)


def migrate(layout, walkers, source):
    per_group = walkers.shape[0]
    half = per_group // 2
    group = lax.axis_index("walk")
    if layout.walk == 2 and half % 2 == 0:
        stay, stay_sent, near, cross, order = split_walkers(walkers, source)
        count = 2 * layout.chol
        across = [(index + layout.chol) % count for index in range(count)]
        axes = ("walk", "chol")
        near = lax.ppermute(near, axes, list(enumerate(across)))
        cross = lax.ppermute(cross, axes, [(i, j ^ 1) for i, j in enumerate(across)])
        return [(near, cross), (stay, layout.shift(stay_sent, db=1))], order
    table = source.reshape(layout.walk, per_group)
    incoming = lax.dynamic_index_in_dim(table, group, 0, keepdims=False)
    incoming_groups = incoming // per_group

    def outgoing(distance):
        row = lax.dynamic_index_in_dim(table, (group + distance) % layout.walk, 0, keepdims=False)
        local = row - group * per_group
        here = (local >= 0) & (local < per_group)
        match = here[None, :] & (ranks(here)[None, :] == jnp.arange(half)[:, None])
        return jnp.take(walkers, jnp.sum(jnp.where(match, local[None, :], 0), axis=1), axis=0)

    arrived = [outgoing(0)]
    for distance in range(1, layout.walk):
        pairs = [(g, (g + distance) % layout.walk) for g in range(layout.walk)]
        arrived.append(lax.ppermute(outgoing(distance), "walk", pairs))
    slots = jnp.arange(per_group)
    same = (incoming_groups[:, None] == incoming_groups[None, :]) & (slots[None, :] < slots[:, None])
    rank = jnp.sum(same.astype(jnp.int32), axis=1)
    distance = (group - incoming_groups) % layout.walk
    migrated = jnp.take(jnp.concatenate(arrived, axis=0), distance * half + rank, axis=0)
    b = lax.axis_index("chol") % 2
    mine = lax.dynamic_slice_in_dim(migrated, b * half, half, 0)
    theirs = lax.dynamic_slice_in_dim(migrated, (1 - b) * half, half, 0)
    theirs = layout.shift(theirs, db=1)
    share = half // 2
    shares = [(mine[:share], theirs[:share]), (mine[share:], theirs[share:])]
    return shares, slots.astype(jnp.int32)


def shards(layout, walkers, trial, cholesky, rotated, fields, source):
    b = lax.axis_index("chol") % 2
    shares, order = migrate(layout, walkers, source)
    sizes = [own.shape[0] for own, _ in shares]
    halves = trial.reshape(2, -1, trial.shape[1])
    streams = []
    for at, (own, other) in enumerate(shares):
        both = (jnp.where(b == 0, own, other), jnp.where(b == 0, other, own))
        slabs = jnp.concatenate(both).reshape(-1, *halves.shape[1:])
        streams.append(Stream(layout, jnp.concatenate([slabs, halves[at : at + 1]])))
    rot_theirs = layout.shift(rotated, db=1)
    for _ in range(layout.z - 1):
        for stream in streams:
            stream.advance()
    early, late = [], []
    for at, stream in enumerate(streams):
        slabs = [array[-1:] for array in (*stream.ring, *stream.across)]
        received = layout.shift(jnp.concatenate(slabs), db=1)
        if at == 1:
            (received,) = stream.advance((received,))
        else:
            stream.advance()
        early.append(received)
        late.append(layout.shift(received[layout.z - 1 : layout.z], dy=1))
    *fulls, inverses = inverses_of(layout, streams, sizes, early, late)
    total = bias_of(fulls, inverses, rotated, rot_theirs)
    parts = lax.all_to_all(
        jnp.broadcast_to(total, (layout.chol, *total.shape)), "chol", 0, 0, tiled=True
    )
    force_bias, kept, *sent = potential_of(order, fields, parts, cholesky)
    received = [layout.shift(part, db=1) for part in sent]

    rounded, base = first_of([kept], fulls, 0)
    rounded_theirs, base_theirs = first_of(received, fulls, 1)
    streams = [Stream(layout, rounded), Stream(layout, rounded_theirs)]
    for _ in range(layout.z):
        for stream in streams:
            stream.advance()
    sent, full = second_of(layout, received, base_theirs, streams)
    theirs = layout.shift(sent, db=1)
    return place(order, theirs, finish(order, kept, base, full)), force_bias


def solution(mesh):
    in_specs = (
        P("walk", "chol", None),
        P("chol", None),
        P(None, "chol", None),
        P(None, "chol", None),
        P("walk", None),
        P(),
    )
    out_specs = (P("walk", "chol", None), P("walk", None))
    layout = Layout(mesh.shape["walk"], mesh.shape["chol"])
    return jax.shard_map(
        functools.partial(shards, layout),
        mesh=mesh,
        in_specs=in_specs,
        out_specs=out_specs,
        check_vma=False,
    )
```

```python
import functools

import jax
import jax.numpy as jnp
from jax import lax
from jax.experimental import pallas as pl
from jax.experimental.pallas import tpu as pltpu
from jax.sharding import PartitionSpec as P

ITERS = 3
TAU_ROOT = 0.1
BLOCK = 16
HIGHEST = lax.Precision.HIGHEST
MIB = 1024 * 1024

F32 = jnp.float32
BF16 = jnp.bfloat16


def params(mebibytes):
    return pltpu.CompilerParams(vmem_limit_bytes=mebibytes * MIB)


def vmem_specs(count):
    return [pl.BlockSpec(memory_space=pltpu.VMEM)] * count


class Layout:
    def __init__(self, walk_size, chol_size):
        self.walk = walk_size
        self.chol = chol_size
        self.z = chol_size // 4

    def shift(self, array, dz=0, dy=0, db=0):
        pairs = []
        for index in range(self.chol):
            z, y, b = index // 4, (index // 2) % 2, index % 2
            target = (((z + dz) % self.z) * 2 + (y ^ dy)) * 2 + (b ^ db)
            pairs.append((index, target))
        return lax.ppermute(array, "chol", pairs)

    def flip(self, array, mask):
        return lax.ppermute(array, "chol", [(i, i ^ mask) for i in range(self.chol)])

    def step(self, array):
        ring = [*range(0, self.z, 2), *reversed(range(1, self.z, 2))]
        target = {z: ring[(at + 1) % self.z] for at, z in enumerate(ring)}
        pairs = [(index, target[index // 4] * 4 + index % 4) for index in range(self.chol)]
        return lax.ppermute(array, "chol", pairs)

    def origin(self, steps, dy):
        index = lax.axis_index("chol")
        z, y = index // 4, lax.rem(index // 2, 2)
        at = jnp.where(lax.rem(z, 2) == 0, z // 2, self.z - (z + 1) // 2)
        at = lax.rem(at + (self.z - steps), self.z)
        z = jnp.where(2 * at < self.z, 2 * at, 2 * (self.z - at) - 1)
        return z * 2 + (y + dy - 2 * y * dy)


class Stream:
    def __init__(self, layout, piece):
        self.layout = layout
        self.ring = [piece]
        self.across = []
        self.last = []

    def moves(self):
        latest = self.ring[-1]
        if len(self.ring) < self.layout.z:
            return [self.layout.shift(latest, dy=1), self.layout.step(latest)]
        half = (latest.shape[0] + 1) // 2
        return [
            self.layout.shift(latest[:half], dy=1),
            self.layout.step(self.across[-1][half:]),
        ]

    def accept(self, moved):
        if len(self.ring) < self.layout.z:
            self.across.append(moved[0])
            self.ring.append(moved[1])
        else:
            self.last = moved

    def advance(self, anchors=()):
        moved = self.moves()
        if anchors or len(self.ring) < self.layout.z:
            anchors, moved = lax.optimization_barrier((anchors, moved))
        self.accept(moved)
        return anchors

    def pieces(self):
        ring = [(array, 0, steps, 0) for steps, array in enumerate(self.ring)]
        across = [(array, 0, steps, 1) for steps, array in enumerate(self.across)]
        lower, upper = self.last
        steps = self.layout.z - 1
        return ring + across + [(lower, 0, steps, 1), (upper, lower.shape[0], steps, 1)]


def operands(streams):
    arrays, slabs = [], []
    for stream in streams:
        slabs.append([])
        for array, first, steps, dy in stream.pieces():
            for at in range(array.shape[0]):
                slabs[-1].append((len(arrays), at, first + at, steps, dy))
            arrays.append(array)
    return arrays, slabs


def product(left, right):
    high, right_high = left.astype(BF16), right.astype(BF16)
    low = (left - high.astype(F32)).astype(BF16)
    right_low = (right - right_high.astype(F32)).astype(BF16)
    return jnp.dot(
        jnp.concatenate([high, high, low], axis=1),
        jnp.concatenate([right_high, right_low, right_high], axis=0),
        preferred_element_type=F32,
    )


def newton_inverses(matrices):
    shape = matrices[0].shape
    same = lax.broadcasted_iota(jnp.int32, shape, 0) == lax.broadcasted_iota(jnp.int32, shape, 1)
    twice = jnp.where(same, 2.0, 0.0).astype(F32)
    estimates = [twice - matrix for matrix in matrices]
    for _ in range(ITERS - 1):
        steps = [twice - product(a, x) for a, x in zip(matrices, estimates)]
        estimates = [product(x, step) for x, step in zip(estimates, steps)]
    return estimates


def inverse_kernel(layout, slabs, counts, *refs):
    streams = len(counts)
    early, late, refs = refs[:streams], refs[streams : 2 * streams], refs[2 * streams :]
    fulls, (out, buffer, turned) = refs[-3 - streams : -3], refs[-3:]
    pieces = refs[: -3 - streams]
    rows, electrons = early[0].shape[1:]
    b = lax.rem(lax.axis_index("chol"), 2)

    for half, stream in enumerate(slabs):
        place = slice(half * rows, (half + 1) * rows)
        theirs = [(early[half], at) for at in range(early[half].shape[0])] + [(late[half], 0)]
        trial = [slab for slab in stream if slab[2] == 4 * counts[half]]
        for (operand, at, _, steps, dy), (part, number) in zip(trial, theirs):
            origin = layout.origin(steps, dy)
            buffer[origin, b, place] = pieces[operand][at]
            buffer[origin, 1 - b, place] = part[number]
    turned[...] = buffer[...].reshape(-1, electrons).T

    matrices = []
    for full, count, stream in zip(fulls, counts, slabs):
        for operand, at, slab, steps, dy in stream:
            if slab < 4 * count:
                block, walker, half = slab // (2 * count), slab // 2 % count, slab % 2
                place = slice(half * rows, (half + 1) * rows)
                full[walker, layout.origin(steps, dy), block, place] = pieces[operand][at]
        for walker in range(count):
            columns = full[walker].reshape(-1, electrons)
            matrices.append(jnp.dot(turned[...], columns, preferred_element_type=F32))
    for number, inverse in enumerate(newton_inverses(matrices)):
        out[number] = inverse.astype(BF16)


def inverses_of(layout, streams, counts, early, late):
    arrays, slabs = operands(streams)
    _, rows, electrons = early[0].shape
    rows = 2 * rows
    chips = layout.chol // 2
    total = sum(counts)
    return pl.pallas_call(
        functools.partial(inverse_kernel, layout, slabs, counts),
        out_shape=[
            jax.ShapeDtypeStruct((count, chips, 2, rows, electrons), BF16) for count in counts
        ]
        + [jax.ShapeDtypeStruct((total, electrons, electrons), BF16)],
        in_specs=vmem_specs(2 * len(counts) + len(arrays)),
        out_specs=vmem_specs(len(counts) + 1),
        scratch_shapes=[
            pltpu.VMEM((chips, 2, rows, electrons), BF16),
            pltpu.VMEM((electrons, 2 * chips * rows), BF16),
        ],
        compiler_params=params(8),
        cost_estimate=pl.CostEstimate(
            flops=2 * total * electrons**2 * (2 * chips * rows + 6 * (ITERS - 1) * electrons),
            bytes_accessed=4 * (total + 1) * 2 * chips * rows * electrons,
            transcendentals=0,
        ),
    )(*early, *late, *arrays)


def bias_kernel(counts, rot_mine, rot_theirs, inverses, *refs):
    fulls, (out, greens) = refs[:-2], refs[-2:]
    vectors, rows, electrons = rot_mine.shape
    index = lax.axis_index("chol")
    chip, b = index // 2, lax.rem(index, 2)
    walkers = [(full, at) for full, count in zip(fulls, counts) for at in range(count)]
    for number, (full, walker) in enumerate(walkers):
        both = full[walker, chip].reshape(2 * rows, electrons)
        green = jnp.dot(both, inverses[number], preferred_element_type=F32).astype(BF16)
        greens[:, :, number] = green.reshape(2, rows // BLOCK, BLOCK, electrons)
    width = len(walkers) * BLOCK
    total = jnp.zeros((vectors * BLOCK, width), F32)
    for half, rot in ((b, rot_mine), (1 - b, rot_theirs)):
        for block in range(rows // BLOCK):
            total += lax.dot_general(
                rot[:, block * BLOCK : (block + 1) * BLOCK, :].reshape(vectors * BLOCK, electrons),
                greens[half, block].reshape(width, electrons),
                (((1,), (1,)), ((), ())),
                preferred_element_type=F32,
            )
    same = lax.rem(lax.broadcasted_iota(jnp.int32, total.shape, 0), BLOCK) == lax.rem(
        lax.broadcasted_iota(jnp.int32, total.shape, 1), BLOCK
    )
    summed = jnp.sum(jnp.where(same, total, 0.0).reshape(vectors, BLOCK, width), axis=1)
    shape = (len(walkers), width)
    pick = (
        lax.broadcasted_iota(jnp.int32, shape, 1) // BLOCK
        == lax.broadcasted_iota(jnp.int32, shape, 0)
    ).astype(F32)
    bias = lax.dot_general(
        pick, summed, (((1,), (1,)), ((), ())), precision=HIGHEST, preferred_element_type=F32
    )
    out[...] = jnp.zeros_like(out)
    for index in range(out.shape[0]):
        out[index, : len(walkers), :vectors] = bias


def bias_of(layout, fulls, inverses, rot_mine, rot_theirs):
    vectors, rows, electrons = rot_mine.shape
    counts = [full.shape[0] for full in fulls]
    total = sum(counts)
    return pl.pallas_call(
        functools.partial(bias_kernel, counts),
        out_shape=jax.ShapeDtypeStruct(
            (layout.chol, pl.cdiv(total, 8) * 8, pl.cdiv(vectors, 128) * 128), F32
        ),
        in_specs=vmem_specs(3 + len(fulls)),
        out_specs=pl.BlockSpec(memory_space=pltpu.VMEM),
        scratch_shapes=[pltpu.VMEM((2, rows // BLOCK, total, BLOCK, electrons), BF16)],
        compiler_params=params(8),
        cost_estimate=pl.CostEstimate(
            flops=4 * total * rows * electrons * (electrons + vectors * BLOCK),
            bytes_accessed=4 * (vectors + total) * rows * electrons,
            transcendentals=0,
        ),
    )(rot_mine, rot_theirs, inverses, *fulls)


def potential_kernel(order, fields, parts, cholesky, *refs):
    bias_out, kept, *sent, weights = refs
    per_group, vectors = fields.shape
    half, piece = kept.shape[0], sent[0].shape[1]
    b = lax.rem(lax.axis_index("chol"), 2)
    row = lax.broadcasted_iota(jnp.int32, (per_group, vectors), 0)
    bias = jnp.zeros((per_group, vectors), F32)
    for core in range(2):
        total = parts[core]
        for index in range(core + 2, parts.shape[0], 2):
            total = total + parts[index]
        for walker in range(half):
            slot = order[core * half + walker]
            bias += jnp.where(row == slot, total[walker : walker + 1, :vectors], 0.0)
    bias = TAU_ROOT * bias
    bias_out[...] = bias
    shifted = (fields[...] - bias).astype(BF16)
    slot = jnp.zeros((per_group * BLOCK, 1), jnp.int32)
    place = lax.broadcasted_iota(jnp.int32, slot.shape, 0) // BLOCK
    for at in range(per_group):
        slot = jnp.where(place == at, order[lax.rem(at + b * half, per_group)], slot)
    tall = (per_group * BLOCK, per_group)
    rows = (lax.broadcasted_iota(jnp.int32, tall, 1) == slot).astype(BF16)
    wide = (vectors, vectors * BLOCK)
    columns = (
        lax.broadcasted_iota(jnp.int32, wide, 1) // BLOCK
        == lax.broadcasted_iota(jnp.int32, wide, 0)
    ).astype(BF16)
    spread = jnp.dot(rows, shifted, preferred_element_type=F32).astype(BF16)
    spread = jnp.dot(spread, columns, preferred_element_type=F32)
    same = lax.rem(lax.broadcasted_iota(jnp.int32, spread.shape, 0), BLOCK) == lax.rem(
        lax.broadcasted_iota(jnp.int32, spread.shape, 1), BLOCK
    )
    weights[...] = jnp.where(same, spread, 0.0).astype(BF16)
    rows, orbitals = cholesky.shape[1:]
    for at in range(0, rows, BLOCK):
        columns = cholesky[:, at : at + BLOCK, :].reshape(vectors * BLOCK, orbitals)
        result = TAU_ROOT * jnp.dot(weights[...], columns, preferred_element_type=F32)
        result = result.astype(BF16).reshape(2 * half, BLOCK, orbitals)
        kept[:, at : at + BLOCK, :] = result[:half]
        start = at % piece
        sent[at // piece][:, start : start + BLOCK, :] = result[half:]


def potential_of(order, fields, parts, cholesky):
    per_group, vectors = fields.shape
    half = per_group // 2
    _, rows, orbitals = cholesky.shape
    sent = jax.ShapeDtypeStruct((half, rows // 2, orbitals), BF16)
    return pl.pallas_call(
        potential_kernel,
        out_shape=[
            jax.ShapeDtypeStruct((per_group, vectors), F32),
            jax.ShapeDtypeStruct((half, rows, orbitals), BF16),
            sent,
            sent,
        ],
        in_specs=[pl.BlockSpec(memory_space=pltpu.SMEM)] + vmem_specs(3),
        out_specs=vmem_specs(4),
        scratch_shapes=[pltpu.VMEM((per_group * BLOCK, vectors * BLOCK), BF16)],
        compiler_params=params(12),
    )(order, fields, parts, cholesky)


def first_kernel(sibling, parts, *refs):
    potential, fulls, (rounded, base) = refs[:parts], refs[parts:-2], refs[-2:]
    b = lax.rem(lax.axis_index("chol"), 2)
    chip = lax.axis_index("chol") // 2
    count = 0
    for full in fulls:
        for walker in range(full.shape[0]):
            rows = jnp.concatenate([part[count] for part in potential], axis=0)
            columns = full[walker].reshape(-1, full.shape[-1])
            term = jnp.dot(rows, columns, preferred_element_type=F32)
            rounded[count] = term.astype(BF16)
            own = full[walker, chip, 1 - b if sibling else b]
            base[count] = own.astype(F32) + term
            count += 1


def first_of(potential, fulls, sibling):
    half, _, orbitals = potential[0].shape
    rows, electrons = fulls[0].shape[-2:]
    shape = (half, rows, electrons)
    return pl.pallas_call(
        functools.partial(first_kernel, sibling, len(potential)),
        out_shape=[jax.ShapeDtypeStruct(shape, BF16), jax.ShapeDtypeStruct(shape, F32)],
        in_specs=vmem_specs(len(potential) + len(fulls)),
        out_specs=vmem_specs(2),
        compiler_params=params(8),
        cost_estimate=pl.CostEstimate(
            flops=2 * half * rows * orbitals * electrons,
            bytes_accessed=2 * half * orbitals * (rows + electrons),
            transcendentals=0,
        ),
    )(*potential, *fulls)


def second_kernel(layout, slabs, parts, *refs):
    potential, base, pieces = refs[:parts], refs[parts], refs[parts + 1 : -2]
    out, full = refs[-2:]
    b = lax.rem(lax.axis_index("chol"), 2)
    for block, stream in zip((b, 1 - b), slabs):
        for operand, at, walker, steps, dy in stream:
            full[walker, layout.origin(steps, dy), block] = pieces[operand][at]
    for walker in range(out.shape[0]):
        rows = jnp.concatenate([part[walker] for part in potential], axis=0)
        columns = full[walker].reshape(-1, full.shape[-1])
        term = jnp.dot(rows, columns, preferred_element_type=F32)
        out[walker] = (base[walker] + 0.5 * term).astype(BF16)


def second_of(layout, potential, base, streams):
    arrays, slabs = operands(streams)
    orbitals = potential[0].shape[2]
    half, rows, electrons = base.shape
    return pl.pallas_call(
        functools.partial(second_kernel, layout, slabs, len(potential)),
        out_shape=[
            jax.ShapeDtypeStruct((half, rows, electrons), BF16),
            jax.ShapeDtypeStruct((half, layout.chol // 2, 2, rows, electrons), BF16),
        ],
        in_specs=vmem_specs(len(potential) + 1 + len(arrays)),
        out_specs=vmem_specs(2),
        compiler_params=params(8),
        cost_estimate=pl.CostEstimate(
            flops=2 * half * rows * orbitals * electrons,
            bytes_accessed=2 * half * orbitals * (rows + 3 * electrons),
            transcendentals=0,
        ),
    )(*potential, base, *arrays)


def finish_kernel(order, potential, base, full, out, results, semaphores):
    half = base.shape[0]
    b = lax.rem(lax.axis_index("chol"), 2)
    copies = []
    for walker in range(half):
        columns = full[walker].reshape(-1, full.shape[-1])
        term = jnp.dot(potential[walker], columns, preferred_element_type=F32)
        results[walker] = (base[walker] + 0.5 * term).astype(BF16)
        copies.append(
            pltpu.make_async_copy(
                results.at[walker], out.at[order[b * half + walker]], semaphores.at[walker]
            )
        )
        copies[-1].start()
    for copy in copies:
        copy.wait()


def finish(order, potential, base, full):
    half, rows, electrons = base.shape
    orbitals = potential.shape[2]
    return pl.pallas_call(
        finish_kernel,
        out_shape=jax.ShapeDtypeStruct((2 * half, rows, electrons), BF16),
        in_specs=[pl.BlockSpec(memory_space=pltpu.SMEM)] + vmem_specs(3),
        out_specs=pl.BlockSpec(memory_space=pl.ANY),
        scratch_shapes=[
            pltpu.VMEM((half, rows, electrons), BF16),
            pltpu.SemaphoreType.DMA((half,)),
        ],
        compiler_params=params(8),
        cost_estimate=pl.CostEstimate(
            flops=2 * half * rows * orbitals * electrons,
            bytes_accessed=2 * half * orbitals * (rows + electrons),
            transcendentals=0,
        ),
    )(order, potential, base, full)


def place_kernel(order, theirs, _, out, semaphores):
    half = theirs.shape[0]
    b = lax.rem(lax.axis_index("chol"), 2)
    copies = [
        pltpu.make_async_copy(
            theirs.at[walker], out.at[order[(1 - b) * half + walker]], semaphores.at[walker]
        )
        for walker in range(half)
    ]
    for copy in copies:
        copy.start()
    for copy in copies:
        copy.wait()


def place(order, theirs, out):
    return pl.pallas_call(
        place_kernel,
        out_shape=jax.ShapeDtypeStruct(out.shape, out.dtype),
        in_specs=[pl.BlockSpec(memory_space=pltpu.SMEM)] + vmem_specs(1)
        + [pl.BlockSpec(memory_space=pl.ANY)],
        out_specs=pl.BlockSpec(memory_space=pl.ANY),
        scratch_shapes=[pltpu.SemaphoreType.DMA((theirs.shape[0],))],
        input_output_aliases={2: 0},
        compiler_params=params(4),
    )(order, theirs, out)


def split_kernel(source, walkers, *refs):
    targets, (order, picked, semaphores) = refs[:4], refs[4:]
    per_group = walkers.shape[0]
    half = per_group // 2
    share = half // 2
    group = lax.axis_index("walk")
    b = lax.rem(lax.axis_index("chol"), 2)
    stayed, arrived, sent = jnp.int32(0), jnp.int32(0), jnp.int32(0)
    for slot in range(per_group):
        local = source[group * per_group + slot] - group * per_group
        stays = ((local >= 0) & (local < per_group)).astype(jnp.int32)
        picked[jnp.where(stays == 1, jnp.minimum(stayed, half - 1), per_group)] = local
        rank = jnp.minimum(jnp.where(stays == 1, stayed, arrived), half - 1)
        core = rank // share
        order[core * half + stays * share + rank - core * share] = jnp.int32(slot)
        stayed, arrived = stayed + stays, arrived + 1 - stays
        local = source[(1 - group) * per_group + slot] - group * per_group
        goes = ((local >= 0) & (local < per_group)).astype(jnp.int32)
        picked[jnp.where(goes == 1, half + jnp.minimum(sent, half - 1), per_group)] = local
        sent = sent + goes
    offsets = (b * share, (1 - b) * share, half + b * share, half + (1 - b) * share)
    copies = []
    for target, offset in reversed(list(zip(targets, offsets))):
        for walker in range(share):
            copies.append(
                pltpu.make_async_copy(
                    walkers.at[picked[offset + walker]],
                    target.at[walker],
                    semaphores.at[len(copies)],
                )
            )
    for copy in copies:
        copy.start()
    for copy in copies:
        copy.wait()


def split_walkers(walkers, source):
    per_group, rows, electrons = walkers.shape
    share = jax.ShapeDtypeStruct((per_group // 4, rows, electrons), walkers.dtype)
    return pl.pallas_call(
        split_kernel,
        out_shape=[share] * 4 + [jax.ShapeDtypeStruct((per_group,), jnp.int32)],
        in_specs=[pl.BlockSpec(memory_space=pltpu.SMEM), pl.BlockSpec(memory_space=pl.ANY)],
        out_specs=[pl.BlockSpec(memory_space=pl.ANY)] * 4
        + [pl.BlockSpec(memory_space=pltpu.SMEM)],
        scratch_shapes=[
            pltpu.SMEM((per_group + 1,), jnp.int32),
            pltpu.SemaphoreType.DMA((per_group,)),
        ],
        compiler_params=params(4),
    )(source, walkers)


def ranks(flags):
    count = flags.shape[-1]
    before = jnp.arange(count)[None, :] < jnp.arange(count)[:, None]
    return jnp.sum(jnp.where(before & flags[..., None, :], 1, 0), axis=-1)


def migrate(layout, walkers, source):
    per_group = walkers.shape[0]
    half = per_group // 2
    group = lax.axis_index("walk")
    if layout.walk == 2 and half % 2 == 0:
        stay, stay_sent, near, cross, order = split_walkers(walkers, source)
        count = 2 * layout.chol
        across = [(index + layout.chol) % count for index in range(count)]
        axes = ("walk", "chol")
        near = lax.ppermute(near, axes, list(enumerate(across)))
        cross = lax.ppermute(cross, axes, [(i, j ^ 1) for i, j in enumerate(across)])
        return [(near, cross), (stay, layout.shift(stay_sent, db=1))], order
    table = source.reshape(layout.walk, per_group)
    incoming = lax.dynamic_index_in_dim(table, group, 0, keepdims=False)
    incoming_groups = incoming // per_group

    def outgoing(distance):
        row = lax.dynamic_index_in_dim(table, (group + distance) % layout.walk, 0, keepdims=False)
        local = row - group * per_group
        here = (local >= 0) & (local < per_group)
        match = here[None, :] & (ranks(here)[None, :] == jnp.arange(half)[:, None])
        return jnp.take(walkers, jnp.sum(jnp.where(match, local[None, :], 0), axis=1), axis=0)

    arrived = [outgoing(0)]
    for distance in range(1, layout.walk):
        pairs = [(g, (g + distance) % layout.walk) for g in range(layout.walk)]
        arrived.append(lax.ppermute(outgoing(distance), "walk", pairs))
    slots = jnp.arange(per_group)
    same = (incoming_groups[:, None] == incoming_groups[None, :]) & (slots[None, :] < slots[:, None])
    rank = jnp.sum(same.astype(jnp.int32), axis=1)
    distance = (group - incoming_groups) % layout.walk
    migrated = jnp.take(jnp.concatenate(arrived, axis=0), distance * half + rank, axis=0)
    b = lax.axis_index("chol") % 2
    mine = lax.dynamic_slice_in_dim(migrated, b * half, half, 0)
    theirs = lax.dynamic_slice_in_dim(migrated, (1 - b) * half, half, 0)
    theirs = layout.shift(theirs, db=1)
    share = half // 2
    shares = [(mine[:share], theirs[:share]), (mine[share:], theirs[share:])]
    return shares, slots.astype(jnp.int32)


def shards(layout, walkers, trial, cholesky, rotated, fields, source):
    b = lax.axis_index("chol") % 2
    shares, order = migrate(layout, walkers, source)
    sizes = [own.shape[0] for own, _ in shares]
    halves = trial.reshape(2, -1, trial.shape[1])
    streams = []
    for at, (own, other) in enumerate(shares):
        both = (jnp.where(b == 0, own, other), jnp.where(b == 0, other, own))
        slabs = jnp.concatenate(both).reshape(-1, *halves.shape[1:])
        streams.append(Stream(layout, jnp.concatenate([slabs, halves[at : at + 1]])))
    rot_theirs = layout.shift(rotated, db=1)
    for _ in range(layout.z - 1):
        for stream in streams:
            stream.advance()
    early, late = [], []
    for at, stream in enumerate(streams):
        slabs = [array[-1:] for array in (*stream.ring, *stream.across)]
        received = layout.shift(jnp.concatenate(slabs), db=1)
        if at == 1:
            (received,) = stream.advance((received,))
        else:
            stream.advance()
        early.append(received)
        late.append(layout.shift(received[layout.z - 1 : layout.z], dy=1))
    *fulls, inverses = inverses_of(layout, streams, sizes, early, late)
    parts = bias_of(layout, fulls, inverses, rotated, rot_theirs)
    parts = lax.all_to_all(parts, "chol", 0, 0, tiled=True)
    force_bias, kept, *sent = potential_of(order, fields, parts, cholesky)
    received = [layout.shift(part, db=1) for part in sent]

    rounded, base = first_of([kept], fulls, 0)
    rounded_theirs, base_theirs = first_of(received, fulls, 1)
    streams = [Stream(layout, rounded), Stream(layout, rounded_theirs)]
    for _ in range(layout.z):
        for stream in streams:
            stream.advance()
    sent, full = second_of(layout, received, base_theirs, streams)
    theirs = layout.shift(sent, db=1)
    return place(order, theirs, finish(order, kept, base, full)), force_bias


def solution(mesh):
    in_specs = (
        P("walk", "chol", None),
        P("chol", None),
        P(None, "chol", None),
        P(None, "chol", None),
        P("walk", None),
        P(),
    )
    out_specs = (P("walk", "chol", None), P("walk", None))
    layout = Layout(mesh.shape["walk"], mesh.shape["chol"])
    return jax.shard_map(
        functools.partial(shards, layout),
        mesh=mesh,
        in_specs=in_specs,
        out_specs=out_specs,
        check_vma=False,
    )
```

```python
import functools

import jax
import jax.numpy as jnp
from jax import lax
from jax.experimental import pallas as pl
from jax.experimental.pallas import tpu as pltpu
from jax.sharding import PartitionSpec as P

ITERS = 3
TAU_ROOT = 0.1
BLOCK = 16
HIGHEST = lax.Precision.HIGHEST
MIB = 1024 * 1024

F32 = jnp.float32
BF16 = jnp.bfloat16


def params(mebibytes):
    return pltpu.CompilerParams(vmem_limit_bytes=mebibytes * MIB)


def vmem_specs(count):
    return [pl.BlockSpec(memory_space=pltpu.VMEM)] * count


class Layout:
    def __init__(self, walk_size, chol_size):
        self.walk = walk_size
        self.chol = chol_size
        self.z = chol_size // 4

    def shift(self, array, dz=0, dy=0, db=0):
        pairs = []
        for index in range(self.chol):
            z, y, b = index // 4, (index // 2) % 2, index % 2
            target = (((z + dz) % self.z) * 2 + (y ^ dy)) * 2 + (b ^ db)
            pairs.append((index, target))
        return lax.ppermute(array, "chol", pairs)

    def flip(self, array, mask):
        return lax.ppermute(array, "chol", [(i, i ^ mask) for i in range(self.chol)])

    def step(self, array):
        ring = [*range(0, self.z, 2), *reversed(range(1, self.z, 2))]
        target = {z: ring[(at + 1) % self.z] for at, z in enumerate(ring)}
        pairs = [(index, target[index // 4] * 4 + index % 4) for index in range(self.chol)]
        return lax.ppermute(array, "chol", pairs)

    def origin(self, steps, dy):
        index = lax.axis_index("chol")
        z, y = index // 4, lax.rem(index // 2, 2)
        at = jnp.where(lax.rem(z, 2) == 0, z // 2, self.z - (z + 1) // 2)
        at = lax.rem(at + (self.z - steps), self.z)
        z = jnp.where(2 * at < self.z, 2 * at, 2 * (self.z - at) - 1)
        return z * 2 + (y + dy - 2 * y * dy)


class Stream:
    def __init__(self, layout, piece):
        self.layout = layout
        self.ring = [piece]
        self.across = []
        self.last = []

    def moves(self):
        latest = self.ring[-1]
        if len(self.ring) < self.layout.z:
            return [self.layout.shift(latest, dy=1), self.layout.step(latest)]
        half = (latest.shape[0] + 1) // 2
        return [
            self.layout.shift(latest[:half], dy=1),
            self.layout.step(self.across[-1][half:]),
        ]

    def accept(self, moved):
        if len(self.ring) < self.layout.z:
            self.across.append(moved[0])
            self.ring.append(moved[1])
        else:
            self.last = moved

    def advance(self, anchors=()):
        moved = self.moves()
        if anchors or len(self.ring) < self.layout.z:
            anchors, moved = lax.optimization_barrier((anchors, moved))
        self.accept(moved)
        return anchors

    def pieces(self):
        ring = [(array, 0, steps, 0) for steps, array in enumerate(self.ring)]
        across = [(array, 0, steps, 1) for steps, array in enumerate(self.across)]
        lower, upper = self.last
        steps = self.layout.z - 1
        return ring + across + [(lower, 0, steps, 1), (upper, lower.shape[0], steps, 1)]


def operands(streams):
    arrays, slabs = [], []
    for stream in streams:
        slabs.append([])
        for array, first, steps, dy in stream.pieces():
            for at in range(array.shape[0]):
                slabs[-1].append((len(arrays), at, first + at, steps, dy))
            arrays.append(array)
    return arrays, slabs


def product(left, right):
    high, right_high = left.astype(BF16), right.astype(BF16)
    low = (left - high.astype(F32)).astype(BF16)
    right_low = (right - right_high.astype(F32)).astype(BF16)
    return jnp.dot(
        jnp.concatenate([high, high, low], axis=1),
        jnp.concatenate([right_high, right_low, right_high], axis=0),
        preferred_element_type=F32,
    )


def newton_inverses(matrices):
    shape = matrices[0].shape
    same = lax.broadcasted_iota(jnp.int32, shape, 0) == lax.broadcasted_iota(jnp.int32, shape, 1)
    twice = jnp.where(same, 2.0, 0.0).astype(F32)
    estimates = [twice - matrix for matrix in matrices]
    for _ in range(ITERS - 1):
        steps = [twice - product(a, x) for a, x in zip(matrices, estimates)]
        estimates = [product(x, step) for x, step in zip(estimates, steps)]
    return estimates


def inverse_kernel(layout, slabs, counts, *refs):
    streams = len(counts)
    early, late, refs = refs[:streams], refs[streams : 2 * streams], refs[2 * streams :]
    fulls, (out, buffer, turned) = refs[-3 - streams : -3], refs[-3:]
    pieces = refs[: -3 - streams]
    rows, electrons = early[0].shape[1:]
    b = lax.rem(lax.axis_index("chol"), 2)

    for half, stream in enumerate(slabs):
        place = slice(half * rows, (half + 1) * rows)
        theirs = [(early[half], at) for at in range(early[half].shape[0])] + [(late[half], 0)]
        trial = [slab for slab in stream if slab[2] == 4 * counts[half]]
        for (operand, at, _, steps, dy), (part, number) in zip(trial, theirs):
            origin = layout.origin(steps, dy)
            buffer[origin, b, place] = pieces[operand][at]
            buffer[origin, 1 - b, place] = part[number]
    turned[...] = buffer[...].reshape(-1, electrons).T

    matrices = []
    for full, count, stream in zip(fulls, counts, slabs):
        for operand, at, slab, steps, dy in stream:
            if slab < 4 * count:
                block, walker, half = slab // (2 * count), slab // 2 % count, slab % 2
                place = slice(half * rows, (half + 1) * rows)
                full[walker, layout.origin(steps, dy), block, place] = pieces[operand][at]
        for walker in range(count):
            columns = full[walker].reshape(-1, electrons)
            matrices.append(jnp.dot(turned[...], columns, preferred_element_type=F32))
    for number, inverse in enumerate(newton_inverses(matrices)):
        out[number] = inverse.astype(BF16)


def inverses_of(layout, streams, counts, early, late):
    arrays, slabs = operands(streams)
    _, rows, electrons = early[0].shape
    rows = 2 * rows
    chips = layout.chol // 2
    total = sum(counts)
    return pl.pallas_call(
        functools.partial(inverse_kernel, layout, slabs, counts),
        out_shape=[
            jax.ShapeDtypeStruct((count, chips, 2, rows, electrons), BF16) for count in counts
        ]
        + [jax.ShapeDtypeStruct((total, electrons, electrons), BF16)],
        in_specs=vmem_specs(2 * len(counts) + len(arrays)),
        out_specs=vmem_specs(len(counts) + 1),
        scratch_shapes=[
            pltpu.VMEM((chips, 2, rows, electrons), BF16),
            pltpu.VMEM((electrons, 2 * chips * rows), BF16),
        ],
        compiler_params=params(8),
        cost_estimate=pl.CostEstimate(
            flops=2 * total * electrons**2 * (2 * chips * rows + 6 * (ITERS - 1) * electrons),
            bytes_accessed=4 * (total + 1) * 2 * chips * rows * electrons,
            transcendentals=0,
        ),
    )(*early, *late, *arrays)


def bias_kernel(counts, rot_mine, rot_theirs, inverses, *refs):
    fulls, (out, greens) = refs[:-2], refs[-2:]
    vectors, rows, electrons = rot_mine.shape
    index = lax.axis_index("chol")
    chip, b = index // 2, lax.rem(index, 2)
    walkers = [(full, at) for full, count in zip(fulls, counts) for at in range(count)]
    for number, (full, walker) in enumerate(walkers):
        both = full[walker, chip].reshape(2 * rows, electrons)
        green = jnp.dot(both, inverses[number], preferred_element_type=F32).astype(BF16)
        greens[:, :, number] = green.reshape(2, rows // BLOCK, BLOCK, electrons)
    width = len(walkers) * BLOCK
    total = jnp.zeros((vectors * BLOCK, width), F32)
    for half, rot in ((b, rot_mine), (1 - b, rot_theirs)):
        for block in range(rows // BLOCK):
            total += lax.dot_general(
                rot[:, block * BLOCK : (block + 1) * BLOCK, :].reshape(vectors * BLOCK, electrons),
                greens[half, block].reshape(width, electrons),
                (((1,), (1,)), ((), ())),
                preferred_element_type=F32,
            )
    same = lax.rem(lax.broadcasted_iota(jnp.int32, total.shape, 0), BLOCK) == lax.rem(
        lax.broadcasted_iota(jnp.int32, total.shape, 1), BLOCK
    )
    summed = jnp.sum(jnp.where(same, total, 0.0).reshape(vectors, BLOCK, width), axis=1)
    shape = (len(walkers), width)
    pick = (
        lax.broadcasted_iota(jnp.int32, shape, 1) // BLOCK
        == lax.broadcasted_iota(jnp.int32, shape, 0)
    ).astype(F32)
    bias = lax.dot_general(
        pick, summed, (((1,), (1,)), ((), ())), precision=HIGHEST, preferred_element_type=F32
    )
    out[...] = jnp.zeros_like(out)
    for index in range(out.shape[0]):
        out[index, : len(walkers), :vectors] = bias


def bias_of(layout, fulls, inverses, rot_mine, rot_theirs):
    vectors, rows, electrons = rot_mine.shape
    counts = [full.shape[0] for full in fulls]
    total = sum(counts)
    return pl.pallas_call(
        functools.partial(bias_kernel, counts),
        out_shape=jax.ShapeDtypeStruct(
            (layout.chol, pl.cdiv(total, 8) * 8, pl.cdiv(vectors, 128) * 128), F32
        ),
        in_specs=vmem_specs(3 + len(fulls)),
        out_specs=pl.BlockSpec(memory_space=pltpu.VMEM),
        scratch_shapes=[pltpu.VMEM((2, rows // BLOCK, total, BLOCK, electrons), BF16)],
        compiler_params=params(8),
        cost_estimate=pl.CostEstimate(
            flops=4 * total * rows * electrons * (electrons + vectors * BLOCK),
            bytes_accessed=4 * (vectors + total) * rows * electrons,
            transcendentals=0,
        ),
    )(rot_mine, rot_theirs, inverses, *fulls)


def potential_kernel(order, fields, parts, cholesky, *refs):
    bias_out, kept, *sent, weights = refs
    per_group, vectors = fields.shape
    half, piece = kept.shape[0], sent[0].shape[1]
    b = lax.rem(lax.axis_index("chol"), 2)
    row = lax.broadcasted_iota(jnp.int32, (per_group, vectors), 0)
    bias = jnp.zeros((per_group, vectors), F32)
    for core in range(2):
        total = parts[core]
        for index in range(core + 2, parts.shape[0], 2):
            total = total + parts[index]
        for walker in range(half):
            slot = order[core * half + walker]
            bias += jnp.where(row == slot, total[walker : walker + 1, :vectors], 0.0)
    bias = TAU_ROOT * bias
    bias_out[...] = bias
    shifted = (fields[...] - bias).astype(BF16)
    slot = jnp.zeros((per_group * BLOCK, 1), jnp.int32)
    place = lax.broadcasted_iota(jnp.int32, slot.shape, 0) // BLOCK
    for at in range(per_group):
        slot = jnp.where(place == at, order[lax.rem(at + b * half, per_group)], slot)
    tall = (per_group * BLOCK, per_group)
    rows = (lax.broadcasted_iota(jnp.int32, tall, 1) == slot).astype(BF16)
    wide = (vectors, vectors * BLOCK)
    columns = (
        lax.broadcasted_iota(jnp.int32, wide, 1) // BLOCK
        == lax.broadcasted_iota(jnp.int32, wide, 0)
    ).astype(BF16)
    spread = jnp.dot(rows, shifted, preferred_element_type=F32).astype(BF16)
    spread = jnp.dot(spread, columns, preferred_element_type=F32)
    same = lax.rem(lax.broadcasted_iota(jnp.int32, spread.shape, 0), BLOCK) == lax.rem(
        lax.broadcasted_iota(jnp.int32, spread.shape, 1), BLOCK
    )
    weights[...] = jnp.where(same, spread, 0.0).astype(BF16)
    rows, orbitals = cholesky.shape[1:]
    for at in range(0, rows, BLOCK):
        columns = cholesky[:, at : at + BLOCK, :].reshape(vectors * BLOCK, orbitals)
        result = TAU_ROOT * jnp.dot(weights[...], columns, preferred_element_type=F32)
        result = result.astype(BF16).reshape(2 * half, BLOCK, orbitals)
        kept[:, at : at + BLOCK, :] = result[:half]
        start = at % piece
        sent[at // piece][:, start : start + BLOCK, :] = result[half:]


def potential_of(order, fields, parts, cholesky):
    per_group, vectors = fields.shape
    half = per_group // 2
    _, rows, orbitals = cholesky.shape
    sent = jax.ShapeDtypeStruct((half, rows // 2, orbitals), BF16)
    return pl.pallas_call(
        potential_kernel,
        out_shape=[
            jax.ShapeDtypeStruct((per_group, vectors), F32),
            jax.ShapeDtypeStruct((half, rows, orbitals), BF16),
            sent,
            sent,
        ],
        in_specs=[pl.BlockSpec(memory_space=pltpu.SMEM)] + vmem_specs(3),
        out_specs=vmem_specs(4),
        scratch_shapes=[pltpu.VMEM((per_group * BLOCK, vectors * BLOCK), BF16)],
        compiler_params=params(12),
    )(order, fields, parts, cholesky)


def first_kernel(sibling, parts, *refs):
    potential, fulls, (rounded, base) = refs[:parts], refs[parts:-2], refs[-2:]
    b = lax.rem(lax.axis_index("chol"), 2)
    chip = lax.axis_index("chol") // 2
    count = 0
    for full in fulls:
        for walker in range(full.shape[0]):
            rows = jnp.concatenate([part[count] for part in potential], axis=0)
            columns = full[walker].reshape(-1, full.shape[-1])
            term = jnp.dot(rows, columns, preferred_element_type=F32)
            rounded[count] = term.astype(BF16)
            own = full[walker, chip, 1 - b if sibling else b]
            base[count] = own.astype(F32) + term
            count += 1


def first_of(potential, fulls, sibling):
    half, _, orbitals = potential[0].shape
    rows, electrons = fulls[0].shape[-2:]
    shape = (half, rows, electrons)
    return pl.pallas_call(
        functools.partial(first_kernel, sibling, len(potential)),
        out_shape=[jax.ShapeDtypeStruct(shape, BF16), jax.ShapeDtypeStruct(shape, F32)],
        in_specs=vmem_specs(len(potential) + len(fulls)),
        out_specs=vmem_specs(2),
        compiler_params=params(8),
        cost_estimate=pl.CostEstimate(
            flops=2 * half * rows * orbitals * electrons,
            bytes_accessed=2 * half * orbitals * (rows + electrons),
            transcendentals=0,
        ),
    )(*potential, *fulls)


def second_kernel(layout, slabs, parts, *refs):
    potential, base, pieces = refs[:parts], refs[parts], refs[parts + 1 : -2]
    out, full = refs[-2:]
    b = lax.rem(lax.axis_index("chol"), 2)
    for block, stream in zip((b, 1 - b), slabs):
        for operand, at, walker, steps, dy in stream:
            full[walker, layout.origin(steps, dy), block] = pieces[operand][at]
    for walker in range(out.shape[0]):
        rows = jnp.concatenate([part[walker] for part in potential], axis=0)
        columns = full[walker].reshape(-1, full.shape[-1])
        term = jnp.dot(rows, columns, preferred_element_type=F32)
        out[walker] = (base[walker] + 0.5 * term).astype(BF16)


def second_of(layout, potential, base, streams):
    arrays, slabs = operands(streams)
    orbitals = potential[0].shape[2]
    half, rows, electrons = base.shape
    return pl.pallas_call(
        functools.partial(second_kernel, layout, slabs, len(potential)),
        out_shape=[
            jax.ShapeDtypeStruct((half, rows, electrons), BF16),
            jax.ShapeDtypeStruct((half, layout.chol // 2, 2, rows, electrons), BF16),
        ],
        in_specs=vmem_specs(len(potential) + 1 + len(arrays)),
        out_specs=vmem_specs(2),
        compiler_params=params(8),
        cost_estimate=pl.CostEstimate(
            flops=2 * half * rows * orbitals * electrons,
            bytes_accessed=2 * half * orbitals * (rows + 3 * electrons),
            transcendentals=0,
        ),
    )(*potential, base, *arrays)


def finish_kernel(potential, base, full, out):
    for walker in range(out.shape[0]):
        columns = full[walker].reshape(-1, full.shape[-1])
        term = jnp.dot(potential[walker], columns, preferred_element_type=F32)
        out[walker] = (base[walker] + 0.5 * term).astype(BF16)


def finish(potential, base, full):
    half, rows, electrons = base.shape
    orbitals = potential.shape[2]
    return pl.pallas_call(
        finish_kernel,
        out_shape=jax.ShapeDtypeStruct((half, rows, electrons), BF16),
        in_specs=vmem_specs(3),
        out_specs=pl.BlockSpec(memory_space=pltpu.VMEM),
        compiler_params=params(8),
        cost_estimate=pl.CostEstimate(
            flops=2 * half * rows * orbitals * electrons,
            bytes_accessed=2 * half * orbitals * (rows + electrons),
            transcendentals=0,
        ),
    )(potential, base, full)


def place_kernel(order, mine, theirs, out, semaphores):
    half = mine.shape[0]
    b = lax.rem(lax.axis_index("chol"), 2)
    copies = []
    for part, core in ((mine, b), (theirs, 1 - b)):
        for walker in range(half):
            target = out.at[order[core * half + walker]]
            copies.append(
                pltpu.make_async_copy(part.at[walker], target, semaphores.at[len(copies)])
            )
    for copy in copies:
        copy.start()
    for copy in copies:
        copy.wait()


def place(order, mine, theirs):
    half, rows, electrons = mine.shape
    return pl.pallas_call(
        place_kernel,
        out_shape=jax.ShapeDtypeStruct((2 * half, rows, electrons), BF16),
        in_specs=[pl.BlockSpec(memory_space=pltpu.SMEM)] + vmem_specs(2),
        out_specs=pl.BlockSpec(memory_space=pl.ANY),
        scratch_shapes=[pltpu.SemaphoreType.DMA((2 * half,))],
        compiler_params=params(4),
    )(order, mine, theirs)


def split_kernel(source, walkers, *refs):
    targets, (order, picked, semaphores) = refs[:4], refs[4:]
    per_group = walkers.shape[0]
    half = per_group // 2
    share = half // 2
    group = lax.axis_index("walk")
    b = lax.rem(lax.axis_index("chol"), 2)
    stayed, arrived, sent = jnp.int32(0), jnp.int32(0), jnp.int32(0)
    for slot in range(per_group):
        local = source[group * per_group + slot] - group * per_group
        stays = ((local >= 0) & (local < per_group)).astype(jnp.int32)
        picked[jnp.where(stays == 1, jnp.minimum(stayed, half - 1), per_group)] = local
        rank = jnp.minimum(jnp.where(stays == 1, stayed, arrived), half - 1)
        core = rank // share
        order[core * half + stays * share + rank - core * share] = jnp.int32(slot)
        stayed, arrived = stayed + stays, arrived + 1 - stays
        local = source[(1 - group) * per_group + slot] - group * per_group
        goes = ((local >= 0) & (local < per_group)).astype(jnp.int32)
        picked[jnp.where(goes == 1, half + jnp.minimum(sent, half - 1), per_group)] = local
        sent = sent + goes
    offsets = (b * share, (1 - b) * share, half + b * share, half + (1 - b) * share)
    copies = []
    for target, offset in reversed(list(zip(targets, offsets))):
        for walker in range(share):
            copies.append(
                pltpu.make_async_copy(
                    walkers.at[picked[offset + walker]],
                    target.at[walker],
                    semaphores.at[len(copies)],
                )
            )
    for copy in copies:
        copy.start()
    for copy in copies:
        copy.wait()


def split_walkers(walkers, source):
    per_group, rows, electrons = walkers.shape
    share = jax.ShapeDtypeStruct((per_group // 4, rows, electrons), walkers.dtype)
    return pl.pallas_call(
        split_kernel,
        out_shape=[share] * 4 + [jax.ShapeDtypeStruct((per_group,), jnp.int32)],
        in_specs=[pl.BlockSpec(memory_space=pltpu.SMEM), pl.BlockSpec(memory_space=pl.ANY)],
        out_specs=[pl.BlockSpec(memory_space=pl.ANY)] * 4
        + [pl.BlockSpec(memory_space=pltpu.SMEM)],
        scratch_shapes=[
            pltpu.SMEM((per_group + 1,), jnp.int32),
            pltpu.SemaphoreType.DMA((per_group,)),
        ],
        compiler_params=params(60),
    )(source, walkers)


def ranks(flags):
    count = flags.shape[-1]
    before = jnp.arange(count)[None, :] < jnp.arange(count)[:, None]
    return jnp.sum(jnp.where(before & flags[..., None, :], 1, 0), axis=-1)


def migrate(layout, walkers, source):
    per_group = walkers.shape[0]
    half = per_group // 2
    group = lax.axis_index("walk")
    if layout.walk == 2 and half % 2 == 0:
        stay, stay_sent, near, cross, order = split_walkers(walkers, source)
        count = 2 * layout.chol
        across = [(index + layout.chol) % count for index in range(count)]
        axes = ("walk", "chol")
        near = lax.ppermute(near, axes, list(enumerate(across)))
        cross = lax.ppermute(cross, axes, [(i, j ^ 1) for i, j in enumerate(across)])
        return [(near, cross), (stay, layout.shift(stay_sent, db=1))], order
    table = source.reshape(layout.walk, per_group)
    incoming = lax.dynamic_index_in_dim(table, group, 0, keepdims=False)
    incoming_groups = incoming // per_group

    def outgoing(distance):
        row = lax.dynamic_index_in_dim(table, (group + distance) % layout.walk, 0, keepdims=False)
        local = row - group * per_group
        here = (local >= 0) & (local < per_group)
        match = here[None, :] & (ranks(here)[None, :] == jnp.arange(half)[:, None])
        return jnp.take(walkers, jnp.sum(jnp.where(match, local[None, :], 0), axis=1), axis=0)

    arrived = [outgoing(0)]
    for distance in range(1, layout.walk):
        pairs = [(g, (g + distance) % layout.walk) for g in range(layout.walk)]
        arrived.append(lax.ppermute(outgoing(distance), "walk", pairs))
    slots = jnp.arange(per_group)
    same = (incoming_groups[:, None] == incoming_groups[None, :]) & (slots[None, :] < slots[:, None])
    rank = jnp.sum(same.astype(jnp.int32), axis=1)
    distance = (group - incoming_groups) % layout.walk
    migrated = jnp.take(jnp.concatenate(arrived, axis=0), distance * half + rank, axis=0)
    b = lax.axis_index("chol") % 2
    mine = lax.dynamic_slice_in_dim(migrated, b * half, half, 0)
    theirs = lax.dynamic_slice_in_dim(migrated, (1 - b) * half, half, 0)
    theirs = layout.shift(theirs, db=1)
    share = half // 2
    shares = [(mine[:share], theirs[:share]), (mine[share:], theirs[share:])]
    return shares, slots.astype(jnp.int32)


def shards(layout, walkers, trial, cholesky, rotated, fields, source):
    b = lax.axis_index("chol") % 2
    shares, order = migrate(layout, walkers, source)
    sizes = [own.shape[0] for own, _ in shares]
    halves = trial.reshape(2, -1, trial.shape[1])
    streams = []
    for at, (own, other) in enumerate(shares):
        both = (jnp.where(b == 0, own, other), jnp.where(b == 0, other, own))
        slabs = jnp.concatenate(both).reshape(-1, *halves.shape[1:])
        streams.append(Stream(layout, jnp.concatenate([slabs, halves[at : at + 1]])))
    rot_theirs = layout.shift(rotated, db=1)
    for _ in range(layout.z - 1):
        for stream in streams:
            stream.advance()
    early, late = [], []
    for at, stream in enumerate(streams):
        slabs = [array[-1:] for array in (*stream.ring, *stream.across)]
        received = layout.shift(jnp.concatenate(slabs), db=1)
        if at == 1:
            (received,) = stream.advance((received,))
        else:
            stream.advance()
        early.append(received)
        late.append(layout.shift(received[layout.z - 1 : layout.z], dy=1))
    *fulls, inverses = inverses_of(layout, streams, sizes, early, late)
    parts = bias_of(layout, fulls, inverses, rotated, rot_theirs)
    parts = lax.all_to_all(parts, "chol", 0, 0, tiled=True)
    force_bias, kept, *sent = potential_of(order, fields, parts, cholesky)
    received = [layout.shift(part, db=1) for part in sent]

    rounded, base = first_of([kept], fulls, 0)
    rounded_theirs, base_theirs = first_of(received, fulls, 1)
    streams = [Stream(layout, rounded), Stream(layout, rounded_theirs)]
    for _ in range(layout.z):
        for stream in streams:
            stream.advance()
    sent, full = second_of(layout, received, base_theirs, streams)
    theirs = layout.shift(sent, db=1)
    return place(order, finish(kept, base, full), theirs), force_bias


def solution(mesh):
    in_specs = (
        P("walk", "chol", None),
        P("chol", None),
        P(None, "chol", None),
        P(None, "chol", None),
        P("walk", None),
        P(),
    )
    out_specs = (P("walk", "chol", None), P("walk", None))
    layout = Layout(mesh.shape["walk"], mesh.shape["chol"])
    return jax.shard_map(
        functools.partial(shards, layout),
        mesh=mesh,
        in_specs=in_specs,
        out_specs=out_specs,
        check_vma=False,
    )
```

```python
import functools

import jax
import jax.numpy as jnp
from jax import lax
from jax.experimental import pallas as pl
from jax.experimental.pallas import tpu as pltpu
from jax.sharding import PartitionSpec as P

ITERS = 3
TAU_ROOT = 0.1
BLOCK = 16
HIGHEST = lax.Precision.HIGHEST
MIB = 1024 * 1024

F32 = jnp.float32
BF16 = jnp.bfloat16


def params(mebibytes):
    return pltpu.CompilerParams(vmem_limit_bytes=mebibytes * MIB)


def vmem_specs(count):
    return [pl.BlockSpec(memory_space=pltpu.VMEM)] * count


class Layout:
    def __init__(self, walk_size, chol_size):
        self.walk = walk_size
        self.chol = chol_size
        self.z = chol_size // 4

    def shift(self, array, dz=0, dy=0, db=0):
        pairs = []
        for index in range(self.chol):
            z, y, b = index // 4, (index // 2) % 2, index % 2
            target = (((z + dz) % self.z) * 2 + (y ^ dy)) * 2 + (b ^ db)
            pairs.append((index, target))
        return lax.ppermute(array, "chol", pairs)

    def flip(self, array, mask):
        return lax.ppermute(array, "chol", [(i, i ^ mask) for i in range(self.chol)])

    def step(self, array):
        ring = [*range(0, self.z, 2), *reversed(range(1, self.z, 2))]
        target = {z: ring[(at + 1) % self.z] for at, z in enumerate(ring)}
        pairs = [(index, target[index // 4] * 4 + index % 4) for index in range(self.chol)]
        return lax.ppermute(array, "chol", pairs)

    def origin(self, steps, dy):
        index = lax.axis_index("chol")
        z, y = index // 4, lax.rem(index // 2, 2)
        at = jnp.where(lax.rem(z, 2) == 0, z // 2, self.z - (z + 1) // 2)
        at = lax.rem(at + (self.z - steps), self.z)
        z = jnp.where(2 * at < self.z, 2 * at, 2 * (self.z - at) - 1)
        return z * 2 + (y + dy - 2 * y * dy)


class Stream:
    def __init__(self, layout, piece):
        self.layout = layout
        self.ring = [piece]
        self.across = []
        self.last = []

    def moves(self):
        latest = self.ring[-1]
        if len(self.ring) < self.layout.z:
            return [self.layout.shift(latest, dy=1), self.layout.step(latest)]
        half = (latest.shape[0] + 1) // 2
        return [
            self.layout.shift(latest[:half], dy=1),
            self.layout.step(self.across[-1][half:]),
        ]

    def accept(self, moved):
        if len(self.ring) < self.layout.z:
            self.across.append(moved[0])
            self.ring.append(moved[1])
        else:
            self.last = moved

    def advance(self, anchors=()):
        moved = self.moves()
        if anchors or len(self.ring) < self.layout.z:
            anchors, moved = lax.optimization_barrier((anchors, moved))
        self.accept(moved)
        return anchors

    def pieces(self):
        ring = [(array, 0, steps, 0) for steps, array in enumerate(self.ring)]
        across = [(array, 0, steps, 1) for steps, array in enumerate(self.across)]
        lower, upper = self.last
        steps = self.layout.z - 1
        return ring + across + [(lower, 0, steps, 1), (upper, lower.shape[0], steps, 1)]


def operands(streams):
    arrays, slabs = [], []
    for stream in streams:
        slabs.append([])
        for array, first, steps, dy in stream.pieces():
            for at in range(array.shape[0]):
                slabs[-1].append((len(arrays), at, first + at, steps, dy))
            arrays.append(array)
    return arrays, slabs


def lay_out_kernel(half, own, other, trial, out):
    count, rows = own.shape[0], own.shape[1] // 2
    b = lax.rem(lax.axis_index("chol"), 2)
    for block, part in ((b, own), (1 - b, other)):
        for walker in range(count):
            for at in range(2):
                place = slice(at * rows, (at + 1) * rows)
                out[(block * count + walker) * 2 + at] = part[walker, place]
    out[4 * count] = trial[half * rows : (half + 1) * rows]


def laid_out(own, other, trial, half):
    count, rows, electrons = own.shape
    return pl.pallas_call(
        functools.partial(lay_out_kernel, half),
        out_shape=jax.ShapeDtypeStruct((4 * count + 1, rows // 2, electrons), own.dtype),
        in_specs=vmem_specs(3),
        out_specs=pl.BlockSpec(memory_space=pltpu.VMEM),
        compiler_params=params(4),
    )(own, other, trial)


def product(left, right):
    high, right_high = left.astype(BF16), right.astype(BF16)
    low = (left - high.astype(F32)).astype(BF16)
    right_low = (right - right_high.astype(F32)).astype(BF16)
    return jnp.dot(
        jnp.concatenate([high, high, low], axis=1),
        jnp.concatenate([right_high, right_low, right_high], axis=0),
        preferred_element_type=F32,
    )


def newton_inverses(matrices):
    shape = matrices[0].shape
    same = lax.broadcasted_iota(jnp.int32, shape, 0) == lax.broadcasted_iota(jnp.int32, shape, 1)
    twice = jnp.where(same, 2.0, 0.0).astype(F32)
    estimates = [twice - matrix for matrix in matrices]
    for _ in range(ITERS - 1):
        steps = [twice - product(a, x) for a, x in zip(matrices, estimates)]
        estimates = [product(x, step) for x, step in zip(estimates, steps)]
    return estimates


def inverse_kernel(layout, slabs, counts, *refs):
    streams = len(counts)
    early, late, refs = refs[:streams], refs[streams : 2 * streams], refs[2 * streams :]
    fulls, (out, buffer, turned) = refs[-3 - streams : -3], refs[-3:]
    pieces = refs[: -3 - streams]
    rows, electrons = early[0].shape[1:]
    b = lax.rem(lax.axis_index("chol"), 2)

    for half, stream in enumerate(slabs):
        place = slice(half * rows, (half + 1) * rows)
        theirs = [(early[half], at) for at in range(early[half].shape[0])] + [(late[half], 0)]
        trial = [slab for slab in stream if slab[2] == 4 * counts[half]]
        for (operand, at, _, steps, dy), (part, number) in zip(trial, theirs):
            origin = layout.origin(steps, dy)
            buffer[origin, b, place] = pieces[operand][at]
            buffer[origin, 1 - b, place] = part[number]
    turned[...] = buffer[...].reshape(-1, electrons).T

    matrices = []
    for full, count, stream in zip(fulls, counts, slabs):
        for operand, at, slab, steps, dy in stream:
            if slab < 4 * count:
                block, walker, half = slab // (2 * count), slab // 2 % count, slab % 2
                place = slice(half * rows, (half + 1) * rows)
                full[walker, layout.origin(steps, dy), block, place] = pieces[operand][at]
        for walker in range(count):
            columns = full[walker].reshape(-1, electrons)
            matrices.append(jnp.dot(turned[...], columns, preferred_element_type=F32))
    for number, inverse in enumerate(newton_inverses(matrices)):
        out[number] = inverse.astype(BF16)


def inverses_of(layout, streams, counts, early, late):
    arrays, slabs = operands(streams)
    _, rows, electrons = early[0].shape
    rows = 2 * rows
    chips = layout.chol // 2
    total = sum(counts)
    return pl.pallas_call(
        functools.partial(inverse_kernel, layout, slabs, counts),
        out_shape=[
            jax.ShapeDtypeStruct((count, chips, 2, rows, electrons), BF16) for count in counts
        ]
        + [jax.ShapeDtypeStruct((total, electrons, electrons), BF16)],
        in_specs=vmem_specs(2 * len(counts) + len(arrays)),
        out_specs=vmem_specs(len(counts) + 1),
        scratch_shapes=[
            pltpu.VMEM((chips, 2, rows, electrons), BF16),
            pltpu.VMEM((electrons, 2 * chips * rows), BF16),
        ],
        compiler_params=params(8),
        cost_estimate=pl.CostEstimate(
            flops=2 * total * electrons**2 * (2 * chips * rows + 6 * (ITERS - 1) * electrons),
            bytes_accessed=4 * (total + 1) * 2 * chips * rows * electrons,
            transcendentals=0,
        ),
    )(*early, *late, *arrays)


def bias_kernel(counts, rot_mine, rot_theirs, inverses, *refs):
    fulls, (out, greens) = refs[:-2], refs[-2:]
    vectors, rows, electrons = rot_mine.shape
    index = lax.axis_index("chol")
    chip, b = index // 2, lax.rem(index, 2)
    walkers = [(full, at) for full, count in zip(fulls, counts) for at in range(count)]
    for number, (full, walker) in enumerate(walkers):
        both = full[walker, chip].reshape(2 * rows, electrons)
        green = jnp.dot(both, inverses[number], preferred_element_type=F32).astype(BF16)
        greens[:, :, number] = green.reshape(2, rows // BLOCK, BLOCK, electrons)
    width = len(walkers) * BLOCK
    total = jnp.zeros((vectors * BLOCK, width), F32)
    for half, rot in ((b, rot_mine), (1 - b, rot_theirs)):
        for block in range(rows // BLOCK):
            total += lax.dot_general(
                rot[:, block * BLOCK : (block + 1) * BLOCK, :].reshape(vectors * BLOCK, electrons),
                greens[half, block].reshape(width, electrons),
                (((1,), (1,)), ((), ())),
                preferred_element_type=F32,
            )
    same = lax.rem(lax.broadcasted_iota(jnp.int32, total.shape, 0), BLOCK) == lax.rem(
        lax.broadcasted_iota(jnp.int32, total.shape, 1), BLOCK
    )
    summed = jnp.sum(jnp.where(same, total, 0.0).reshape(vectors, BLOCK, width), axis=1)
    shape = (len(walkers), width)
    pick = (
        lax.broadcasted_iota(jnp.int32, shape, 1) // BLOCK
        == lax.broadcasted_iota(jnp.int32, shape, 0)
    ).astype(F32)
    bias = lax.dot_general(
        pick, summed, (((1,), (1,)), ((), ())), precision=HIGHEST, preferred_element_type=F32
    )
    out[...] = jnp.zeros_like(out)
    for index in range(out.shape[0]):
        out[index, : len(walkers), :vectors] = bias


def bias_of(layout, fulls, inverses, rot_mine, rot_theirs):
    vectors, rows, electrons = rot_mine.shape
    counts = [full.shape[0] for full in fulls]
    total = sum(counts)
    return pl.pallas_call(
        functools.partial(bias_kernel, counts),
        out_shape=jax.ShapeDtypeStruct(
            (layout.chol, pl.cdiv(total, 8) * 8, pl.cdiv(vectors, 128) * 128), F32
        ),
        in_specs=vmem_specs(3 + len(fulls)),
        out_specs=pl.BlockSpec(memory_space=pltpu.VMEM),
        scratch_shapes=[pltpu.VMEM((2, rows // BLOCK, total, BLOCK, electrons), BF16)],
        compiler_params=params(8),
        cost_estimate=pl.CostEstimate(
            flops=4 * total * rows * electrons * (electrons + vectors * BLOCK),
            bytes_accessed=4 * (vectors + total) * rows * electrons,
            transcendentals=0,
        ),
    )(rot_mine, rot_theirs, inverses, *fulls)


def potential_kernel(order, fields, parts, cholesky, *refs):
    bias_out, kept, *sent, weights = refs
    per_group, vectors = fields.shape
    half, piece = kept.shape[0], sent[0].shape[1]
    b = lax.rem(lax.axis_index("chol"), 2)
    row = lax.broadcasted_iota(jnp.int32, (per_group, vectors), 0)
    bias = jnp.zeros((per_group, vectors), F32)
    for core in range(2):
        total = parts[core]
        for index in range(core + 2, parts.shape[0], 2):
            total = total + parts[index]
        for walker in range(half):
            slot = order[core * half + walker]
            bias += jnp.where(row == slot, total[walker : walker + 1, :vectors], 0.0)
    bias = TAU_ROOT * bias
    bias_out[...] = bias
    shifted = (fields[...] - bias).astype(BF16)
    slot = jnp.zeros((per_group * BLOCK, 1), jnp.int32)
    place = lax.broadcasted_iota(jnp.int32, slot.shape, 0) // BLOCK
    for at in range(per_group):
        slot = jnp.where(place == at, order[lax.rem(at + b * half, per_group)], slot)
    tall = (per_group * BLOCK, per_group)
    rows = (lax.broadcasted_iota(jnp.int32, tall, 1) == slot).astype(BF16)
    wide = (vectors, vectors * BLOCK)
    columns = (
        lax.broadcasted_iota(jnp.int32, wide, 1) // BLOCK
        == lax.broadcasted_iota(jnp.int32, wide, 0)
    ).astype(BF16)
    spread = jnp.dot(rows, shifted, preferred_element_type=F32).astype(BF16)
    spread = jnp.dot(spread, columns, preferred_element_type=F32)
    same = lax.rem(lax.broadcasted_iota(jnp.int32, spread.shape, 0), BLOCK) == lax.rem(
        lax.broadcasted_iota(jnp.int32, spread.shape, 1), BLOCK
    )
    weights[...] = jnp.where(same, spread, 0.0).astype(BF16)
    rows, orbitals = cholesky.shape[1:]
    for at in range(0, rows, BLOCK):
        columns = cholesky[:, at : at + BLOCK, :].reshape(vectors * BLOCK, orbitals)
        result = TAU_ROOT * jnp.dot(weights[...], columns, preferred_element_type=F32)
        result = result.astype(BF16).reshape(2 * half, BLOCK, orbitals)
        kept[:, at : at + BLOCK, :] = result[:half]
        start = at % piece
        sent[at // piece][:, start : start + BLOCK, :] = result[half:]


def potential_of(order, fields, parts, cholesky):
    per_group, vectors = fields.shape
    half = per_group // 2
    _, rows, orbitals = cholesky.shape
    sent = jax.ShapeDtypeStruct((half, rows // 2, orbitals), BF16)
    return pl.pallas_call(
        potential_kernel,
        out_shape=[
            jax.ShapeDtypeStruct((per_group, vectors), F32),
            jax.ShapeDtypeStruct((half, rows, orbitals), BF16),
            sent,
            sent,
        ],
        in_specs=[pl.BlockSpec(memory_space=pltpu.SMEM)] + vmem_specs(3),
        out_specs=vmem_specs(4),
        scratch_shapes=[pltpu.VMEM((per_group * BLOCK, vectors * BLOCK), BF16)],
        compiler_params=params(12),
    )(order, fields, parts, cholesky)


def first_kernel(sibling, parts, *refs):
    potential, fulls, (rounded, base) = refs[:parts], refs[parts:-2], refs[-2:]
    b = lax.rem(lax.axis_index("chol"), 2)
    chip = lax.axis_index("chol") // 2
    count = 0
    for full in fulls:
        for walker in range(full.shape[0]):
            rows = jnp.concatenate([part[count] for part in potential], axis=0)
            columns = full[walker].reshape(-1, full.shape[-1])
            term = jnp.dot(rows, columns, preferred_element_type=F32)
            rounded[count] = term.astype(BF16)
            own = full[walker, chip, 1 - b if sibling else b]
            base[count] = own.astype(F32) + term
            count += 1


def first_of(potential, fulls, sibling):
    half, _, orbitals = potential[0].shape
    rows, electrons = fulls[0].shape[-2:]
    shape = (half, rows, electrons)
    return pl.pallas_call(
        functools.partial(first_kernel, sibling, len(potential)),
        out_shape=[jax.ShapeDtypeStruct(shape, BF16), jax.ShapeDtypeStruct(shape, F32)],
        in_specs=vmem_specs(len(potential) + len(fulls)),
        out_specs=vmem_specs(2),
        compiler_params=params(8),
        cost_estimate=pl.CostEstimate(
            flops=2 * half * rows * orbitals * electrons,
            bytes_accessed=2 * half * orbitals * (rows + electrons),
            transcendentals=0,
        ),
    )(*potential, *fulls)


def second_kernel(layout, slabs, parts, *refs):
    potential, base, pieces = refs[:parts], refs[parts], refs[parts + 1 : -2]
    out, full = refs[-2:]
    b = lax.rem(lax.axis_index("chol"), 2)
    for block, stream in zip((b, 1 - b), slabs):
        for operand, at, walker, steps, dy in stream:
            full[walker, layout.origin(steps, dy), block] = pieces[operand][at]
    for walker in range(out.shape[0]):
        rows = jnp.concatenate([part[walker] for part in potential], axis=0)
        columns = full[walker].reshape(-1, full.shape[-1])
        term = jnp.dot(rows, columns, preferred_element_type=F32)
        out[walker] = (base[walker] + 0.5 * term).astype(BF16)


def second_of(layout, potential, base, streams):
    arrays, slabs = operands(streams)
    orbitals = potential[0].shape[2]
    half, rows, electrons = base.shape
    return pl.pallas_call(
        functools.partial(second_kernel, layout, slabs, len(potential)),
        out_shape=[
            jax.ShapeDtypeStruct((half, rows, electrons), BF16),
            jax.ShapeDtypeStruct((half, layout.chol // 2, 2, rows, electrons), BF16),
        ],
        in_specs=vmem_specs(len(potential) + 1 + len(arrays)),
        out_specs=vmem_specs(2),
        compiler_params=params(8),
        cost_estimate=pl.CostEstimate(
            flops=2 * half * rows * orbitals * electrons,
            bytes_accessed=2 * half * orbitals * (rows + 3 * electrons),
            transcendentals=0,
        ),
    )(*potential, base, *arrays)


def finish_kernel(potential, base, full, out):
    for walker in range(out.shape[0]):
        columns = full[walker].reshape(-1, full.shape[-1])
        term = jnp.dot(potential[walker], columns, preferred_element_type=F32)
        out[walker] = (base[walker] + 0.5 * term).astype(BF16)


def finish(potential, base, full):
    half, rows, electrons = base.shape
    orbitals = potential.shape[2]
    return pl.pallas_call(
        finish_kernel,
        out_shape=jax.ShapeDtypeStruct((half, rows, electrons), BF16),
        in_specs=vmem_specs(3),
        out_specs=pl.BlockSpec(memory_space=pltpu.VMEM),
        compiler_params=params(8),
        cost_estimate=pl.CostEstimate(
            flops=2 * half * rows * orbitals * electrons,
            bytes_accessed=2 * half * orbitals * (rows + electrons),
            transcendentals=0,
        ),
    )(potential, base, full)


def place_kernel(order, mine, theirs, out, semaphores):
    half = mine.shape[0]
    b = lax.rem(lax.axis_index("chol"), 2)
    copies = []
    for part, core in ((mine, b), (theirs, 1 - b)):
        for walker in range(half):
            target = out.at[order[core * half + walker]]
            copies.append(
                pltpu.make_async_copy(part.at[walker], target, semaphores.at[len(copies)])
            )
    for copy in copies:
        copy.start()
    for copy in copies:
        copy.wait()


def place(order, mine, theirs):
    half, rows, electrons = mine.shape
    return pl.pallas_call(
        place_kernel,
        out_shape=jax.ShapeDtypeStruct((2 * half, rows, electrons), BF16),
        in_specs=[pl.BlockSpec(memory_space=pltpu.SMEM)] + vmem_specs(2),
        out_specs=pl.BlockSpec(memory_space=pl.ANY),
        scratch_shapes=[pltpu.SemaphoreType.DMA((2 * half,))],
        compiler_params=params(4),
    )(order, mine, theirs)


def split_kernel(source, walkers, *refs):
    targets, (order, picked, semaphores) = refs[:4], refs[4:]
    per_group = walkers.shape[0]
    half = per_group // 2
    share = half // 2
    group = lax.axis_index("walk")
    b = lax.rem(lax.axis_index("chol"), 2)
    stayed, arrived, sent = jnp.int32(0), jnp.int32(0), jnp.int32(0)
    for slot in range(per_group):
        local = source[group * per_group + slot] - group * per_group
        stays = ((local >= 0) & (local < per_group)).astype(jnp.int32)
        picked[jnp.where(stays == 1, jnp.minimum(stayed, half - 1), per_group)] = local
        rank = jnp.minimum(jnp.where(stays == 1, stayed, arrived), half - 1)
        core = rank // share
        order[core * half + stays * share + rank - core * share] = jnp.int32(slot)
        stayed, arrived = stayed + stays, arrived + 1 - stays
        local = source[(1 - group) * per_group + slot] - group * per_group
        goes = ((local >= 0) & (local < per_group)).astype(jnp.int32)
        picked[jnp.where(goes == 1, half + jnp.minimum(sent, half - 1), per_group)] = local
        sent = sent + goes
    offsets = (b * share, (1 - b) * share, half + b * share, half + (1 - b) * share)
    copies = []
    for target, offset in reversed(list(zip(targets, offsets))):
        for walker in range(share):
            copies.append(
                pltpu.make_async_copy(
                    walkers.at[picked[offset + walker]],
                    target.at[walker],
                    semaphores.at[len(copies)],
                )
            )
    for copy in copies:
        copy.start()
    for copy in copies:
        copy.wait()


def split_walkers(walkers, source):
    per_group, rows, electrons = walkers.shape
    share = jax.ShapeDtypeStruct((per_group // 4, rows, electrons), walkers.dtype)
    return pl.pallas_call(
        split_kernel,
        out_shape=[share] * 4 + [jax.ShapeDtypeStruct((per_group,), jnp.int32)],
        in_specs=[pl.BlockSpec(memory_space=pltpu.SMEM), pl.BlockSpec(memory_space=pl.ANY)],
        out_specs=[pl.BlockSpec(memory_space=pl.ANY)] * 4
        + [pl.BlockSpec(memory_space=pltpu.SMEM)],
        scratch_shapes=[
            pltpu.SMEM((per_group + 1,), jnp.int32),
            pltpu.SemaphoreType.DMA((per_group,)),
        ],
        compiler_params=params(4),
    )(source, walkers)


def ranks(flags):
    count = flags.shape[-1]
    before = jnp.arange(count)[None, :] < jnp.arange(count)[:, None]
    return jnp.sum(jnp.where(before & flags[..., None, :], 1, 0), axis=-1)


def migrate(layout, walkers, source):
    per_group = walkers.shape[0]
    half = per_group // 2
    group = lax.axis_index("walk")
    if layout.walk == 2 and half % 2 == 0:
        stay, stay_sent, near, cross, order = split_walkers(walkers, source)
        count = 2 * layout.chol
        across = [(index + layout.chol) % count for index in range(count)]
        axes = ("walk", "chol")
        near = lax.ppermute(near, axes, list(enumerate(across)))
        cross = lax.ppermute(cross, axes, [(i, j ^ 1) for i, j in enumerate(across)])
        return [(near, cross), (stay, layout.shift(stay_sent, db=1))], order
    table = source.reshape(layout.walk, per_group)
    incoming = lax.dynamic_index_in_dim(table, group, 0, keepdims=False)
    incoming_groups = incoming // per_group

    def outgoing(distance):
        row = lax.dynamic_index_in_dim(table, (group + distance) % layout.walk, 0, keepdims=False)
        local = row - group * per_group
        here = (local >= 0) & (local < per_group)
        match = here[None, :] & (ranks(here)[None, :] == jnp.arange(half)[:, None])
        return jnp.take(walkers, jnp.sum(jnp.where(match, local[None, :], 0), axis=1), axis=0)

    arrived = [outgoing(0)]
    for distance in range(1, layout.walk):
        pairs = [(g, (g + distance) % layout.walk) for g in range(layout.walk)]
        arrived.append(lax.ppermute(outgoing(distance), "walk", pairs))
    slots = jnp.arange(per_group)
    same = (incoming_groups[:, None] == incoming_groups[None, :]) & (slots[None, :] < slots[:, None])
    rank = jnp.sum(same.astype(jnp.int32), axis=1)
    distance = (group - incoming_groups) % layout.walk
    migrated = jnp.take(jnp.concatenate(arrived, axis=0), distance * half + rank, axis=0)
    b = lax.axis_index("chol") % 2
    mine = lax.dynamic_slice_in_dim(migrated, b * half, half, 0)
    theirs = lax.dynamic_slice_in_dim(migrated, (1 - b) * half, half, 0)
    theirs = layout.shift(theirs, db=1)
    share = half // 2
    shares = [(mine[:share], theirs[:share]), (mine[share:], theirs[share:])]
    return shares, slots.astype(jnp.int32)


def shards(layout, walkers, trial, cholesky, rotated, fields, source):
    shares, order = migrate(layout, walkers, source)
    sizes = [own.shape[0] for own, _ in shares]
    streams = [
        Stream(layout, laid_out(own, other, trial, half))
        for half, (own, other) in enumerate(shares)
    ]
    rot_theirs = layout.shift(rotated, db=1)
    for _ in range(layout.z - 1):
        for stream in streams:
            stream.advance()
    early, late = [], []
    for at, stream in enumerate(streams):
        slabs = [array[-1:] for array in (*stream.ring, *stream.across)]
        received = layout.shift(jnp.concatenate(slabs), db=1)
        if at == 1:
            (received,) = stream.advance((received,))
        else:
            stream.advance()
        early.append(received)
        late.append(layout.shift(received[layout.z - 1 : layout.z], dy=1))
    *fulls, inverses = inverses_of(layout, streams, sizes, early, late)
    parts = bias_of(layout, fulls, inverses, rotated, rot_theirs)
    parts = lax.all_to_all(parts, "chol", 0, 0, tiled=True)
    force_bias, kept, *sent = potential_of(order, fields, parts, cholesky)
    received = [layout.shift(part, db=1) for part in sent]

    rounded, base = first_of([kept], fulls, 0)
    rounded_theirs, base_theirs = first_of(received, fulls, 1)
    streams = [Stream(layout, rounded), Stream(layout, rounded_theirs)]
    for _ in range(layout.z):
        for stream in streams:
            stream.advance()
    sent, full = second_of(layout, received, base_theirs, streams)
    theirs = layout.shift(sent, db=1)
    return place(order, finish(kept, base, full), theirs), force_bias


def solution(mesh):
    in_specs = (
        P("walk", "chol", None),
        P("chol", None),
        P(None, "chol", None),
        P(None, "chol", None),
        P("walk", None),
        P(),
    )
    out_specs = (P("walk", "chol", None), P("walk", None))
    layout = Layout(mesh.shape["walk"], mesh.shape["chol"])
    return jax.shard_map(
        functools.partial(shards, layout),
        mesh=mesh,
        in_specs=in_specs,
        out_specs=out_specs,
        check_vma=False,
    )
```

```python
import functools

import jax
import jax.numpy as jnp
from jax import lax
from jax.experimental import pallas as pl
from jax.experimental.pallas import tpu as pltpu
from jax.sharding import PartitionSpec as P

ITERS = 3
TAU_ROOT = 0.1
BLOCK = 16
HIGHEST = lax.Precision.HIGHEST
MIB = 1024 * 1024

F32 = jnp.float32
BF16 = jnp.bfloat16


def params(mebibytes):
    return pltpu.CompilerParams(vmem_limit_bytes=mebibytes * MIB)


def vmem_specs(count):
    return [pl.BlockSpec(memory_space=pltpu.VMEM)] * count


class Layout:
    def __init__(self, walk_size, chol_size):
        self.walk = walk_size
        self.chol = chol_size
        self.z = chol_size // 4

    def shift(self, array, dz=0, dy=0, db=0):
        pairs = []
        for index in range(self.chol):
            z, y, b = index // 4, (index // 2) % 2, index % 2
            target = (((z + dz) % self.z) * 2 + (y ^ dy)) * 2 + (b ^ db)
            pairs.append((index, target))
        return lax.ppermute(array, "chol", pairs)

    def flip(self, array, mask):
        return lax.ppermute(array, "chol", [(i, i ^ mask) for i in range(self.chol)])

    def step(self, array):
        ring = [*range(0, self.z, 2), *reversed(range(1, self.z, 2))]
        target = {z: ring[(at + 1) % self.z] for at, z in enumerate(ring)}
        pairs = [(index, target[index // 4] * 4 + index % 4) for index in range(self.chol)]
        return lax.ppermute(array, "chol", pairs)

    def origin(self, steps, dy):
        index = lax.axis_index("chol")
        z, y = index // 4, lax.rem(index // 2, 2)
        at = jnp.where(lax.rem(z, 2) == 0, z // 2, self.z - (z + 1) // 2)
        at = lax.rem(at + (self.z - steps), self.z)
        z = jnp.where(2 * at < self.z, 2 * at, 2 * (self.z - at) - 1)
        return z * 2 + (y + dy - 2 * y * dy)


class Stream:
    def __init__(self, layout, piece):
        self.layout = layout
        self.ring = [piece]
        self.across = []
        self.last = []

    def moves(self):
        latest = self.ring[-1]
        if len(self.ring) < self.layout.z:
            return [self.layout.shift(latest, dy=1), self.layout.step(latest)]
        half = (latest.shape[0] + 1) // 2
        return [
            self.layout.shift(latest[:half], dy=1),
            self.layout.step(self.across[-1][half:]),
        ]

    def accept(self, moved):
        if len(self.ring) < self.layout.z:
            self.across.append(moved[0])
            self.ring.append(moved[1])
        else:
            self.last = moved

    def advance(self, anchors=()):
        moved = self.moves()
        if anchors or len(self.ring) < self.layout.z:
            anchors, moved = lax.optimization_barrier((anchors, moved))
        self.accept(moved)
        return anchors

    def pieces(self):
        ring = [(array, 0, steps, 0) for steps, array in enumerate(self.ring)]
        across = [(array, 0, steps, 1) for steps, array in enumerate(self.across)]
        lower, upper = self.last
        steps = self.layout.z - 1
        return ring + across + [(lower, 0, steps, 1), (upper, lower.shape[0], steps, 1)]


def operands(streams):
    arrays, slabs = [], []
    for stream in streams:
        slabs.append([])
        for array, first, steps, dy in stream.pieces():
            for at in range(array.shape[0]):
                slabs[-1].append((len(arrays), at, first + at, steps, dy))
            arrays.append(array)
    return arrays, slabs


def lay_out_kernel(half, own, other, trial, out):
    count, rows = own.shape[0], own.shape[1] // 2
    b = lax.rem(lax.axis_index("chol"), 2)
    for block, part in ((b, own), (1 - b, other)):
        for walker in range(count):
            for at in range(2):
                place = slice(at * rows, (at + 1) * rows)
                out[(block * count + walker) * 2 + at] = part[walker, place]
    out[4 * count] = trial[half * rows : (half + 1) * rows]


def laid_out(own, other, trial, half):
    count, rows, electrons = own.shape
    return pl.pallas_call(
        functools.partial(lay_out_kernel, half),
        out_shape=jax.ShapeDtypeStruct((4 * count + 1, rows // 2, electrons), own.dtype),
        in_specs=vmem_specs(3),
        out_specs=pl.BlockSpec(memory_space=pltpu.VMEM),
        compiler_params=params(4),
    )(own, other, trial)


def product(left, right):
    high, right_high = left.astype(BF16), right.astype(BF16)
    low = (left - high.astype(F32)).astype(BF16)
    right_low = (right - right_high.astype(F32)).astype(BF16)
    return jnp.dot(
        jnp.concatenate([high, high, low], axis=1),
        jnp.concatenate([right_high, right_low, right_high], axis=0),
        preferred_element_type=F32,
    )


def newton_inverses(matrices):
    shape = matrices[0].shape
    same = lax.broadcasted_iota(jnp.int32, shape, 0) == lax.broadcasted_iota(jnp.int32, shape, 1)
    identity = jnp.where(same, 1.0, 0.0).astype(F32)
    powers = [identity - matrix for matrix in matrices]
    estimates = [identity + power for power in powers]
    for _ in range(ITERS - 1):
        powers = [product(power, power) for power in powers]
        estimates = [x + product(x, power) for x, power in zip(estimates, powers)]
    return estimates


def inverse_kernel(layout, slabs, counts, *refs):
    streams = len(counts)
    early, late, refs = refs[:streams], refs[streams : 2 * streams], refs[2 * streams :]
    fulls, (out, buffer, turned) = refs[-3 - streams : -3], refs[-3:]
    pieces = refs[: -3 - streams]
    rows, electrons = early[0].shape[1:]
    b = lax.rem(lax.axis_index("chol"), 2)

    for half, stream in enumerate(slabs):
        place = slice(half * rows, (half + 1) * rows)
        theirs = [(early[half], at) for at in range(early[half].shape[0])] + [(late[half], 0)]
        trial = [slab for slab in stream if slab[2] == 4 * counts[half]]
        for (operand, at, _, steps, dy), (part, number) in zip(trial, theirs):
            origin = layout.origin(steps, dy)
            buffer[origin, b, place] = pieces[operand][at]
            buffer[origin, 1 - b, place] = part[number]
    turned[...] = buffer[...].reshape(-1, electrons).T

    matrices = []
    for full, count, stream in zip(fulls, counts, slabs):
        for operand, at, slab, steps, dy in stream:
            if slab < 4 * count:
                block, walker, half = slab // (2 * count), slab // 2 % count, slab % 2
                place = slice(half * rows, (half + 1) * rows)
                full[walker, layout.origin(steps, dy), block, place] = pieces[operand][at]
        for walker in range(count):
            columns = full[walker].reshape(-1, electrons)
            matrices.append(jnp.dot(turned[...], columns, preferred_element_type=F32))
    for number, inverse in enumerate(newton_inverses(matrices)):
        out[number] = inverse.astype(BF16)


def inverses_of(layout, streams, counts, early, late):
    arrays, slabs = operands(streams)
    _, rows, electrons = early[0].shape
    rows = 2 * rows
    chips = layout.chol // 2
    total = sum(counts)
    return pl.pallas_call(
        functools.partial(inverse_kernel, layout, slabs, counts),
        out_shape=[
            jax.ShapeDtypeStruct((count, chips, 2, rows, electrons), BF16) for count in counts
        ]
        + [jax.ShapeDtypeStruct((total, electrons, electrons), BF16)],
        in_specs=vmem_specs(2 * len(counts) + len(arrays)),
        out_specs=vmem_specs(len(counts) + 1),
        scratch_shapes=[
            pltpu.VMEM((chips, 2, rows, electrons), BF16),
            pltpu.VMEM((electrons, 2 * chips * rows), BF16),
        ],
        compiler_params=params(8),
        cost_estimate=pl.CostEstimate(
            flops=2 * total * electrons**2 * (2 * chips * rows + 6 * (ITERS - 1) * electrons),
            bytes_accessed=4 * (total + 1) * 2 * chips * rows * electrons,
            transcendentals=0,
        ),
    )(*early, *late, *arrays)


def bias_kernel(counts, rot_mine, rot_theirs, inverses, *refs):
    fulls, (out, greens) = refs[:-2], refs[-2:]
    vectors, rows, electrons = rot_mine.shape
    index = lax.axis_index("chol")
    chip, b = index // 2, lax.rem(index, 2)
    walkers = [(full, at) for full, count in zip(fulls, counts) for at in range(count)]
    for number, (full, walker) in enumerate(walkers):
        both = full[walker, chip].reshape(2 * rows, electrons)
        green = jnp.dot(both, inverses[number], preferred_element_type=F32).astype(BF16)
        greens[:, :, number] = green.reshape(2, rows // BLOCK, BLOCK, electrons)
    width = len(walkers) * BLOCK
    total = jnp.zeros((vectors * BLOCK, width), F32)
    for half, rot in ((b, rot_mine), (1 - b, rot_theirs)):
        for block in range(rows // BLOCK):
            total += lax.dot_general(
                rot[:, block * BLOCK : (block + 1) * BLOCK, :].reshape(vectors * BLOCK, electrons),
                greens[half, block].reshape(width, electrons),
                (((1,), (1,)), ((), ())),
                preferred_element_type=F32,
            )
    same = lax.rem(lax.broadcasted_iota(jnp.int32, total.shape, 0), BLOCK) == lax.rem(
        lax.broadcasted_iota(jnp.int32, total.shape, 1), BLOCK
    )
    summed = jnp.sum(jnp.where(same, total, 0.0).reshape(vectors, BLOCK, width), axis=1)
    shape = (len(walkers), width)
    pick = (
        lax.broadcasted_iota(jnp.int32, shape, 1) // BLOCK
        == lax.broadcasted_iota(jnp.int32, shape, 0)
    ).astype(F32)
    bias = lax.dot_general(
        pick, summed, (((1,), (1,)), ((), ())), precision=HIGHEST, preferred_element_type=F32
    )
    out[...] = jnp.zeros_like(out)
    for index in range(out.shape[0]):
        out[index, : len(walkers), :vectors] = bias


def bias_of(layout, fulls, inverses, rot_mine, rot_theirs):
    vectors, rows, electrons = rot_mine.shape
    counts = [full.shape[0] for full in fulls]
    total = sum(counts)
    return pl.pallas_call(
        functools.partial(bias_kernel, counts),
        out_shape=jax.ShapeDtypeStruct(
            (layout.chol, pl.cdiv(total, 8) * 8, pl.cdiv(vectors, 128) * 128), F32
        ),
        in_specs=vmem_specs(3 + len(fulls)),
        out_specs=pl.BlockSpec(memory_space=pltpu.VMEM),
        scratch_shapes=[pltpu.VMEM((2, rows // BLOCK, total, BLOCK, electrons), BF16)],
        compiler_params=params(8),
        cost_estimate=pl.CostEstimate(
            flops=4 * total * rows * electrons * (electrons + vectors * BLOCK),
            bytes_accessed=4 * (vectors + total) * rows * electrons,
            transcendentals=0,
        ),
    )(rot_mine, rot_theirs, inverses, *fulls)


def potential_kernel(order, fields, parts, cholesky, *refs):
    bias_out, kept, *sent, weights = refs
    per_group, vectors = fields.shape
    half, piece = kept.shape[0], sent[0].shape[1]
    b = lax.rem(lax.axis_index("chol"), 2)
    row = lax.broadcasted_iota(jnp.int32, (per_group, vectors), 0)
    bias = jnp.zeros((per_group, vectors), F32)
    for core in range(2):
        total = parts[core]
        for index in range(core + 2, parts.shape[0], 2):
            total = total + parts[index]
        for walker in range(half):
            slot = order[core * half + walker]
            bias += jnp.where(row == slot, total[walker : walker + 1, :vectors], 0.0)
    bias = TAU_ROOT * bias
    bias_out[...] = bias
    shifted = (fields[...] - bias).astype(BF16)
    slot = jnp.zeros((per_group * BLOCK, 1), jnp.int32)
    place = lax.broadcasted_iota(jnp.int32, slot.shape, 0) // BLOCK
    for at in range(per_group):
        slot = jnp.where(place == at, order[lax.rem(at + b * half, per_group)], slot)
    tall = (per_group * BLOCK, per_group)
    rows = (lax.broadcasted_iota(jnp.int32, tall, 1) == slot).astype(BF16)
    wide = (vectors, vectors * BLOCK)
    columns = (
        lax.broadcasted_iota(jnp.int32, wide, 1) // BLOCK
        == lax.broadcasted_iota(jnp.int32, wide, 0)
    ).astype(BF16)
    spread = jnp.dot(rows, shifted, preferred_element_type=F32).astype(BF16)
    spread = jnp.dot(spread, columns, preferred_element_type=F32)
    same = lax.rem(lax.broadcasted_iota(jnp.int32, spread.shape, 0), BLOCK) == lax.rem(
        lax.broadcasted_iota(jnp.int32, spread.shape, 1), BLOCK
    )
    weights[...] = jnp.where(same, spread, 0.0).astype(BF16)
    rows, orbitals = cholesky.shape[1:]
    for at in range(0, rows, BLOCK):
        columns = cholesky[:, at : at + BLOCK, :].reshape(vectors * BLOCK, orbitals)
        result = TAU_ROOT * jnp.dot(weights[...], columns, preferred_element_type=F32)
        result = result.astype(BF16).reshape(2 * half, BLOCK, orbitals)
        kept[:, at : at + BLOCK, :] = result[:half]
        start = at % piece
        sent[at // piece][:, start : start + BLOCK, :] = result[half:]


def potential_of(order, fields, parts, cholesky):
    per_group, vectors = fields.shape
    half = per_group // 2
    _, rows, orbitals = cholesky.shape
    sent = jax.ShapeDtypeStruct((half, rows // 2, orbitals), BF16)
    return pl.pallas_call(
        potential_kernel,
        out_shape=[
            jax.ShapeDtypeStruct((per_group, vectors), F32),
            jax.ShapeDtypeStruct((half, rows, orbitals), BF16),
            sent,
            sent,
        ],
        in_specs=[pl.BlockSpec(memory_space=pltpu.SMEM)] + vmem_specs(3),
        out_specs=vmem_specs(4),
        scratch_shapes=[pltpu.VMEM((per_group * BLOCK, vectors * BLOCK), BF16)],
        compiler_params=params(12),
    )(order, fields, parts, cholesky)


def first_kernel(sibling, parts, *refs):
    potential, fulls, (rounded, base) = refs[:parts], refs[parts:-2], refs[-2:]
    b = lax.rem(lax.axis_index("chol"), 2)
    chip = lax.axis_index("chol") // 2
    count = 0
    for full in fulls:
        for walker in range(full.shape[0]):
            rows = jnp.concatenate([part[count] for part in potential], axis=0)
            columns = full[walker].reshape(-1, full.shape[-1])
            term = jnp.dot(rows, columns, preferred_element_type=F32)
            rounded[count] = term.astype(BF16)
            own = full[walker, chip, 1 - b if sibling else b]
            base[count] = own.astype(F32) + term
            count += 1


def first_of(potential, fulls, sibling):
    half, _, orbitals = potential[0].shape
    rows, electrons = fulls[0].shape[-2:]
    shape = (half, rows, electrons)
    return pl.pallas_call(
        functools.partial(first_kernel, sibling, len(potential)),
        out_shape=[jax.ShapeDtypeStruct(shape, BF16), jax.ShapeDtypeStruct(shape, F32)],
        in_specs=vmem_specs(len(potential) + len(fulls)),
        out_specs=vmem_specs(2),
        compiler_params=params(8),
        cost_estimate=pl.CostEstimate(
            flops=2 * half * rows * orbitals * electrons,
            bytes_accessed=2 * half * orbitals * (rows + electrons),
            transcendentals=0,
        ),
    )(*potential, *fulls)


def second_kernel(layout, slabs, parts, *refs):
    potential, base, pieces = refs[:parts], refs[parts], refs[parts + 1 : -2]
    out, full = refs[-2:]
    b = lax.rem(lax.axis_index("chol"), 2)
    for block, stream in zip((b, 1 - b), slabs):
        for operand, at, walker, steps, dy in stream:
            full[walker, layout.origin(steps, dy), block] = pieces[operand][at]
    for walker in range(out.shape[0]):
        rows = jnp.concatenate([part[walker] for part in potential], axis=0)
        columns = full[walker].reshape(-1, full.shape[-1])
        term = jnp.dot(rows, columns, preferred_element_type=F32)
        out[walker] = (base[walker] + 0.5 * term).astype(BF16)


def second_of(layout, potential, base, streams):
    arrays, slabs = operands(streams)
    orbitals = potential[0].shape[2]
    half, rows, electrons = base.shape
    return pl.pallas_call(
        functools.partial(second_kernel, layout, slabs, len(potential)),
        out_shape=[
            jax.ShapeDtypeStruct((half, rows, electrons), BF16),
            jax.ShapeDtypeStruct((half, layout.chol // 2, 2, rows, electrons), BF16),
        ],
        in_specs=vmem_specs(len(potential) + 1 + len(arrays)),
        out_specs=vmem_specs(2),
        compiler_params=params(8),
        cost_estimate=pl.CostEstimate(
            flops=2 * half * rows * orbitals * electrons,
            bytes_accessed=2 * half * orbitals * (rows + 3 * electrons),
            transcendentals=0,
        ),
    )(*potential, base, *arrays)


def finish_kernel(potential, base, full, out):
    for walker in range(out.shape[0]):
        columns = full[walker].reshape(-1, full.shape[-1])
        term = jnp.dot(potential[walker], columns, preferred_element_type=F32)
        out[walker] = (base[walker] + 0.5 * term).astype(BF16)


def finish(potential, base, full):
    half, rows, electrons = base.shape
    orbitals = potential.shape[2]
    return pl.pallas_call(
        finish_kernel,
        out_shape=jax.ShapeDtypeStruct((half, rows, electrons), BF16),
        in_specs=vmem_specs(3),
        out_specs=pl.BlockSpec(memory_space=pltpu.VMEM),
        compiler_params=params(8),
        cost_estimate=pl.CostEstimate(
            flops=2 * half * rows * orbitals * electrons,
            bytes_accessed=2 * half * orbitals * (rows + electrons),
            transcendentals=0,
        ),
    )(potential, base, full)


def place_kernel(order, mine, theirs, out, semaphores):
    half = mine.shape[0]
    b = lax.rem(lax.axis_index("chol"), 2)
    copies = []
    for part, core in ((mine, b), (theirs, 1 - b)):
        for walker in range(half):
            target = out.at[order[core * half + walker]]
            copies.append(
                pltpu.make_async_copy(part.at[walker], target, semaphores.at[len(copies)])
            )
    for copy in copies:
        copy.start()
    for copy in copies:
        copy.wait()


def place(order, mine, theirs):
    half, rows, electrons = mine.shape
    return pl.pallas_call(
        place_kernel,
        out_shape=jax.ShapeDtypeStruct((2 * half, rows, electrons), BF16),
        in_specs=[pl.BlockSpec(memory_space=pltpu.SMEM)] + vmem_specs(2),
        out_specs=pl.BlockSpec(memory_space=pl.ANY),
        scratch_shapes=[pltpu.SemaphoreType.DMA((2 * half,))],
        compiler_params=params(4),
    )(order, mine, theirs)


def split_kernel(source, walkers, *refs):
    targets, (order, picked, semaphores) = refs[:4], refs[4:]
    per_group = walkers.shape[0]
    half = per_group // 2
    share = half // 2
    group = lax.axis_index("walk")
    b = lax.rem(lax.axis_index("chol"), 2)
    stayed, arrived, sent = jnp.int32(0), jnp.int32(0), jnp.int32(0)
    for slot in range(per_group):
        local = source[group * per_group + slot] - group * per_group
        stays = ((local >= 0) & (local < per_group)).astype(jnp.int32)
        picked[jnp.where(stays == 1, jnp.minimum(stayed, half - 1), per_group)] = local
        rank = jnp.minimum(jnp.where(stays == 1, stayed, arrived), half - 1)
        core = rank // share
        order[core * half + stays * share + rank - core * share] = jnp.int32(slot)
        stayed, arrived = stayed + stays, arrived + 1 - stays
        local = source[(1 - group) * per_group + slot] - group * per_group
        goes = ((local >= 0) & (local < per_group)).astype(jnp.int32)
        picked[jnp.where(goes == 1, half + jnp.minimum(sent, half - 1), per_group)] = local
        sent = sent + goes
    offsets = (b * share, (1 - b) * share, half + b * share, half + (1 - b) * share)
    copies = []
    for target, offset in reversed(list(zip(targets, offsets))):
        for walker in range(share):
            copies.append(
                pltpu.make_async_copy(
                    walkers.at[picked[offset + walker]],
                    target.at[walker],
                    semaphores.at[len(copies)],
                )
            )
    for copy in copies:
        copy.start()
    for copy in copies:
        copy.wait()


def split_walkers(walkers, source):
    per_group, rows, electrons = walkers.shape
    share = jax.ShapeDtypeStruct((per_group // 4, rows, electrons), walkers.dtype)
    return pl.pallas_call(
        split_kernel,
        out_shape=[share] * 4 + [jax.ShapeDtypeStruct((per_group,), jnp.int32)],
        in_specs=[pl.BlockSpec(memory_space=pltpu.SMEM), pl.BlockSpec(memory_space=pl.ANY)],
        out_specs=[pl.BlockSpec(memory_space=pl.ANY)] * 4
        + [pl.BlockSpec(memory_space=pltpu.SMEM)],
        scratch_shapes=[
            pltpu.SMEM((per_group + 1,), jnp.int32),
            pltpu.SemaphoreType.DMA((per_group,)),
        ],
        compiler_params=params(4),
    )(source, walkers)


def ranks(flags):
    count = flags.shape[-1]
    before = jnp.arange(count)[None, :] < jnp.arange(count)[:, None]
    return jnp.sum(jnp.where(before & flags[..., None, :], 1, 0), axis=-1)


def migrate(layout, walkers, source):
    per_group = walkers.shape[0]
    half = per_group // 2
    group = lax.axis_index("walk")
    if layout.walk == 2 and half % 2 == 0:
        stay, stay_sent, near, cross, order = split_walkers(walkers, source)
        count = 2 * layout.chol
        across = [(index + layout.chol) % count for index in range(count)]
        axes = ("walk", "chol")
        near = lax.ppermute(near, axes, list(enumerate(across)))
        cross = lax.ppermute(cross, axes, [(i, j ^ 1) for i, j in enumerate(across)])
        return [(near, cross), (stay, layout.shift(stay_sent, db=1))], order
    table = source.reshape(layout.walk, per_group)
    incoming = lax.dynamic_index_in_dim(table, group, 0, keepdims=False)
    incoming_groups = incoming // per_group

    def outgoing(distance):
        row = lax.dynamic_index_in_dim(table, (group + distance) % layout.walk, 0, keepdims=False)
        local = row - group * per_group
        here = (local >= 0) & (local < per_group)
        match = here[None, :] & (ranks(here)[None, :] == jnp.arange(half)[:, None])
        return jnp.take(walkers, jnp.sum(jnp.where(match, local[None, :], 0), axis=1), axis=0)

    arrived = [outgoing(0)]
    for distance in range(1, layout.walk):
        pairs = [(g, (g + distance) % layout.walk) for g in range(layout.walk)]
        arrived.append(lax.ppermute(outgoing(distance), "walk", pairs))
    slots = jnp.arange(per_group)
    same = (incoming_groups[:, None] == incoming_groups[None, :]) & (slots[None, :] < slots[:, None])
    rank = jnp.sum(same.astype(jnp.int32), axis=1)
    distance = (group - incoming_groups) % layout.walk
    migrated = jnp.take(jnp.concatenate(arrived, axis=0), distance * half + rank, axis=0)
    b = lax.axis_index("chol") % 2
    mine = lax.dynamic_slice_in_dim(migrated, b * half, half, 0)
    theirs = lax.dynamic_slice_in_dim(migrated, (1 - b) * half, half, 0)
    theirs = layout.shift(theirs, db=1)
    share = half // 2
    shares = [(mine[:share], theirs[:share]), (mine[share:], theirs[share:])]
    return shares, slots.astype(jnp.int32)


def shards(layout, walkers, trial, cholesky, rotated, fields, source):
    shares, order = migrate(layout, walkers, source)
    sizes = [own.shape[0] for own, _ in shares]
    streams = [
        Stream(layout, laid_out(own, other, trial, half))
        for half, (own, other) in enumerate(shares)
    ]
    rot_theirs = layout.shift(rotated, db=1)
    for _ in range(layout.z - 1):
        for stream in streams:
            stream.advance()
    early, late = [], []
    for at, stream in enumerate(streams):
        slabs = [array[-1:] for array in (*stream.ring, *stream.across)]
        received = layout.shift(jnp.concatenate(slabs), db=1)
        if at == 1:
            (received,) = stream.advance((received,))
        else:
            stream.advance()
        early.append(received)
        late.append(layout.shift(received[layout.z - 1 : layout.z], dy=1))
    *fulls, inverses = inverses_of(layout, streams, sizes, early, late)
    parts = bias_of(layout, fulls, inverses, rotated, rot_theirs)
    parts = lax.all_to_all(parts, "chol", 0, 0, tiled=True)
    force_bias, kept, *sent = potential_of(order, fields, parts, cholesky)
    received = [layout.shift(part, db=1) for part in sent]

    rounded, base = first_of([kept], fulls, 0)
    rounded_theirs, base_theirs = first_of(received, fulls, 1)
    streams = [Stream(layout, rounded), Stream(layout, rounded_theirs)]
    for _ in range(layout.z):
        for stream in streams:
            stream.advance()
    sent, full = second_of(layout, received, base_theirs, streams)
    theirs = layout.shift(sent, db=1)
    return place(order, finish(kept, base, full), theirs), force_bias


def solution(mesh):
    in_specs = (
        P("walk", "chol", None),
        P("chol", None),
        P(None, "chol", None),
        P(None, "chol", None),
        P("walk", None),
        P(),
    )
    out_specs = (P("walk", "chol", None), P("walk", None))
    layout = Layout(mesh.shape["walk"], mesh.shape["chol"])
    return jax.shard_map(
        functools.partial(shards, layout),
        mesh=mesh,
        in_specs=in_specs,
        out_specs=out_specs,
        check_vma=False,
    )
```
